32 devices in a mesh: dp: 32 (over z, y, x, core).
Axes of the slice: x: 2, y: 2, z: 4, core: 2. Of those that a mesh axis runs over, the one named last changes fastest.
Arguments:
- tokens: float32 [65536, 384], P('dp'), may hold values from -11 to 11
- cloud_lengths: int32 [512], P('dp'), may hold values from 32 to 128, as said below
- owner_slot: int32 [65536], P('dp'), may hold values from -1 to 1279, as said below
- targets: float32 [40960, 96], P('dp'), may hold values from -5 to 5
- prenorm_gain: float32 [384], replicated, may hold values from 0.25 to 1.75
- prenorm_shift: float32 [384], replicated, may hold values from -1.75 to 1.75
- attention_in: float32 [384, 1152], replicated, may hold values from -0.3125 to 0.3125
- attention_out: float32 [384, 384], replicated, may hold values from -1.25 to 1.25
- attention_shift: float32 [384], replicated, may hold values from -1.75 to 1.75
- midnorm_gain: float32 [384], replicated, may hold values from 0.25 to 1.75
- midnorm_shift: float32 [384], replicated, may hold values from -1.75 to 1.75
- expand_weight: float32 [384, 1536], replicated, may hold values from -0.3125 to 0.3125
- expand_shift: float32 [1536], replicated, may hold values from -1.75 to 1.75
- reduce_weight: float32 [1536, 384], replicated, may hold values from -0.21875 to 0.21875
- reduce_shift: float32 [384], replicated, may hold values from -1.75 to 1.75
- lastnorm_gain: float32 [384], replicated, may hold values from 0.25 to 1.75
- lastnorm_shift: float32 [384], replicated, may hold values from -1.75 to 1.75
- head_weight: float32 [384, 96], replicated, may hold values from -0.3125 to 0.3125
- head_shift: float32 [96], replicated, may hold values from -1.75 to 1.75
Outputs:
- mean_loss: float32 [], replicated
- predictions: float32 [65536, 96], P('dp')
- input_grad: float32 [65536, 384], P('dp')
- grad_prenorm_gain: float32 [384], replicated
- grad_prenorm_shift: float32 [384], replicated
- grad_attention_in: float32 [384, 1152], replicated
- grad_attention_out: float32 [384, 384], replicated
- grad_attention_shift: float32 [384], replicated
- grad_midnorm_gain: float32 [384], replicated
- grad_midnorm_shift: float32 [384], replicated
- grad_expand_weight: float32 [384, 1536], replicated
- grad_expand_shift: float32 [1536], replicated
- grad_reduce_weight: float32 [1536, 384], replicated
- grad_reduce_shift: float32 [384], replicated
- grad_lastnorm_gain: float32 [384], replicated
- grad_lastnorm_shift: float32 [384], replicated
- grad_head_weight: float32 [384, 96], replicated
- grad_head_shift: float32 [96], replicated
- rms_stats: float32 [3], replicated
The draws below stay inside these ranges and needn't reach their ends.
Inputs may be any that keep to these rules, and one draw needn't show every extreme that they name: `cloud_lengths`: in every block of 16 entries one cloud has exactly 128 patches and another exactly 32; the clouds of a block fit in its 2048 places. `owner_slot`: -1 on visible patches and padding. A masked patch's slot is o * capacity + c for owner device o and place c below capacity; slots are distinct within one device's places. Each cloud of n patches has exactly (3 n) // 5 masked ones. Some owner receives 40 patches from every device.
All inputs are finite; a program needn't handle non-finite values.
Results may differ from the reference program's by a relative error of at most 0.0003.
Values sent between devices are 32-bit elements; how exact they have to be, the bound alone decides.
No kernel may reach another device: no remote copies, remote signals or barrier semaphores. Data moves between devices by JAX's collectives and lax.ppermute only.
A program may use at most 192 MiB of HBM per device.

```python
import math
import jax
import jax.numpy as jnp
from jax import lax

D = 384
HEADS = 6
HEAD_DIM = 64
FF = 1536
PTS = 32
OUTW = 96
TOK_DEV = 2048
CLOUD_MAX = 128
CLOUD_MIN = 32
CLOUDS_DEV = 16
SLOTS_DEV = 1280
TOKENS = 65536
TARGET_ROWS = 40960
N_DP = 32


def cloud_plan(key):
    device_count = TOKENS // TOK_DEV
    clouds_each = TOK_DEV // CLOUD_MAX
    lengths = jax.random.randint(jax.random.fold_in(key, 11), (device_count, clouds_each), CLOUD_MIN, CLOUD_MAX + 1)
    longest = jax.random.randint(jax.random.fold_in(key, 12), (device_count, 1), 0, clouds_each)
    offset_draw = jax.random.randint(jax.random.fold_in(key, 13), (device_count, 1), 0, clouds_each - 1)
    shortest = (longest + 1 + offset_draw) % clouds_each
    column = jnp.arange(clouds_each, dtype=jnp.int32)[None, :]
    lengths = jnp.where(column == longest, CLOUD_MAX, lengths)
    lengths = jnp.where(column == shortest, CLOUD_MIN, lengths)
    return lengths.astype(jnp.int32)


def draw_cloud_lengths(key, part):
    return cloud_plan(key).reshape(-1)


def draw_owner_slot(key, part):
    lengths = cloud_plan(key)
    key = jax.random.fold_in(key, 2)
    device_count = TOKENS // TOK_DEV
    capacity = SLOTS_DEV // device_count
    bounds = jnp.cumsum(lengths, axis=1).astype(jnp.int32)
    places = jnp.arange(TOK_DEV, dtype=jnp.int32)
    groups = jnp.sum((places[None, :, None] >= bounds[:, None, :]).astype(jnp.int32), axis=2)
    quotas = jnp.concatenate([3 * lengths // 5, jnp.zeros((device_count, 1), jnp.int32)], axis=1)
    allowed = jnp.take_along_axis(quotas, groups, axis=1)
    noise_keys = jax.random.randint(jax.random.fold_in(key, 1), (device_count, TOK_DEV), 0, 1 << 15) * TOK_DEV + places[None, :]

    def rank_device(pieces):
        group_row, noise_row = pieces
        same_group = group_row[:, None] == group_row[None, :]
        return jnp.sum((same_group & (noise_row[None, :] < noise_row[:, None])).astype(jnp.int32), axis=1)
    token_ranks = lax.map(rank_device, (groups, noise_keys))
    masked = token_ranks < allowed
    favoured = jax.random.randint(jax.random.fold_in(key, 3), (), 0, device_count)
    slot_ids = jnp.arange(SLOTS_DEV, dtype=jnp.int32)
    priority = jax.random.randint(jax.random.fold_in(key, 4), (device_count, SLOTS_DEV), 0, 1 << 15) * SLOTS_DEV + slot_ids[None, :]
    priority = jnp.where((slot_ids // capacity == favoured)[None, :], slot_ids[None, :] - SLOTS_DEV, priority)
    slot_order = jnp.argsort(priority, axis=1).astype(jnp.int32)
    position = jnp.cumsum(masked.astype(jnp.int32), axis=1) - 1
    chosen = jnp.take_along_axis(slot_order, jnp.clip(position, 0, SLOTS_DEV - 1), axis=1)
    return jnp.where(masked, chosen, -1).astype(jnp.int32).reshape(-1)


def draw_tokens(key, part):
    key = jax.random.fold_in(key, 3)
    ramp_place = jnp.arange(TOKENS, dtype=jnp.float32)[:, None] / TOKENS
    values = jnp.clip(jax.random.normal(key, (TOKENS, D), jnp.float32), -6.0, 6.0)
    ramp_scale = 0.6 + 1.2 * ramp_place
    return values * ramp_scale


def draw_targets(key, part):
    key = jax.random.fold_in(key, 4)
    ramp_place = jnp.arange(TARGET_ROWS, dtype=jnp.float32)[:, None] / TARGET_ROWS
    values = 0.8 * jnp.clip(jax.random.normal(key, (TARGET_ROWS, OUTW), jnp.float32), -4.0, 4.0)
    return values * (0.5 + ramp_place)


def noise(key, shape, width, most, kind=jnp.bfloat16):
    values = jax.random.normal(key, shape, jnp.float32) * width
    return jnp.minimum(jnp.maximum(values, -most), most).astype(kind)


def setup_inputs(seed: int = 0) -> dict:
    streams_of = jax.random.split(jax.random.key(seed), 20)
    tokens = draw_tokens(jax.random.fold_in(streams_of[19], 71), 0)
    cloud_lengths = draw_cloud_lengths(jax.random.fold_in(streams_of[19], 71), 0)
    owner_slot = draw_owner_slot(jax.random.fold_in(streams_of[19], 71), 0)
    targets = draw_targets(jax.random.fold_in(streams_of[19], 71), 0)
    prenorm_gain = jnp.clip(1.0 + 0.15 * jax.random.normal(streams_of[4], (D,), jnp.float32), 0.25, 1.75)
    prenorm_shift = noise(streams_of[5], (D,), 0.3, 1.75, jnp.float32)
    attention_in = noise(streams_of[6], (D, 3 * D), D ** -0.5, 0.3125, jnp.float32)
    attention_out = noise(streams_of[7], (D, D), (D // 16) ** -0.5, 1.25, jnp.float32)
    attention_shift = noise(streams_of[8], (D,), 0.3, 1.75, jnp.float32)
    midnorm_gain = jnp.clip(1.0 + 0.15 * jax.random.normal(streams_of[9], (D,), jnp.float32), 0.25, 1.75)
    midnorm_shift = noise(streams_of[10], (D,), 0.3, 1.75, jnp.float32)
    expand_weight = noise(streams_of[11], (D, FF), D ** -0.5, 0.3125, jnp.float32)
    expand_shift = noise(streams_of[12], (FF,), 0.3, 1.75, jnp.float32)
    reduce_weight = noise(streams_of[13], (FF, D), (FF // 2) ** -0.5, 0.21875, jnp.float32)
    reduce_shift = noise(streams_of[14], (D,), 0.3, 1.75, jnp.float32)
    lastnorm_gain = jnp.clip(1.0 + 0.15 * jax.random.normal(streams_of[15], (D,), jnp.float32), 0.25, 1.75)
    lastnorm_shift = noise(streams_of[16], (D,), 0.3, 1.75, jnp.float32)
    head_weight = noise(streams_of[17], (D, OUTW), D ** -0.5, 0.3125, jnp.float32)
    head_shift = noise(streams_of[18], (OUTW,), 0.3, 1.75, jnp.float32)
    return dict(tokens=tokens, cloud_lengths=cloud_lengths, owner_slot=owner_slot, targets=targets, prenorm_gain=prenorm_gain, prenorm_shift=prenorm_shift, attention_in=attention_in, attention_out=attention_out, attention_shift=attention_shift, midnorm_gain=midnorm_gain, midnorm_shift=midnorm_shift, expand_weight=expand_weight, expand_shift=expand_shift, reduce_weight=reduce_weight, reduce_shift=reduce_shift, lastnorm_gain=lastnorm_gain, lastnorm_shift=lastnorm_shift, head_weight=head_weight, head_shift=head_shift)


EPSILON = 1e-05
HIGHEST = lax.Precision.HIGHEST

@jax.custom_vjp
def low(v):
    return lax.optimization_barrier(v.astype(jnp.bfloat16)).astype(jnp.float32)

@jax.custom_vjp
def low_back(v):
    return v

def low_keep(v):
    return (low(v), None)

def low_pass(kept, grad):
    return (grad,)

def back_keep(v):
    return (v, None)

def back_low(kept, grad):
    return (low(grad),)
low.defvjp(low_keep, low_pass)
low_back.defvjp(back_keep, back_low)

def normalize(values, scale_gain, scale_shift):
    average = lax.optimization_barrier(jnp.mean(values, axis=-1, keepdims=True))
    centred = values - average
    spread = lax.optimization_barrier(jnp.mean(centred * centred, axis=-1, keepdims=True))
    return centred * lax.rsqrt(spread + EPSILON) * scale_gain + scale_shift

def matmul(left_rows, right_rows):
    return jnp.dot(left_rows, right_rows, precision=HIGHEST, preferred_element_type=jnp.float32)

def softmin(distance, over_axis):
    lowest = lax.optimization_barrier(jnp.min(distance, axis=over_axis, keepdims=True))
    inside = lax.optimization_barrier(jnp.mean(jnp.exp(lowest - distance), axis=over_axis, keepdims=True))
    return jnp.squeeze(lowest - jnp.log(inside), over_axis)

def chamfer(predicted, expected):
    row_count = predicted.shape[0]
    points_pred = predicted.reshape(row_count, PTS, 3)
    points_true = expected.reshape(row_count, PTS, 3)
    differ = points_pred[:, :, None, :] - points_true[:, None, :, :]
    distance = lax.optimization_barrier(jnp.sum(differ * differ, axis=-1))
    return lax.optimization_barrier(jnp.mean(softmin(distance, 2), axis=1)) + lax.optimization_barrier(jnp.mean(softmin(distance, 1), axis=1))

def group_table(lengths_row):
    bounds = jnp.cumsum(lengths_row).astype(jnp.int32)
    places = jnp.arange(TOK_DEV, dtype=jnp.int32)
    groups = lax.optimization_barrier(jnp.sum((places[:, None] >= bounds[None, :]).astype(jnp.int32), axis=1))
    return (groups, (places < bounds[-1]).astype(jnp.float32))

def attention(normed, weight_in, groups):
    joint_rows = matmul(normed, weight_in).reshape(TOK_DEV, 3, HEADS, HEAD_DIM)
    scores = jnp.einsum('qhe,khe->hqk', joint_rows[:, 0], joint_rows[:, 1], precision=HIGHEST) / math.sqrt(HEAD_DIM)
    scores = jnp.where((groups[:, None] == groups[None, :])[None], scores, -jnp.inf)
    probability = jax.nn.softmax(scores, axis=-1)
    attended = jnp.einsum('hqk,khe->qhe', probability, joint_rows[:, 2], precision=HIGHEST)
    return attended.reshape(TOK_DEV, D)

def reference(tokens, cloud_lengths, owner_slot, targets, prenorm_gain, prenorm_shift, attention_in, attention_out, attention_shift, midnorm_gain, midnorm_shift, expand_weight, expand_shift, reduce_weight, reduce_shift, lastnorm_gain, lastnorm_shift, head_weight, head_shift):
    capacity = SLOTS_DEV // N_DP
    masked = owner_slot >= 0
    safe_slot = jnp.maximum(owner_slot, 0)
    device_of = jnp.arange(TOKENS, dtype=jnp.int32) // TOK_DEV
    target_row = safe_slot // capacity * SLOTS_DEV + device_of * capacity + safe_slot % capacity
    mask_float = masked.astype(jnp.float32)
    expected = targets[target_row.astype(jnp.int32)] * mask_float[:, None]
    groups, valid_rows = jax.vmap(group_table)(cloud_lengths.reshape(N_DP, CLOUDS_DEV))
    params = (prenorm_gain, prenorm_shift, attention_in, attention_out, attention_shift, midnorm_gain, midnorm_shift, expand_weight, expand_shift, reduce_weight, reduce_shift, lastnorm_gain, lastnorm_shift, head_weight, head_shift)

    def forward(weights, token_input):
        pre_gain, pre_shift, joint_weight, out_weight, out_shift, mid_gain, mid_shift, up_weight, up_shift, down_weight, down_shift, last_gain, last_shift, final_weight, final_shift = weights

        def one_device(pieces):
            token_rows, group_rows, valid_part, expected_rows, mask_rows = pieces
            normed_in = normalize(token_rows, pre_gain, pre_shift)
            mixed_rows = matmul(attention(normed_in, joint_weight, group_rows), out_weight) + out_shift
            middle = token_rows + mixed_rows
            pre_act = matmul(normalize(middle, mid_gain, mid_shift), up_weight) + up_shift
            hidden = jax.nn.gelu(pre_act, approximate=False)
            branch = matmul(hidden, down_weight) + down_shift
            stream = middle + branch
            predicted = (matmul(normalize(stream, last_gain, last_shift), final_weight) + final_shift) * valid_part[:, None]
            chamfer_total = jnp.sum(chamfer(predicted, expected_rows) * mask_rows)
            weight_rows = valid_part[:, None]
            square_sums = jnp.stack([jnp.sum(stream * stream * weight_rows), jnp.sum(mixed_rows * mixed_rows * weight_rows), jnp.sum(branch * branch * weight_rows)])
            return ((chamfer_total, predicted), square_sums)
        (totals, predicted), square_sums = lax.map(jax.checkpoint(one_device), (token_input.reshape(N_DP, TOK_DEV, D), groups, valid_rows, expected.reshape(N_DP, TOK_DEV, OUTW), mask_float.reshape(N_DP, TOK_DEV)))
        return ((jnp.sum(totals), predicted.reshape(TOKENS, OUTW)), lax.optimization_barrier(jnp.sum(square_sums, axis=0)))
    (loss_total, predictions), pullback, square_sums = jax.vjp(forward, params, tokens, has_aux=True)
    grad_params, input_grad = pullback((jnp.ones((), jnp.float32), jnp.zeros_like(predictions)))
    masked_count = jnp.sum(mask_float)
    valid_count = jnp.sum(valid_rows)
    rms_stats = jnp.sqrt(square_sums / (valid_count * D))
    grad_prenorm_gain, grad_prenorm_shift, grad_attention_in, grad_attention_out, grad_attention_shift, grad_midnorm_gain, grad_midnorm_shift, grad_expand_weight, grad_expand_shift, grad_reduce_weight, grad_reduce_shift, grad_lastnorm_gain, grad_lastnorm_shift, grad_head_weight, grad_head_shift = grad_params
    return (loss_total / masked_count, predictions, input_grad, grad_prenorm_gain / masked_count, grad_prenorm_shift / masked_count, grad_attention_in / masked_count, grad_attention_out / masked_count, grad_attention_shift / masked_count, grad_midnorm_gain / masked_count, grad_midnorm_shift / masked_count, grad_expand_weight / masked_count, grad_expand_shift / masked_count, grad_reduce_weight / masked_count, grad_reduce_shift / masked_count, grad_lastnorm_gain / masked_count, grad_lastnorm_shift / masked_count, grad_head_weight / masked_count, grad_head_shift / masked_count, rms_stats)
```

```python
import math

import jax
import jax.numpy as jnp
from jax import lax
from jax.experimental import pallas as pl
from jax.experimental.pallas import tpu as pltpu
from jax.sharding import PartitionSpec as P

HEADS = 6
CLOUD_MAX = 128
TILE = 256
EPSILON = 1e-05
F32 = jnp.float32
BF16 = jnp.bfloat16
VMEM_BYTES = 60 * 1024 * 1024


def split(values):
    high = values.astype(BF16)
    low = (values - high.astype(F32)).astype(BF16)
    return high, low


def dot(left, right, left_dim=1, right_dim=0):
    return lax.dot_general(
        left, right, (((left_dim,), (right_dim,)), ((), ())), preferred_element_type=F32
    )


def dot3(left, right, left_dim=1, right_dim=0):
    left_high, left_low = left
    right_high, right_low = right
    return dot(left_high, right_high, left_dim, right_dim) + (
        dot(left_high, right_low, left_dim, right_dim)
        + dot(left_low, right_high, left_dim, right_dim)
    )


def norm_parts(values):
    average = jnp.mean(values, axis=-1, keepdims=True)
    centred = values - average
    spread = jnp.mean(centred * centred, axis=-1, keepdims=True)
    inverse = lax.rsqrt(spread + EPSILON)
    return centred * inverse, inverse


def norm_back(grad_out, unit_rows, inverse, scale_gain):
    scaled = grad_out * scale_gain
    average_grad = jnp.mean(scaled, axis=-1, keepdims=True)
    project_grad = jnp.mean(scaled * unit_rows, axis=-1, keepdims=True)
    return inverse * (scaled - average_grad - unit_rows * project_grad)


def column_sum(values):
    return jnp.sum(values, axis=0, keepdims=True)


def split_weight(source, high, low, step=128):
    rows = source.shape[0]

    def body(index, carry):
        place = pl.ds(pl.multiple_of(index * step, step), step)
        high[place, :], low[place, :] = split(source[place, :])
        return carry

    lax.fori_loop(0, rows // step, body, 0)


def spaced(length):
    return (length + 7) // 8 * 8


def aligned_rows(token_count, cloud_count):
    return (token_count + 8 * cloud_count + TILE - 1) // TILE * TILE


def cloud_totals(lens):
    total, spread = jnp.int32(0), jnp.int32(0)
    for cloud in range(lens.shape[0]):
        total = total + lens[cloud]
        spread = spread + spaced(lens[cloud])
    return total, spread


def move_rows(source, target, source_start, target_start, count):
    def body(group, carry):
        for row in range(8):
            place = group * 8 + row
            target[pl.ds(target_start + place, 1), :] = source[pl.ds(source_start + place, 1), :]
        return carry

    lax.fori_loop(0, (count + 7) // 8, body, 0)


def restore_rows(lens, source, target):
    token_count = target.shape[0]

    def cloud(index, carry):
        start, spaced_start = carry
        length = lens[index]
        whole = length // 8
        move_rows(source, target, start_of(spaced_start), start, whole * 8)

        def row(place, carry):
            target[pl.ds(start + place, 1), :] = source[pl.ds(spaced_start + place, 1), :]
            return carry

        lax.fori_loop(whole * 8, length, row, 0)
        return start + length, spaced_start + spaced(length)

    total, _ = lax.fori_loop(0, lens.shape[0], cloud, (jnp.int32(0), jnp.int32(0)))
    edge = (total + 7) // 8 * 8

    def blank_row(place, carry):
        target[pl.ds(place, 1), :] = jnp.zeros((1, target.shape[1]), target.dtype)
        return carry

    lax.fori_loop(total, edge, blank_row, 0)

    def blank(group, carry):
        rows = pl.ds(pl.multiple_of(group * 8, 8), 8)
        target[rows, :] = jnp.zeros((8, target.shape[1]), target.dtype)
        return carry

    lax.fori_loop(edge // 8, token_count // 8, blank, 0)


def start_of(place):
    return pl.multiple_of(place, 8)


def gelu_parts(pre_act):
    cumulative = 0.5 * (1.0 + lax.erf(pre_act * (1.0 / math.sqrt(2.0))))
    density = jnp.exp(-0.5 * pre_act * pre_act) * (1.0 / math.sqrt(2.0 * math.pi))
    return pre_act * cumulative, cumulative + pre_act * density


def forward_kernel(
    lens, tokens_hbm, owner, targets, prenorm_gain, prenorm_shift, attention_in, attention_out,
    attention_shift, midnorm_gain, midnorm_shift, expand_weight, expand_shift, reduce_weight,
    reduce_shift, lastnorm_gain, lastnorm_shift, head_turned, head_shift, head_weight,
    tokens_out, joint_out, attended_out, middle_out, slope_out, grad_stream_out, predicted,
    sum_reduce, sum_head, small, tiles_out,
    raw, tokens, owners, joint, attended, middle, grad_stream, spaced_pred, slope,
    in_high, in_low, out_high, out_low, expand_high, expand_low, reduce_high, reduce_low,
    head_high, head_low, turned_high, turned_low, target_parts, pred_rows, true_rows, distance, second,
    col_low, col_sum, token_sem, joint_sem, out_sems, slope_sem,
):
    token_count = owner.shape[1]
    slot_count, width_out = targets.shape
    points = width_out // 3
    tiles = middle.shape[0] // TILE
    width = middle.shape[1]
    total, spread = cloud_totals(lens)
    used = (spread + TILE - 1) // TILE
    tiles_out[0] = used

    def tile_rows(index):
        return pl.ds(pl.multiple_of(index * TILE, TILE), TILE)

    token_copy = pltpu.make_async_copy(tokens_hbm, raw.at[pl.ds(0, token_count)], token_sem)
    token_copy.start()
    split_weight(attention_in, in_high, in_low)
    split_weight(attention_out, out_high, out_low)
    split_weight(expand_weight, expand_high, expand_low)
    split_weight(reduce_weight, reduce_high, reduce_low)
    split_weight(head_weight, head_high, head_low)
    turned_high[...], turned_low[...] = split(head_turned[...])
    turned = targets[...].T
    high, low = split(turned)
    target_parts[:width_out, :] = high
    target_parts[width_out:, :] = low
    small[...] = jnp.zeros_like(small)
    sum_reduce[...] = jnp.zeros_like(sum_reduce)
    sum_head[...] = jnp.zeros_like(sum_head)
    raw[token_count:, :] = jnp.zeros((raw.shape[0] - token_count, width), F32)
    owners[...] = jnp.full(owners.shape, -2, jnp.int32)
    token_copy.wait()
    wide = lax.broadcasted_iota(jnp.int32, (1, 2 * CLOUD_MAX), 1)
    tokens[tile_rows(used - 1), :] = jnp.zeros((TILE, width), F32)

    def place_cloud(index, carry):
        start, spaced_start = carry
        length = lens[index]
        move_rows(raw, tokens, start, spaced_start, length)
        base = jnp.minimum(start // 128, token_count // 128 - 2)
        offset, spaced_offset = start - base * 128, spaced_start % 128
        slots = owner[:, pl.ds(pl.multiple_of(base * 128, 128), 256)]
        slots = pltpu.roll(slots, (spaced_offset - offset) % 256, 1)
        lanes = pl.ds(pl.multiple_of(spaced_start // 128 * 128, 128), 256)
        inside = jnp.logical_and(wide >= spaced_offset, wide < spaced_offset + length)
        owners[:, lanes] = jnp.where(inside, slots, owners[:, lanes])
        return start + length, spaced_start + spaced(length)

    lax.fori_loop(0, lens.shape[0], place_cloud, (jnp.int32(0), jnp.int32(0)))

    def joint_tile(index, carry):
        rows = tile_rows(index)
        unit, _ = norm_parts(tokens[rows, :])
        normed = split(unit * prenorm_gain[...] + prenorm_shift[...])
        joint[rows, :] = dot3(normed, (in_high[...], in_low[...]))
        pltpu.make_async_copy(joint.at[rows], joint_out.at[rows], joint_sem.at[index]).start()
        return carry

    lax.fori_loop(0, used, joint_tile, 0)
    tail = pl.ds(pl.multiple_of(used * TILE, TILE), CLOUD_MAX)
    joint[tail, :] = jnp.zeros((CLOUD_MAX, joint.shape[1]), F32)
    tail_copy = pltpu.make_async_copy(joint.at[tail], joint_out.at[tail], joint_sem.at[tiles])
    tail_copy.start()
    attended[tile_rows(used - 1), :] = jnp.zeros((TILE, width), F32)

    lane = lax.broadcasted_iota(jnp.int32, (CLOUD_MAX, 128), 1)
    first_head = lane < 64
    wide_lane = lax.broadcasted_iota(jnp.int32, (2 * CLOUD_MAX, CLOUD_MAX), 1)
    empty = jnp.zeros((CLOUD_MAX, 128), BF16)

    def cloud(index, start):
        length = lens[index]
        rows = pl.ds(start_of(start), CLOUD_MAX)
        inside = wide_lane < length
        for pair in range(HEADS // 2):
            query = joint[rows, pair * 128 : pair * 128 + 128] * 0.125
            key_high, key_low = split(joint[rows, width + pair * 128 : width + pair * 128 + 128])
            value_high, value_low = split(
                joint[rows, 2 * width + pair * 128 : 2 * width + pair * 128 + 128]
            )
            both = jnp.concatenate(
                [jnp.where(first_head, query, 0.0), jnp.where(first_head, 0.0, query)], axis=0
            )
            left = jnp.concatenate(split(both), axis=1)
            right = jnp.concatenate(
                [
                    jnp.concatenate([key_high, key_high], axis=1),
                    jnp.concatenate([key_low, empty], axis=1),
                ],
                axis=0,
            )
            scores = dot(left, right, 1, 1)
            scores = scores[:, :128] + scores[:, 128:]
            scores = jnp.where(inside, scores, -1e30)
            peak = jnp.max(scores, axis=-1, keepdims=True)
            weights = jnp.exp(scores - peak)
            probs = weights * (1.0 / jnp.sum(weights, axis=-1, keepdims=True))
            left = jnp.concatenate(split(probs), axis=1)
            right = jnp.concatenate(
                [
                    jnp.concatenate([value_high, value_low], axis=1),
                    jnp.concatenate([value_high, empty], axis=1),
                ],
                axis=0,
            )
            mixed = dot(left, right)
            mixed = mixed[:, :128] + mixed[:, 128:]
            attended[rows, pair * 128 : pair * 128 + 128] = jnp.where(
                first_head, mixed[:CLOUD_MAX], mixed[CLOUD_MAX:]
            )
        return start + spaced(length)

    lax.fori_loop(0, lens.shape[0], cloud, jnp.int32(0))

    slots = lax.broadcasted_iota(jnp.int32, (slot_count, TILE), 0)

    def out_copies(index):
        rows = tile_rows(index)
        return [
            pltpu.make_async_copy(source.at[rows], target.at[rows], out_sems.at[place, index])
            for place, (source, target) in enumerate(
                [
                    (attended, attended_out),
                    (middle, middle_out),
                    (grad_stream, grad_stream_out),
                    (tokens, tokens_out),
                ]
            )
        ]

    def slope_copy(index):
        slot = lax.rem(index, 2)
        return pltpu.make_async_copy(
            slope.at[slot], slope_out.at[tile_rows(index)], slope_sem.at[slot]
        )

    def chamfer_half(half):
        xs = [pred_rows[half, pl.ds(c, points, stride=3), :] for c in range(3)]

        def first(j, row_low):
            gap = [xs[c] - true_rows[half, pl.ds(3 * j + c, 1), :] for c in range(3)]
            apart = gap[0] * gap[0] + gap[1] * gap[1] + gap[2] * gap[2]
            distance[j] = apart
            lowest = jnp.min(apart, axis=0, keepdims=True)
            weight = jnp.exp(lowest - apart)
            inside = column_sum(weight)
            col_low[pl.ds(j, 1), :] = lowest
            col_sum[pl.ds(j, 1), :] = inside
            second[j] = weight * (1.0 / (points * inside))
            return jnp.minimum(row_low, apart)

        row_low = lax.fori_loop(
            0, points, first, jnp.full((points, 128), jnp.inf, F32), unroll=8
        )

        def middle_pass(j, row_sum):
            weight = jnp.exp(row_low - distance[j])
            distance[j] = weight
            return row_sum + weight

        row_sum = lax.fori_loop(0, points, middle_pass, jnp.zeros((points, 128), F32), unroll=8)
        row_scale = 1.0 / (points * row_sum)

        def last(j, carry):
            weight = second[j] + distance[j] * row_scale
            return (carry[0] + weight,) + tuple(
                carry[1 + c] + weight * true_rows[half, pl.ds(3 * j + c, 1), :] for c in range(3)
            )

        zero = jnp.zeros((points, 128), F32)
        sums = lax.fori_loop(0, points, last, (zero,) * 4, unroll=8)
        terms = column_sum(row_low - jnp.log(row_sum * (1.0 / points))) + column_sum(
            col_low[...] - jnp.log(col_sum[...] * (1.0 / points))
        )
        grads = [2.0 * (sums[0] * xs[c] - sums[1 + c]) for c in range(3)]
        return terms * (1.0 / points), grads

    def block_tile(index, carry):
        rows = tile_rows(index)
        slot_row = owners[:, tile_rows(index)]
        valid_lane = slot_row > -2
        valid_row = jnp.broadcast_to(valid_lane.astype(F32), (8, TILE)).T[:, :1] > 0.5
        mixed = dot3(split(attended[rows, :]), (out_high[...], out_low[...])) + attention_shift[...]
        mid = tokens[rows, :] + mixed
        middle[rows, :] = mid
        unit, _ = norm_parts(mid)
        normed = split(unit * midnorm_gain[...] + midnorm_shift[...])
        pre_act = dot3(normed, (expand_high[...], expand_low[...])) + expand_shift[...]
        hidden, steep = gelu_parts(pre_act)

        @pl.when(index >= 2)
        def _():
            slope_copy(index - 2).wait()

        slope[lax.rem(index, 2)] = steep
        slope_copy(index).start()
        hidden = split(hidden)
        branch = dot3(hidden, (reduce_high[...], reduce_low[...])) + reduce_shift[...]
        stream = mid + branch
        unit, inverse = norm_parts(stream)
        normed = split(unit * lastnorm_gain[...] + lastnorm_shift[...])
        pred = dot3((turned_high[...], turned_low[...]), normed, 1, 1) + head_shift[...]
        pred = jnp.where(valid_lane, pred, 0.0)
        for half in range(TILE // 128):
            pred_rows[half] = pred[:, half * 128 : half * 128 + 128]
        spaced_pred[rows, :] = pred.T
        chosen = (slots == slot_row).astype(F32).astype(BF16)
        true_points = dot(target_parts[...], chosen)
        true_points = true_points[:width_out] + true_points[width_out:]
        for half in range(TILE // 128):
            true_rows[half] = true_points[:, half * 128 : half * 128 + 128]
        masked = slot_row >= 0
        losses = []
        for half in range(TILE // 128):
            terms, grads = chamfer_half(half)
            losses.append(terms)
            for c in range(3):
                pred_rows[half, pl.ds(c, points, stride=3), :] = grads[c]
        grad_turned = jnp.concatenate([pred_rows[half] for half in range(TILE // 128)], axis=1)
        grad_turned = jnp.where(masked, grad_turned, 0.0)
        loss = jnp.where(masked, jnp.concatenate(losses, axis=1), 0.0)
        grad_pred = grad_turned.T
        sum_head[...] += dot3(split(grad_turned), normed)
        grad_last = dot3(split(grad_pred), (head_high[...], head_low[...]), 1, 1)
        grad_str = norm_back(grad_last, unit, inverse, lastnorm_gain[...])
        grad_stream[rows, :] = grad_str
        sum_reduce[...] += dot3(split(grad_str.T), hidden)
        small[0:1, :TILE] += loss
        small[1:2, :TILE] += masked.astype(F32)
        small[2:3, :width] += column_sum(jnp.where(valid_row, stream * stream, 0.0))
        small[3:4, :width] += column_sum(jnp.where(valid_row, mixed * mixed, 0.0))
        small[4:5, :width] += column_sum(jnp.where(valid_row, branch * branch, 0.0))
        small[5:6, :width] += column_sum(grad_last * unit)
        small[6:7, :width] += column_sum(grad_last)
        small[7:8, :width] += column_sum(grad_str)
        small[8:9, :width_out] += column_sum(grad_pred)
        for copy in out_copies(index):
            copy.start()
        return carry

    lax.fori_loop(0, used, block_tile, 0)
    small[9:10, :128] = jnp.where(
        lax.broadcasted_iota(jnp.int32, (1, 128), 1) == 0, total.astype(F32), 0.0
    )

    restore_rows(lens, spaced_pred, predicted)

    @pl.when(used >= 2)
    def _():
        slope_copy(used - 2).wait()

    slope_copy(used - 1).wait()
    tail_copy.wait()

    def finish(index, carry):
        rows = tile_rows(index)
        pltpu.make_async_copy(joint.at[rows], joint_out.at[rows], joint_sem.at[index]).wait()
        for copy in out_copies(index):
            copy.wait()
        return carry

    lax.fori_loop(0, used, finish, 0)


def any_spec():
    return pl.BlockSpec(memory_space=pl.ANY)


def vmem_spec():
    return pl.BlockSpec(memory_space=pltpu.VMEM)


def smem_spec():
    return pl.BlockSpec(memory_space=pltpu.SMEM)


def shape(*dims):
    return jax.ShapeDtypeStruct(dims, F32)


def run_forward(tokens, lens, owner, targets, weights):
    token_count, width = tokens.shape
    joint_width = weights["attention_in"].shape[1]
    hidden_width = weights["expand_weight"].shape[1]
    slot_count, width_out = targets.shape
    spaced_count = aligned_rows(token_count, lens.shape[0])
    tiles = spaced_count // TILE
    points = width_out // 3
    names = (
        "prenorm_gain", "prenorm_shift", "attention_in", "attention_out", "attention_shift",
        "midnorm_gain", "midnorm_shift", "expand_weight", "expand_shift", "reduce_weight",
        "reduce_shift", "lastnorm_gain", "lastnorm_shift", "head_turned", "head_shift", "head_weight",
    )
    pairs = []
    for name in ("attention_in", "attention_out", "expand_weight", "reduce_weight", "head_weight", "head_turned"):
        pairs += [pltpu.VMEM(weights[name].shape, BF16)] * 2
    return pl.pallas_call(
        forward_kernel,
        out_shape=(
            shape(spaced_count, width),
            shape(spaced_count + CLOUD_MAX, joint_width),
            shape(spaced_count, width),
            shape(spaced_count, width),
            shape(spaced_count, hidden_width),
            shape(spaced_count, width),
            shape(token_count, width_out),
            shape(width, hidden_width),
            shape(width_out, width),
            shape(16, hidden_width),
            jax.ShapeDtypeStruct((1,), jnp.int32),
        ),
        in_specs=[smem_spec(), any_spec()] + [vmem_spec()] * (2 + len(names)),
        out_specs=[any_spec()] * 6 + [vmem_spec()] * 4 + [smem_spec()],
        scratch_shapes=[
            pltpu.VMEM((token_count + 8, width), F32),
            pltpu.VMEM((spaced_count, width), F32),
            pltpu.VMEM((1, spaced_count + 256), jnp.int32),
            pltpu.VMEM((spaced_count + CLOUD_MAX, joint_width), F32),
            pltpu.VMEM((spaced_count + CLOUD_MAX, width), F32),
            pltpu.VMEM((spaced_count, width), F32),
            pltpu.VMEM((spaced_count, width), F32),
            pltpu.VMEM((spaced_count, width_out), F32),
            pltpu.VMEM((2, TILE, hidden_width), F32),
        ]
        + pairs
        + [
            pltpu.VMEM((2 * width_out, slot_count), BF16),
            pltpu.VMEM((TILE // 128, width_out, 128), F32),
            pltpu.VMEM((TILE // 128, width_out, 128), F32),
            pltpu.VMEM((points, points, 128), F32),
            pltpu.VMEM((points, points, 128), F32),
            pltpu.VMEM((points, 128), F32),
            pltpu.VMEM((points, 128), F32),
            pltpu.SemaphoreType.DMA,
            pltpu.SemaphoreType.DMA((tiles + 1,)),
            pltpu.SemaphoreType.DMA((4, tiles)),
            pltpu.SemaphoreType.DMA((2,)),
        ],
        compiler_params=pltpu.CompilerParams(vmem_limit_bytes=VMEM_BYTES),
        name="forward",
    )(lens, tokens, owner, targets, *[weights[name] for name in names])


def mlp_back_kernel(
    used_ref, grad_stream, slope, middle, attended, midnorm_gain, midnorm_shift, reduce_weight,
    expand_weight, attention_out,
    grad_middle, grad_attended, sum_expand, sum_out, small,
    reduce_high, reduce_low, expand_high, expand_low, out_high, out_low,
):
    index = pl.program_id(0)
    used = used_ref[0]
    width = middle.shape[1]

    @pl.when(index == 0)
    def _():
        split_weight(reduce_weight, reduce_high, reduce_low)
        split_weight(expand_weight, expand_high, expand_low)
        split_weight(attention_out, out_high, out_low)
        sum_expand[...] = jnp.zeros_like(sum_expand)
        sum_out[...] = jnp.zeros_like(sum_out)
        small[...] = jnp.zeros_like(small)

    @pl.when(index < used)
    def _():
        grad_str = grad_stream[...]
        unit, inverse = norm_parts(middle[...])
        normed = unit * midnorm_gain[...] + midnorm_shift[...]
        grad_pre = dot3(split(grad_str), (reduce_high[...], reduce_low[...]), 1, 1) * slope[...]
        parts = split(grad_pre)
        sum_expand[...] += dot3(split(normed.T), parts)
        grad_normed = dot3(parts, (expand_high[...], expand_low[...]), 1, 1)
        grad_mid = grad_str + norm_back(grad_normed, unit, inverse, midnorm_gain[...])
        grad_middle[...] = grad_mid
        parts = split(grad_mid)
        grad_attended[...] = dot3(parts, (out_high[...], out_low[...]), 1, 1)
        sum_out[...] += dot3(split(attended[...].T), parts)
        small[0:1, :] += column_sum(grad_pre)
        small[1:2, :width] += column_sum(grad_normed * unit)
        small[2:3, :width] += column_sum(grad_normed)
        small[3:4, :width] += column_sum(grad_mid)

    @pl.when(index >= used)
    def _():
        grad_attended[...] = jnp.zeros_like(grad_attended)


def run_mlp_back(used, grad_stream, slope, middle, attended, weights):
    token_count, width = middle.shape
    hidden_width = slope.shape[1]

    def row_map(index, used):
        return (jnp.minimum(index, used[0] - 1), 0)

    def next_map(index, used):
        return (jnp.minimum(index, used[0]), 0)

    def rows(columns):
        return pl.BlockSpec((TILE, columns), row_map)

    def whole(array):
        return pl.BlockSpec(array.shape, lambda index, used: (0, 0))

    names = ("midnorm_gain", "midnorm_shift", "reduce_weight", "expand_weight", "attention_out")
    extra = [weights[name] for name in names]
    sums = (shape(width, hidden_width), shape(width, width), shape(8, hidden_width))
    pairs = []
    for name in names[2:]:
        pairs += [pltpu.VMEM(weights[name].shape, BF16)] * 2
    return pl.pallas_call(
        mlp_back_kernel,
        out_shape=(shape(token_count, width), shape(token_count + CLOUD_MAX, width)) + sums,
        grid_spec=pltpu.PrefetchScalarGridSpec(
            num_scalar_prefetch=1,
            grid=(token_count // TILE,),
            in_specs=[rows(width), rows(hidden_width), rows(width), rows(width)]
            + [whole(array) for array in extra],
            out_specs=[rows(width), pl.BlockSpec((TILE, width), next_map)] + [whole(array) for array in sums],
            scratch_shapes=pairs,
        ),
        compiler_params=pltpu.CompilerParams(vmem_limit_bytes=VMEM_BYTES),
        name="mlp_back",
    )(used, grad_stream, slope, middle, attended, *extra)


def attention_back_kernel(
    lens, used_ref, joint, grad_attended, tokens, grad_middle, prenorm_gain, prenorm_shift,
    attention_in,
    input_grad, sum_in, small,
    grad_joint, spaced_grad, in_high, in_low,
):
    width = tokens.shape[1]
    used = used_ref[0]
    split_weight(attention_in, in_high, in_low)
    sum_in[...] = jnp.zeros_like(sum_in)
    small[...] = jnp.zeros_like(small)

    def tile_rows(index):
        return pl.ds(pl.multiple_of(index * TILE, TILE), TILE)

    grad_joint[tile_rows(used - 1), :] = jnp.zeros((TILE, grad_joint.shape[1]), F32)
    lane = lax.broadcasted_iota(jnp.int32, (CLOUD_MAX, 128), 1)
    first_head = lane < 64
    key_place = lax.broadcasted_iota(jnp.int32, (CLOUD_MAX, 2 * CLOUD_MAX), 0)
    query_place = lax.broadcasted_iota(jnp.int32, (CLOUD_MAX, 2 * CLOUD_MAX), 1) % CLOUD_MAX
    empty = jnp.zeros((CLOUD_MAX, 128), BF16)

    def both_heads(values):
        return jnp.concatenate(
            [jnp.where(first_head, values, 0.0), jnp.where(first_head, 0.0, values)], axis=0
        )

    def cloud(index, start):
        length = lens[index]
        rows = pl.ds(start_of(start), CLOUD_MAX)
        inside = key_place < length
        live = jnp.logical_and(inside, query_place < length)
        for pair in range(HEADS // 2):
            at = [slice(part * width + pair * 128, part * width + pair * 128 + 128) for part in range(3)]
            query = split(both_heads(joint[rows, at[0]] * 0.125))
            key = split(joint[rows, at[1]])
            value = split(joint[rows, at[2]])
            grad = split(both_heads(grad_attended[rows, at[0]]))
            scores = dot3(key, query, 1, 1)
            scores = jnp.where(inside, scores, -1e30)
            peak = jnp.max(scores, axis=0, keepdims=True)
            weights = jnp.exp(scores - peak)
            probs = weights * (1.0 / column_sum(weights))
            probs = jnp.where(live, probs, 0.0)
            grad_probs = dot3(value, grad, 1, 1)
            shared = column_sum(probs * grad_probs)
            grad_scores = probs * (grad_probs - shared)
            parts = split(grad_scores)
            grad_joint[rows, at[2]] = dot3(split(probs), grad)
            grad_joint[rows, at[1]] = dot3(parts, query)
            left = jnp.concatenate(split(grad_scores.T), axis=1)
            right = jnp.concatenate(
                [
                    jnp.concatenate([key[0], key[1]], axis=1),
                    jnp.concatenate([key[0], empty], axis=1),
                ],
                axis=0,
            )
            grad_query = dot(left, right)
            grad_query = (grad_query[:, :128] + grad_query[:, 128:]) * 0.125
            grad_joint[rows, at[0]] = jnp.where(
                first_head, grad_query[:CLOUD_MAX], grad_query[CLOUD_MAX:]
            )
        return start + spaced(length)

    lax.fori_loop(0, lens.shape[0], cloud, jnp.int32(0))

    def joint_tile(index, carry):
        rows = tile_rows(index)
        unit, inverse = norm_parts(tokens[rows, :])
        normed = unit * prenorm_gain[...] + prenorm_shift[...]
        parts = split(grad_joint[rows, :])
        sum_in[...] += dot3(split(normed.T), parts)
        grad_normed = dot3(parts, (in_high[...], in_low[...]), 1, 1)
        spaced_grad[rows, :] = grad_middle[rows, :] + norm_back(
            grad_normed, unit, inverse, prenorm_gain[...]
        )
        small[0:1, :] += column_sum(grad_normed * unit)
        small[1:2, :] += column_sum(grad_normed)
        return carry

    lax.fori_loop(0, used, joint_tile, 0)

    restore_rows(lens, spaced_grad, input_grad)


def run_attention_back(lens, used, joint, grad_attended, tokens, grad_middle, weights, token_count):
    spaced_count, width = tokens.shape
    joint_width = joint.shape[1]
    names = ("prenorm_gain", "prenorm_shift", "attention_in")
    return pl.pallas_call(
        attention_back_kernel,
        out_shape=(shape(token_count, width), shape(width, joint_width), shape(8, width)),
        in_specs=[smem_spec()] * 2 + [vmem_spec()] * 7,
        out_specs=[vmem_spec()] * 3,
        scratch_shapes=[
            pltpu.VMEM((spaced_count + CLOUD_MAX, joint_width), F32),
            pltpu.VMEM((spaced_count, width), F32),
        ]
        + [pltpu.VMEM(weights["attention_in"].shape, BF16)] * 2,
        compiler_params=pltpu.CompilerParams(vmem_limit_bytes=VMEM_BYTES),
        name="attention_back",
    )(lens, used, joint, grad_attended, tokens, grad_middle, *[weights[name] for name in names])


def shards(
    tokens, cloud_lengths, owner_slot, targets, prenorm_gain, prenorm_shift, attention_in,
    attention_out, attention_shift, midnorm_gain, midnorm_shift, expand_weight, expand_shift,
    reduce_weight, reduce_shift, lastnorm_gain, lastnorm_shift, head_weight, head_shift,
):
    token_count, width = tokens.shape
    device_count = lax.axis_size("dp")
    slot_count, width_out = targets.shape
    capacity = slot_count // device_count
    arrived = lax.all_to_all(
        targets.reshape(device_count, capacity, width_out), "dp", split_axis=0, concat_axis=0, tiled=True
    ).reshape(slot_count, width_out)
    weights = dict(
        prenorm_gain=prenorm_gain[None], prenorm_shift=prenorm_shift[None], attention_in=attention_in,
        attention_out=attention_out, attention_shift=attention_shift[None],
        midnorm_gain=midnorm_gain[None], midnorm_shift=midnorm_shift[None],
        expand_weight=expand_weight, expand_shift=expand_shift[None], reduce_weight=reduce_weight,
        reduce_shift=reduce_shift[None], lastnorm_gain=lastnorm_gain[None],
        lastnorm_shift=lastnorm_shift[None], head_weight=head_weight, head_turned=head_weight.T,
        head_shift=head_shift[:, None],
    )
    (
        spaced_tokens, joint, attended, middle, slope, grad_stream, predicted, sum_reduce, sum_head, small, used,
    ) = run_forward(tokens, cloud_lengths, owner_slot[None], arrived, weights)
    grad_middle, grad_attended, sum_expand, sum_out, small_mid = run_mlp_back(
        used, grad_stream, slope, middle, attended, weights
    )
    input_grad, sum_in, small_in = run_attention_back(
        cloud_lengths, used, joint, grad_attended, spaced_tokens, grad_middle, weights, token_count
    )
    sum_reduce, sum_head, small, sum_expand, sum_out, small_mid, sum_in, small_in = lax.psum(
        (sum_reduce, sum_head, small, sum_expand, sum_out, small_mid, sum_in, small_in), "dp"
    )
    masked_count = jnp.sum(small[1])
    scale = 1.0 / masked_count
    mean_loss = jnp.sum(small[0]) / masked_count
    rms_stats = jnp.sqrt(jnp.sum(small[2:5], axis=1) / (jnp.sum(small[9]) * width))
    return (
        mean_loss,
        predicted,
        input_grad,
        small_in[0] / masked_count,
        small_in[1] / masked_count,
        sum_in / masked_count,
        sum_out / masked_count,
        small_mid[3, :width] / masked_count,
        small_mid[1, :width] / masked_count,
        small_mid[2, :width] / masked_count,
        sum_expand / masked_count,
        small_mid[0] / masked_count,
        sum_reduce.T / masked_count,
        small[7, :width] / masked_count,
        small[5, :width] / masked_count,
        small[6, :width] / masked_count,
        sum_head.T / masked_count,
        small[8, :width_out] / masked_count,
        rms_stats,
    )


def solution(mesh):
    row = P("dp", None)
    return jax.shard_map(
        shards,
        mesh=mesh,
        in_specs=(row, P("dp"), P("dp"), row) + (P(),) * 15,
        out_specs=(P(), row, row) + (P(),) * 16,
        check_vma=False,
    )
```

```python
import math

import jax
import jax.numpy as jnp
from jax import lax
from jax.experimental import pallas as pl
from jax.experimental.pallas import tpu as pltpu
from jax.sharding import PartitionSpec as P

HEADS = 6
CLOUD_MAX = 128
TILE = 256
EPSILON = 1e-05
F32 = jnp.float32
BF16 = jnp.bfloat16
VMEM_BYTES = 60 * 1024 * 1024


def split(values):
    high = values.astype(BF16)
    low = (values - high.astype(F32)).astype(BF16)
    return high, low


def dot(left, right, left_dim=1, right_dim=0):
    return lax.dot_general(
        left, right, (((left_dim,), (right_dim,)), ((), ())), preferred_element_type=F32
    )


def dot3(left, right, left_dim=1, right_dim=0):
    left_high, left_low = left
    right_high, right_low = right
    return dot(left_high, right_high, left_dim, right_dim) + (
        dot(left_high, right_low, left_dim, right_dim)
        + dot(left_low, right_high, left_dim, right_dim)
    )


def norm_parts(values):
    average = jnp.mean(values, axis=-1, keepdims=True)
    centred = values - average
    spread = jnp.mean(centred * centred, axis=-1, keepdims=True)
    inverse = lax.rsqrt(spread + EPSILON)
    return centred * inverse, inverse


def norm_back(grad_out, unit_rows, inverse, scale_gain):
    scaled = grad_out * scale_gain
    average_grad = jnp.mean(scaled, axis=-1, keepdims=True)
    project_grad = jnp.mean(scaled * unit_rows, axis=-1, keepdims=True)
    return inverse * (scaled - average_grad - unit_rows * project_grad)


def any_spec():
    return pl.BlockSpec(memory_space=pl.ANY)


def vmem_spec():
    return pl.BlockSpec(memory_space=pltpu.VMEM)


def smem_spec():
    return pl.BlockSpec(memory_space=pltpu.SMEM)


def shape(*dims):
    return jax.ShapeDtypeStruct(dims, F32)


def row_of(vector):
    return vector[...][None, :]


def column_sum(values):
    return jnp.sum(values, axis=0, keepdims=True)


def split_weight(source, high, low, step=128):
    rows = source.shape[0]

    def body(index, carry):
        place = pl.ds(pl.multiple_of(index * step, step), step)
        high[place, :], low[place, :] = split(source[place, :])
        return carry

    lax.fori_loop(0, rows // step, body, 0)


def spaced(length):
    return (length + 7) // 8 * 8


def aligned_rows(token_count, cloud_count):
    return (token_count + 8 * cloud_count + TILE - 1) // TILE * TILE


def cloud_totals(lens):
    total, spread = jnp.int32(0), jnp.int32(0)
    for cloud in range(lens.shape[0]):
        total = total + lens[cloud]
        spread = spread + spaced(lens[cloud])
    return total, spread


def gather_rows(source, target, source_start, target_start, count):
    offset = source_start % 8
    base = source_start - offset
    kept = lax.broadcasted_iota(jnp.int32, (8, source.shape[1]), 0) < 8 - offset

    def turned(group):
        rows = pl.ds(start_of(base + group * 8), 8)
        return pltpu.roll(source[rows, :], (8 - offset) % 8, 0)

    def body(group, current):
        following = turned(group + 1)
        target[pl.ds(start_of(target_start + group * 8), 8), :] = jnp.where(kept, current, following)
        return following

    lax.fori_loop(0, (count + 7) // 8, body, turned(0))


def scatter_rows(source, target, source_start, target_start, count):
    offset = target_start % 8
    base = target_start - offset
    kept = lax.broadcasted_iota(jnp.int32, (8, source.shape[1]), 0) < offset

    def body(group, before):
        following = pltpu.roll(source[pl.ds(start_of(source_start + group * 8), 8), :], offset, 0)
        target[pl.ds(start_of(base + group * 8), 8), :] = jnp.where(kept, before, following)
        return following

    lax.fori_loop(0, (offset + count + 7) // 8, body, target[pl.ds(start_of(base), 8), :])


def restore_rows(lens, source, target, token_count):
    def cloud(index, carry):
        start, spaced_start = carry
        scatter_rows(source, target, spaced_start, start, lens[index])
        return start + lens[index], spaced_start + spaced(lens[index])

    target[0:8, :] = jnp.zeros((8, target.shape[1]), target.dtype)
    total, _ = lax.fori_loop(0, lens.shape[0], cloud, (jnp.int32(0), jnp.int32(0)))
    places = lax.broadcasted_iota(jnp.int32, (8, target.shape[1]), 0)

    def blank(group, carry):
        rows = pl.ds(start_of(group * 8), 8)
        target[rows, :] = jnp.where(places + group * 8 < total, target[rows, :], 0.0)
        return carry

    lax.fori_loop(total // 8, token_count // 8, blank, 0)


def start_of(place):
    return pl.multiple_of(place, 8)


def gelu_parts(pre_act):
    cumulative = 0.5 * (1.0 + lax.erf(pre_act * (1.0 / math.sqrt(2.0))))
    density = jnp.exp(-0.5 * pre_act * pre_act) * (1.0 / math.sqrt(2.0 * math.pi))
    return pre_act * cumulative, cumulative + pre_act * density


def slot_place(relative, part, devices):
    x, y, rest = (relative >> 1) & 1, (relative >> 2) & 1, relative >> 3
    major, minor = (x, y) if part == 0 else (y, x)
    return relative & 1, major * (devices // 4) + minor * (devices // 8) + rest


def tile_list(shapes):
    return [
        (which, row, column)
        for which, (rows, columns) in enumerate(shapes)
        for row in range(0, rows, 8)
        for column in range(0, columns, 128)
    ]


def atom_tiles(shapes, devices):
    return -(-len(tile_list(shapes)) // (2 * devices))


def slots_shape(shapes, devices):
    return (2, devices // 2, atom_tiles(shapes, devices) * 8, 128)


def pack_tiles(sources, pack, devices):
    me = lax.axis_index("dp")
    tiles = tile_list([source.shape for source in sources])
    each = atom_tiles([source.shape for source in sources], devices)
    for atom in range(-(-len(tiles) // each)):
        part, owner = atom // devices, atom % devices
        bit, place = slot_place(me ^ owner, part, devices)
        for number, (which, row, column) in enumerate(tiles[atom * each : atom * each + each]):
            pack[bit, part, place, number * 8 : number * 8 + 8, :] = sources[which][
                row : row + 8, column : column + 128
            ]


def unpack_tiles(pack, targets, devices, scale):
    me = lax.axis_index("dp")
    tiles = tile_list([target.shape for target in targets])
    each = atom_tiles([target.shape for target in targets], devices)
    for atom in range(-(-len(tiles) // each)):
        part, owner = atom // devices, atom % devices
        bit, place = slot_place(me ^ owner, part, devices)
        for number, (which, row, column) in enumerate(tiles[atom * each : atom * each + each]):
            piece = pack[bit, part, place, number * 8 : number * 8 + 8, :]
            targets[which][row : row + 8, column : column + 128] = (
                piece if scale is None else piece * scale
            )


def swap(values, bits, devices):
    return lax.ppermute(values, "dp", [(device, device ^ bits) for device in range(devices)])


def rest_groups(devices):
    count = (devices // 8).bit_length() - 1
    groups = []
    while count:
        step = 2 if count >= 2 else 1
        count -= step
        groups.append((3 + count, 1 << step))
    return groups


class DeviceSum:
    def __init__(self, keep, send, devices):
        self.devices = devices
        self.groups = rest_groups(devices)
        self.keep, self.send = keep, send
        self.stage = 0
        self.last = 5 + 2 * len(self.groups)

    def start(self):
        devices, stage, count = self.devices, self.stage, len(self.groups)
        if stage == 0:
            self.moving = [swap(self.send, 1, devices)]
        elif stage <= 2:
            size = devices // (4, 8)[stage - 1]
            bits = ((2, 4), (4, 2))[stage - 1]
            self.moving = [swap(half[size:], bit, devices) for half, bit in zip(self.halves, bits)]
            self.halves = [half[:size] for half in self.halves]
        elif stage < 3 + count:
            shift, size = self.groups[stage - 3]
            total = self.total.reshape((size, -1) + self.total.shape[1:])
            self.moving = [swap(total[slot], slot << shift, devices) for slot in range(1, size)]
            self.total = total[0]
        elif stage < 3 + 2 * count:
            shift, size = self.groups[3 + 2 * count - 1 - stage]
            self.moving = [swap(self.total, slot << shift, devices) for slot in range(1, size)]
        elif stage < 5 + 2 * count:
            bits = ((4, 2), (2, 4))[stage - 3 - 2 * count]
            self.moving = [swap(half, bit, devices) for half, bit in zip(self.halves, bits)]
        else:
            self.moving = [swap(self.total, 1, devices)]

    def finish(self):
        stage, count = self.stage, len(self.groups)
        if stage == 0:
            total = self.keep + self.moving[0]
            self.halves = [total[0], total[1]]
        elif stage <= 2:
            self.halves = [half + moved for half, moved in zip(self.halves, self.moving)]
            if stage == 2:
                self.total = jnp.stack(self.halves, axis=1)
        elif stage < 3 + count:
            self.total = sum(self.moving, self.total)
        elif stage < 3 + 2 * count:
            self.total = jnp.concatenate([self.total] + self.moving, axis=0)
            if stage == 2 + 2 * count:
                self.halves = [self.total[:, 0], self.total[:, 1]]
        elif stage < 5 + 2 * count:
            self.halves = [jnp.concatenate([half, moved]) for half, moved in zip(self.halves, self.moving)]
            if stage == 4 + 2 * count:
                self.total = jnp.stack(self.halves)
        else:
            self.theirs = self.moving[0]
        self.stage += 1

    def done(self):
        return self.stage > self.last


def beside(sums, outs):
    sums = [one for one in sums if not one.done()]
    for one in sums:
        one.start()
    moving, outs = lax.optimization_barrier(([one.moving for one in sums], outs))
    for one, moved in zip(sums, moving):
        one.moving = moved
        one.finish()
    return outs


def run_out(sums):
    while not all(one.done() for one in sums):
        for one in sums:
            if not one.done():
                one.start()
                one.finish()


def attend_kernel(
    lens, tokens_hbm, owner, prenorm_gain, prenorm_shift, attention_in,
    tokens_out, joint_out, attended_out, owners, used_out,
    raw, tokens, joint, attended, in_high, in_low, token_sem, joint_sem, out_sems,
):
    token_count = owner.shape[1]
    tiles = tokens.shape[0] // TILE
    width = tokens.shape[1]
    total, spread = cloud_totals(lens)
    used = (spread + TILE - 1) // TILE
    used_out[0] = used

    def tile_rows(index):
        return pl.ds(pl.multiple_of(index * TILE, TILE), TILE)

    token_copy = pltpu.make_async_copy(tokens_hbm, raw.at[pl.ds(0, token_count)], token_sem)
    token_copy.start()
    split_weight(attention_in, in_high, in_low)
    raw[token_count:, :] = jnp.zeros((raw.shape[0] - token_count, width), F32)
    owners[...] = jnp.full(owners.shape, -2, jnp.int32)
    token_copy.wait()
    wide = lax.broadcasted_iota(jnp.int32, (1, 2 * CLOUD_MAX), 1)
    tokens[tile_rows(used - 1), :] = jnp.zeros((TILE, width), F32)

    def place_cloud(index, carry):
        start, spaced_start = carry
        length = lens[index]
        gather_rows(raw, tokens, start, spaced_start, length)
        base = jnp.minimum(start // 128, token_count // 128 - 2)
        offset, spaced_offset = start - base * 128, spaced_start % 128
        slots = owner[:, pl.ds(pl.multiple_of(base * 128, 128), 256)]
        slots = pltpu.roll(slots, (spaced_offset - offset) % 256, 1)
        lanes = pl.ds(pl.multiple_of(spaced_start // 128 * 128, 128), 256)
        inside = jnp.logical_and(wide >= spaced_offset, wide < spaced_offset + length)
        owners[:, lanes] = jnp.where(inside, slots, owners[:, lanes])
        return start + length, spaced_start + spaced(length)

    lax.fori_loop(0, lens.shape[0], place_cloud, (jnp.int32(0), jnp.int32(0)))

    def joint_copies(index):
        rows = tile_rows(index)
        return [
            pltpu.make_async_copy(joint.at[rows], joint_out.at[rows], joint_sem.at[index]),
            pltpu.make_async_copy(tokens.at[rows], tokens_out.at[rows], out_sems.at[0, index]),
        ]

    def joint_tile(index, carry):
        rows = tile_rows(index)
        unit, _ = norm_parts(tokens[rows, :])
        normed = split(unit * row_of(prenorm_gain) + row_of(prenorm_shift))
        joint[rows, :] = dot3(normed, (in_high[...], in_low[...]))
        for copy in joint_copies(index):
            copy.start()
        return carry

    lax.fori_loop(0, used, joint_tile, 0)
    tail = pl.ds(pl.multiple_of(used * TILE, TILE), CLOUD_MAX)
    joint[tail, :] = jnp.zeros((CLOUD_MAX, joint.shape[1]), F32)
    tail_copy = pltpu.make_async_copy(joint.at[tail], joint_out.at[tail], joint_sem.at[tiles])
    tail_copy.start()
    attended[tile_rows(used - 1), :] = jnp.zeros((TILE, width), F32)

    lane = lax.broadcasted_iota(jnp.int32, (CLOUD_MAX, 128), 1)
    first_head = lane < 64
    wide_lane = lax.broadcasted_iota(jnp.int32, (2 * CLOUD_MAX, CLOUD_MAX), 1)
    empty = jnp.zeros((CLOUD_MAX, 128), BF16)

    def cloud(index, start):
        length = lens[index]
        rows = pl.ds(start_of(start), CLOUD_MAX)
        inside = wide_lane < length
        pairs = range(HEADS // 2)
        lefts, rights = [], []
        for pair in pairs:
            query = joint[rows, pair * 128 : pair * 128 + 128] * 0.125
            key_high, key_low = split(joint[rows, width + pair * 128 : width + pair * 128 + 128])
            both = jnp.concatenate(
                [jnp.where(first_head, query, 0.0), jnp.where(first_head, 0.0, query)], axis=0
            )
            lefts.append(jnp.concatenate(split(both), axis=1))
            rights.append(
                jnp.concatenate(
                    [
                        jnp.concatenate([key_high, key_high], axis=1),
                        jnp.concatenate([key_low, empty], axis=1),
                    ],
                    axis=0,
                )
            )
        scores = [dot(left, right, 1, 1) for left, right in zip(lefts, rights)]
        scores = [jnp.where(inside, score[:, :128] + score[:, 128:], -1e30) for score in scores]
        peaks = [jnp.max(score, axis=-1, keepdims=True) for score in scores]
        weights = [jnp.exp(score - peak) for score, peak in zip(scores, peaks)]
        scales = [1.0 / jnp.sum(weight, axis=-1, keepdims=True) for weight in weights]
        lefts = [jnp.concatenate(split(weight * scale), axis=1) for weight, scale in zip(weights, scales)]
        rights = []
        for pair in pairs:
            value_high, value_low = split(
                joint[rows, 2 * width + pair * 128 : 2 * width + pair * 128 + 128]
            )
            rights.append(
                jnp.concatenate(
                    [
                        jnp.concatenate([value_high, value_low], axis=1),
                        jnp.concatenate([value_high, empty], axis=1),
                    ],
                    axis=0,
                )
            )
        mixed = [dot(left, right) for left, right in zip(lefts, rights)]
        for pair in pairs:
            both = mixed[pair][:, :128] + mixed[pair][:, 128:]
            attended[rows, pair * 128 : pair * 128 + 128] = jnp.where(
                first_head, both[:CLOUD_MAX], both[CLOUD_MAX:]
            )
        return start + spaced(length)

    lax.fori_loop(0, lens.shape[0], cloud, jnp.int32(0))

    def attended_copy(index):
        rows = tile_rows(index)
        return pltpu.make_async_copy(attended.at[rows], attended_out.at[rows], out_sems.at[1, index])

    def begin(index, carry):
        attended_copy(index).start()
        return carry

    def finish(index, carry):
        attended_copy(index).wait()
        for copy in joint_copies(index):
            copy.wait()
        return carry

    lax.fori_loop(0, used, begin, 0)
    tail_copy.wait()
    lax.fori_loop(0, used, finish, 0)


def run_attend(tokens, lens, owner, prenorm_gain, prenorm_shift, attention_in):
    token_count, width = tokens.shape
    joint_width = attention_in.shape[1]
    spaced_count = aligned_rows(token_count, lens.shape[0])
    tiles = spaced_count // TILE
    return pl.pallas_call(
        attend_kernel,
        out_shape=(
            shape(spaced_count, width),
            shape(spaced_count + CLOUD_MAX, joint_width),
            shape(spaced_count, width),
            jax.ShapeDtypeStruct((1, spaced_count + 256), jnp.int32),
            jax.ShapeDtypeStruct((1,), jnp.int32),
        ),
        in_specs=[smem_spec(), any_spec()] + [vmem_spec()] * 4,
        out_specs=[any_spec()] * 3 + [vmem_spec(), smem_spec()],
        scratch_shapes=[
            pltpu.VMEM((token_count + 16, width), F32),
            pltpu.VMEM((spaced_count, width), F32),
            pltpu.VMEM((spaced_count + CLOUD_MAX, joint_width), F32),
            pltpu.VMEM((spaced_count + CLOUD_MAX, width), F32),
            pltpu.VMEM(attention_in.shape, BF16),
            pltpu.VMEM(attention_in.shape, BF16),
            pltpu.SemaphoreType.DMA,
            pltpu.SemaphoreType.DMA((tiles + 1,)),
            pltpu.SemaphoreType.DMA((2, tiles)),
        ],
        compiler_params=pltpu.CompilerParams(vmem_limit_bytes=VMEM_BYTES),
        name="attend",
    )(lens, tokens, owner, prenorm_gain, prenorm_shift, attention_in)


def block_kernel(
    devices, lens, used_ref, attended, tokens, owners, targets, attention_out,
    attention_shift, midnorm_gain, midnorm_shift, expand_weight, expand_shift, reduce_weight,
    reduce_shift, lastnorm_gain, lastnorm_shift, head_turned, head_shift,
    middle, slope, grad_stream, predicted, keep_out, send_out,
    sum_reduce, sum_head, small, pack,
    out_high, out_low, expand_high, expand_low, reduce_high, reduce_low,
    head_high, head_low, turned_high, turned_low, target_parts, pred_rows, true_rows, distance, second,
    col_low, col_sum, shift_column, pack_sem,
):
    index = pl.program_id(0)
    used = used_ref[0]
    slot_count, width_out = targets.shape
    points = width_out // 3
    width = middle.shape[1]
    copies = [
        pltpu.make_async_copy(pack.at[0], keep_out, pack_sem.at[0]),
        pltpu.make_async_copy(pack.at[1], send_out, pack_sem.at[1]),
    ]

    @pl.when(index == 0)
    def _():
        split_weight(attention_out, out_high, out_low)
        split_weight(expand_weight, expand_high, expand_low)
        split_weight(reduce_weight, reduce_high, reduce_low)
        shift_column[...] = jnp.broadcast_to(row_of(head_shift), (8, width_out)).T[:, :1]
        turned_high[...], turned_low[...] = split(head_turned[...])
        head_high[...], head_low[...] = split(head_turned[...].T)
        high, low = split(targets[...].T)
        target_parts[:width_out, :] = high
        target_parts[width_out:, :] = low
        small[...] = jnp.zeros_like(small)
        sum_reduce[...] = jnp.zeros_like(sum_reduce)
        sum_head[...] = jnp.zeros_like(sum_head)

    def chamfer_half(half):
        xs = [pred_rows[half, pl.ds(c, points, stride=3), :] for c in range(3)]

        def first(j, row_low):
            gap = [xs[c] - true_rows[half, pl.ds(3 * j + c, 1), :] for c in range(3)]
            apart = gap[0] * gap[0] + gap[1] * gap[1] + gap[2] * gap[2]
            distance[j] = apart
            lowest = jnp.min(apart, axis=0, keepdims=True)
            weight = jnp.exp(lowest - apart)
            inside = column_sum(weight)
            col_low[pl.ds(j, 1), :] = lowest
            col_sum[pl.ds(j, 1), :] = inside
            second[j] = weight * (1.0 / (points * inside))
            return jnp.minimum(row_low, apart)

        row_low = lax.fori_loop(
            0, points, first, jnp.full((points, 128), jnp.inf, F32), unroll=8
        )

        def middle_pass(j, row_sum):
            weight = jnp.exp(row_low - distance[j])
            distance[j] = weight
            return row_sum + weight

        row_sum = lax.fori_loop(0, points, middle_pass, jnp.zeros((points, 128), F32), unroll=8)
        row_scale = 1.0 / (points * row_sum)

        def last(j, carry):
            weight = second[j] + distance[j] * row_scale
            return (carry[0] + weight,) + tuple(
                carry[1 + c] + weight * true_rows[half, pl.ds(3 * j + c, 1), :] for c in range(3)
            )

        zero = jnp.zeros((points, 128), F32)
        sums = lax.fori_loop(0, points, last, (zero,) * 4, unroll=8)
        terms = column_sum(row_low - jnp.log(row_sum * (1.0 / points))) + column_sum(
            col_low[...] - jnp.log(col_sum[...] * (1.0 / points))
        )
        grads = [2.0 * (sums[0] * xs[c] - sums[1 + c]) for c in range(3)]
        return terms * (1.0 / points), grads

    @pl.when(index < used)
    def _():
        slots = lax.broadcasted_iota(jnp.int32, (slot_count, TILE), 0)
        slot_row = owners[...]
        valid_lane = slot_row > -2
        valid_row = jnp.broadcast_to(valid_lane.astype(F32), (8, TILE)).T[:, :1] > 0.5
        mixed = dot3(split(attended[...]), (out_high[...], out_low[...])) + row_of(attention_shift)
        mid = tokens[...] + mixed
        middle[...] = mid
        unit, _ = norm_parts(mid)
        normed = split(unit * row_of(midnorm_gain) + row_of(midnorm_shift))
        pre_act = dot3(normed, (expand_high[...], expand_low[...])) + row_of(expand_shift)
        hidden, steep = gelu_parts(pre_act)
        slope[...] = steep
        hidden = split(hidden)
        branch = dot3(hidden, (reduce_high[...], reduce_low[...])) + row_of(reduce_shift)
        stream = mid + branch
        unit, inverse = norm_parts(stream)
        normed = split(unit * row_of(lastnorm_gain) + row_of(lastnorm_shift))
        pred = dot3((turned_high[...], turned_low[...]), normed, 1, 1) + shift_column[...]
        pred = jnp.where(valid_lane, pred, 0.0)
        for half in range(TILE // 128):
            pred_rows[half] = pred[:, half * 128 : half * 128 + 128]
        predicted[...] = pred.T
        chosen = (slots == slot_row).astype(F32).astype(BF16)
        true_points = dot(target_parts[...], chosen)
        true_points = true_points[:width_out] + true_points[width_out:]
        for half in range(TILE // 128):
            true_rows[half] = true_points[:, half * 128 : half * 128 + 128]
        masked = slot_row >= 0
        losses = []
        for half in range(TILE // 128):
            terms, grads = chamfer_half(half)
            losses.append(terms)
            for c in range(3):
                pred_rows[half, pl.ds(c, points, stride=3), :] = grads[c]
        grad_turned = jnp.concatenate([pred_rows[half] for half in range(TILE // 128)], axis=1)
        grad_turned = jnp.where(masked, grad_turned, 0.0)
        loss = jnp.where(masked, jnp.concatenate(losses, axis=1), 0.0)
        grad_pred = grad_turned.T
        sum_head[...] += dot3(split(grad_turned), normed)
        grad_last = dot3(split(grad_pred), (head_high[...], head_low[...]), 1, 1)
        grad_str = norm_back(grad_last, unit, inverse, row_of(lastnorm_gain))
        grad_stream[...] = grad_str
        sum_reduce[...] += dot3(split(grad_str.T), hidden)
        small[0:1, :TILE] += loss
        small[1:2, :TILE] += masked.astype(F32)
        small[2:3, :] += column_sum(jnp.where(valid_row, stream * stream, 0.0))
        small[3:4, :] += column_sum(jnp.where(valid_row, mixed * mixed, 0.0))
        small[4:5, :] += column_sum(jnp.where(valid_row, branch * branch, 0.0))
        small[5:6, :] += column_sum(grad_last * unit)
        small[6:7, :] += column_sum(grad_last)
        small[7:8, :] += column_sum(grad_str)
        small[8:9, :width_out] += column_sum(grad_pred)
        small[9:10, :TILE] += valid_lane.astype(F32)

    @pl.when(index == used - 1)
    def _():
        pack_tiles([sum_reduce, sum_head, small], pack, devices)
        for copy in copies:
            copy.start()

    @pl.when(index == pl.num_programs(0) - 1)
    def _():
        for copy in copies:
            copy.wait()


def row_map(index, used):
    return (jnp.minimum(index, used[0] - 1), 0)


def rows_spec(columns, step=TILE):
    return pl.BlockSpec((step, columns), row_map)


def whole_spec(array):
    return pl.BlockSpec(array.shape, lambda index, used: (0,) * len(array.shape))


def run_block(used, lens, attended, tokens, owners, targets, weights, devices):
    spaced_count, width = tokens.shape
    hidden_width = weights["expand_weight"].shape[1]
    slot_count, width_out = targets.shape
    points = width_out // 3
    names = (
        "attention_out", "attention_shift",
        "midnorm_gain", "midnorm_shift", "expand_weight", "expand_shift", "reduce_weight",
        "reduce_shift", "lastnorm_gain", "lastnorm_shift", "head_turned", "head_shift",
    )
    extra = [targets] + [weights[name] for name in names]
    pairs = []
    for name in ("attention_out", "expand_weight", "reduce_weight"):
        pairs += [pltpu.VMEM(weights[name].shape, BF16)] * 2
    pairs += [pltpu.VMEM((width, width_out), BF16)] * 2 + [pltpu.VMEM((width_out, width), BF16)] * 2
    chunk = block_chunk(width, hidden_width, width_out)
    slots = slots_shape(chunk, devices)
    return pl.pallas_call(
        lambda used, lens, *refs: block_kernel(devices, lens, used, *refs),
        out_shape=(
            shape(spaced_count, width),
            shape(spaced_count, hidden_width),
            shape(spaced_count, width),
            shape(spaced_count, width_out),
            shape(*slots),
            shape(*slots),
        ),
        grid_spec=pltpu.PrefetchScalarGridSpec(
            num_scalar_prefetch=1,
            grid=(spaced_count // TILE,),
            in_specs=[
                smem_spec(),
                rows_spec(width),
                rows_spec(width),
                pl.BlockSpec((1, TILE), lambda index, used: (0, jnp.minimum(index, used[0] - 1))),
            ]
            + [whole_spec(array) for array in extra],
            out_specs=[rows_spec(width), rows_spec(hidden_width), rows_spec(width), rows_spec(width_out)]
            + [any_spec()] * 2,
            scratch_shapes=[pltpu.VMEM(dims, F32) for dims in chunk]
            + [pltpu.VMEM((2,) + slots, F32)]
            + pairs
            + [
                pltpu.VMEM((2 * width_out, slot_count), BF16),
                pltpu.VMEM((TILE // 128, width_out, 128), F32),
                pltpu.VMEM((TILE // 128, width_out, 128), F32),
                pltpu.VMEM((points, points, 128), F32),
                pltpu.VMEM((points, points, 128), F32),
                pltpu.VMEM((points, 128), F32),
                pltpu.VMEM((points, 128), F32),
                pltpu.VMEM((width_out, 1), F32),
                pltpu.SemaphoreType.DMA((2,)),
            ],
        ),
        compiler_params=pltpu.CompilerParams(vmem_limit_bytes=VMEM_BYTES),
        name="block",
    )(used, lens, attended, tokens, owners, *extra)


def block_chunk(width, hidden_width, width_out):
    return [(width, hidden_width), (width_out, width), (16, width)]


def mlp_chunk(width, hidden_width):
    return [(width, hidden_width), (width, width), (8, width)]


def in_chunk(width):
    return [(width, 3 * width), (8, width)]


def mlp_back_kernel(
    devices, used_ref, grad_stream, slope, middle, attended, midnorm_gain, midnorm_shift, reduce_weight,
    expand_weight, attention_out,
    grad_middle, grad_attended, keep_out, send_out,
    sum_expand, sum_out, small, pack,
    reduce_high, reduce_low, expand_high, expand_low, out_high, out_low, pack_sem,
):
    index = pl.program_id(0)
    used = used_ref[0]
    width = middle.shape[1]
    copies = [
        pltpu.make_async_copy(pack.at[0], keep_out, pack_sem.at[0]),
        pltpu.make_async_copy(pack.at[1], send_out, pack_sem.at[1]),
    ]

    @pl.when(index == 0)
    def _():
        split_weight(reduce_weight, reduce_high, reduce_low)
        split_weight(expand_weight, expand_high, expand_low)
        split_weight(attention_out, out_high, out_low)
        sum_expand[...] = jnp.zeros_like(sum_expand)
        sum_out[...] = jnp.zeros_like(sum_out)
        small[...] = jnp.zeros_like(small)

    @pl.when(index < used)
    def _():
        grad_str = grad_stream[...]
        unit, inverse = norm_parts(middle[...])
        normed = unit * row_of(midnorm_gain) + row_of(midnorm_shift)
        grad_pre = dot3(split(grad_str), (reduce_high[...], reduce_low[...]), 1, 1) * slope[...]
        parts = split(grad_pre)
        sum_expand[...] += dot3(split(normed.T), parts)
        grad_normed = dot3(parts, (expand_high[...], expand_low[...]), 1, 1)
        grad_mid = grad_str + norm_back(grad_normed, unit, inverse, row_of(midnorm_gain))
        grad_middle[...] = grad_mid
        parts = split(grad_mid)
        grad_attended[...] = dot3(parts, (out_high[...], out_low[...]), 1, 1)
        sum_out[...] += dot3(split(attended[...].T), parts)
        shift_sum = column_sum(grad_pre)
        for part in range(shift_sum.shape[1] // width):
            small[part : part + 1, :] += shift_sum[:, part * width : part * width + width]
        small[4:5, :] += column_sum(grad_normed * unit)
        small[5:6, :] += column_sum(grad_normed)
        small[6:7, :] += column_sum(grad_mid)

    @pl.when(index >= used)
    def _():
        grad_attended[...] = jnp.zeros_like(grad_attended)

    @pl.when(index == used - 1)
    def _():
        pack_tiles([sum_expand, sum_out, small], pack, devices)
        for copy in copies:
            copy.start()

    @pl.when(index == pl.num_programs(0) - 1)
    def _():
        for copy in copies:
            copy.wait()


def run_mlp_back(used, grad_stream, slope, middle, attended, weights, devices):
    token_count, width = middle.shape
    hidden_width = slope.shape[1]

    def next_map(index, used):
        return (jnp.minimum(index, used[0]), 0)

    names = ("midnorm_gain", "midnorm_shift", "reduce_weight", "expand_weight", "attention_out")
    extra = [weights[name] for name in names]
    chunk = mlp_chunk(width, hidden_width)
    slots = slots_shape(chunk, devices)
    pairs = []
    for name in names[2:]:
        pairs += [pltpu.VMEM(weights[name].shape, BF16)] * 2
    return pl.pallas_call(
        lambda *refs: mlp_back_kernel(devices, *refs),
        out_shape=(
            shape(token_count, width), shape(token_count + CLOUD_MAX, width), shape(*slots), shape(*slots),
        ),
        grid_spec=pltpu.PrefetchScalarGridSpec(
            num_scalar_prefetch=1,
            grid=(token_count // TILE,),
            in_specs=[rows_spec(width), rows_spec(hidden_width), rows_spec(width), rows_spec(width)]
            + [whole_spec(array) for array in extra],
            out_specs=[rows_spec(width), pl.BlockSpec((TILE, width), next_map)] + [any_spec()] * 2,
            scratch_shapes=[pltpu.VMEM(dims, F32) for dims in chunk]
            + [pltpu.VMEM((2,) + slots, F32)]
            + pairs
            + [pltpu.SemaphoreType.DMA((2,))],
        ),
        compiler_params=pltpu.CompilerParams(vmem_limit_bytes=VMEM_BYTES),
        name="mlp_back",
    )(used, grad_stream, slope, middle, attended, *extra)


def attention_back_kernel(
    first, last, lens, joint_hbm, grad_hbm, *refs,
):
    joint_grad_out, joint, grad_rows, joint_grad, in_sems, out_sem = refs[-6:]
    width = grad_rows.shape[2]
    skipped = jnp.int32(0)
    for index in range(first):
        skipped = skipped + spaced(lens[index])

    lane = lax.broadcasted_iota(jnp.int32, (CLOUD_MAX, 128), 1)
    first_head = lane < 64
    key_place = lax.broadcasted_iota(jnp.int32, (CLOUD_MAX, 2 * CLOUD_MAX), 0)
    query_place = lax.broadcasted_iota(jnp.int32, (CLOUD_MAX, 2 * CLOUD_MAX), 1) % CLOUD_MAX
    empty = jnp.zeros((CLOUD_MAX, 128), BF16)

    def both_heads(values):
        return jnp.concatenate(
            [jnp.where(first_head, values, 0.0), jnp.where(first_head, 0.0, values)], axis=0
        )

    def fetch(start, slot):
        rows = pl.ds(start_of(start), CLOUD_MAX)
        return [
            pltpu.make_async_copy(joint_hbm.at[rows], joint.at[slot], in_sems.at[0, slot]),
            pltpu.make_async_copy(grad_hbm.at[rows], grad_rows.at[slot], in_sems.at[1, slot]),
        ]

    def store(start, slot):
        rows = pl.ds(start_of(start), CLOUD_MAX)
        return pltpu.make_async_copy(joint_grad.at[slot], joint_grad_out.at[rows], out_sem)

    for copy in fetch(skipped, 0):
        copy.start()

    def cloud(index, carry):
        before, start = carry
        length = lens[index]
        slot = lax.rem(index - first, 2)
        following = start + spaced(length)

        @pl.when(index + 1 < last)
        def _():
            for copy in fetch(following, 1 - slot):
                copy.start()

        for copy in fetch(start, slot):
            copy.wait()
        inside = key_place < length
        live = jnp.logical_and(inside, query_place < length)
        pairs = range(HEADS // 2)
        at = [
            [slice(part * width + pair * 128, part * width + pair * 128 + 128) for part in range(3)]
            for pair in pairs
        ]
        query = [split(both_heads(joint[slot, :, at[pair][0]] * 0.125)) for pair in pairs]
        key = [split(joint[slot, :, at[pair][1]]) for pair in pairs]
        value = [split(joint[slot, :, at[pair][2]]) for pair in pairs]
        grad = [split(both_heads(grad_rows[slot, :, at[pair][0]])) for pair in pairs]
        scores = [dot3(key[pair], query[pair], 1, 1) for pair in pairs]
        grad_probs = [dot3(value[pair], grad[pair], 1, 1) for pair in pairs]
        scores = [jnp.where(inside, score, -1e30) for score in scores]
        peaks = [jnp.max(score, axis=0, keepdims=True) for score in scores]
        weights = [jnp.exp(score - peak) for score, peak in zip(scores, peaks)]
        scales = [1.0 / column_sum(weight) for weight in weights]
        probs = [jnp.where(live, weight * scale, 0.0) for weight, scale in zip(weights, scales)]
        shared = [column_sum(prob * grad_prob) for prob, grad_prob in zip(probs, grad_probs)]
        grad_scores = [probs[pair] * (grad_probs[pair] - shared[pair]) for pair in pairs]
        turned = [grad_score.T for grad_score in grad_scores]
        for pair in pairs:
            joint_grad[slot, :, at[pair][2]] = dot3(split(probs[pair]), grad[pair])
        for pair in pairs:
            joint_grad[slot, :, at[pair][1]] = dot3(split(grad_scores[pair]), query[pair])
        for pair in pairs:
            left = jnp.concatenate(split(turned[pair]), axis=1)
            right = jnp.concatenate(
                [
                    jnp.concatenate([key[pair][0], key[pair][1]], axis=1),
                    jnp.concatenate([key[pair][0], empty], axis=1),
                ],
                axis=0,
            )
            grad_query = dot(left, right)
            grad_query = (grad_query[:, :128] + grad_query[:, 128:]) * 0.125
            joint_grad[slot, :, at[pair][0]] = jnp.where(
                first_head, grad_query[:CLOUD_MAX], grad_query[CLOUD_MAX:]
            )
        @pl.when(index > first)
        def _():
            store(before, 1 - slot).wait()

        store(start, slot).start()
        return start, following

    before, _ = lax.fori_loop(first, last, cloud, (skipped, skipped))
    store(before, (last - 1 - first) % 2).wait()


def run_attention_back(first, last, lens, joint, grad_attended, joint_grad=None):
    width = grad_attended.shape[1]
    joint_width = joint.shape[1]
    more = [] if joint_grad is None else [joint_grad]
    return pl.pallas_call(
        lambda *refs: attention_back_kernel(first, last, *refs),
        out_shape=shape(*joint.shape),
        in_specs=[smem_spec()] + [any_spec()] * (2 + len(more)),
        out_specs=any_spec(),
        scratch_shapes=[
            pltpu.VMEM((2, CLOUD_MAX, joint_width), F32),
            pltpu.VMEM((2, CLOUD_MAX, width), F32),
            pltpu.VMEM((2, CLOUD_MAX, joint_width), F32),
            pltpu.SemaphoreType.DMA((2, 2)),
            pltpu.SemaphoreType.DMA,
        ],
        input_output_aliases={3: 0} if more else {},
        compiler_params=pltpu.CompilerParams(vmem_limit_bytes=VMEM_BYTES),
        name="attention_back",
    )(lens, joint, grad_attended, *more)


def in_back_kernel(
    devices, used_ref, lens, grad_joint, tokens, prenorm_gain, prenorm_shift, attention_in,
    keep_out, send_out,
    sum_in, small, joint_sum, pack, pack_sem,
):
    index = pl.program_id(0)
    used = used_ref[0]
    width = tokens.shape[1]
    copies = [
        pltpu.make_async_copy(pack.at[0], keep_out, pack_sem.at[0]),
        pltpu.make_async_copy(pack.at[1], send_out, pack_sem.at[1]),
    ]

    @pl.when(index == 0)
    def _():
        sum_in[...] = jnp.zeros_like(sum_in)
        joint_sum[...] = jnp.zeros_like(joint_sum)

    @pl.when(index < used)
    def _():
        _, spread = cloud_totals(lens)
        live = lax.broadcasted_iota(jnp.int32, (TILE, 1), 0) + index * TILE < spread
        unit, _ = norm_parts(tokens[...])
        grads = jnp.where(live, grad_joint[...], 0.0)
        joint_sum[...] += column_sum(grads)
        sum_in[...] += dot3(split(unit.T), split(grads))

    @pl.when(index == used - 1)
    def _():
        weighted = split(sum_in[...] * attention_in[...])
        ones = jnp.ones((8, joint_sum.shape[1]), BF16)
        small[...] = jnp.zeros_like(small)
        small[0:1, :] = (dot(ones, weighted[0], 1, 1) + dot(ones, weighted[1], 1, 1))[:1]
        columns = split(jnp.broadcast_to(joint_sum[...], (8, joint_sum.shape[1])))
        small[1:2, :] = dot3(columns, split(attention_in[...]), 1, 1)[:1]
        gains = jnp.broadcast_to(row_of(prenorm_gain), (8, width)).T[:, :1]
        shifts = jnp.broadcast_to(row_of(prenorm_shift), (8, width)).T[:, :1]
        sum_in[...] = sum_in[...] * gains + shifts * joint_sum[...]
        pack_tiles([sum_in, small], pack, devices)
        for copy in copies:
            copy.start()

    @pl.when(index == pl.num_programs(0) - 1)
    def _():
        for copy in copies:
            copy.wait()


def run_in_back(used, lens, grad_joint, tokens, weights, devices):
    spaced_count, width = tokens.shape
    joint_width = grad_joint.shape[1]
    extra = [weights[name] for name in ("prenorm_gain", "prenorm_shift", "attention_in")]
    chunk = in_chunk(width)
    slots = slots_shape(chunk, devices)
    return pl.pallas_call(
        lambda used, lens, *refs: in_back_kernel(devices, used, lens, *refs),
        out_shape=(shape(*slots), shape(*slots)),
        grid_spec=pltpu.PrefetchScalarGridSpec(
            num_scalar_prefetch=1,
            grid=(spaced_count // TILE,),
            in_specs=[smem_spec(), rows_spec(joint_width), rows_spec(width)]
            + [whole_spec(array) for array in extra],
            out_specs=[any_spec()] * 2,
            scratch_shapes=[pltpu.VMEM(dims, F32) for dims in chunk]
            + [
                pltpu.VMEM((1, joint_width), F32),
                pltpu.VMEM((2,) + slots, F32),
                pltpu.SemaphoreType.DMA((2,)),
            ],
        ),
        compiler_params=pltpu.CompilerParams(vmem_limit_bytes=VMEM_BYTES),
        name="in_back",
    )(used, lens, grad_joint, tokens, *extra)


def input_kernel(
    used_ref, grad_joint, tokens, grad_middle, prenorm_gain, attention_in, spaced_grad, in_high, in_low,
):
    index = pl.program_id(0)

    @pl.when(index == 0)
    def _():
        split_weight(attention_in, in_high, in_low)

    @pl.when(index < used_ref[0])
    def _():
        unit, inverse = norm_parts(tokens[...])
        grad_normed = dot3(split(grad_joint[...]), (in_high[...], in_low[...]), 1, 1)
        spaced_grad[...] = grad_middle[...] + norm_back(grad_normed, unit, inverse, row_of(prenorm_gain))


def run_input(used, grad_joint, tokens, grad_middle, weights):
    spaced_count, width = tokens.shape
    extra = [weights["prenorm_gain"], weights["attention_in"]]
    return pl.pallas_call(
        input_kernel,
        out_shape=shape(spaced_count, width),
        grid_spec=pltpu.PrefetchScalarGridSpec(
            num_scalar_prefetch=1,
            grid=(spaced_count // TILE,),
            in_specs=[rows_spec(grad_joint.shape[1]), rows_spec(width), rows_spec(width)]
            + [whole_spec(array) for array in extra],
            out_specs=rows_spec(width),
            scratch_shapes=[pltpu.VMEM(weights["attention_in"].shape, BF16)] * 2,
        ),
        compiler_params=pltpu.CompilerParams(vmem_limit_bytes=VMEM_BYTES),
        name="input_grad",
    )(used, grad_joint, tokens, grad_middle, *extra)


def restore_kernel(lens, spaced_grad, spaced_pred, input_grad, predicted_turned, pred_rows):
    token_count = input_grad.shape[0]
    restore_rows(lens, spaced_grad, input_grad, token_count)
    restore_rows(lens, spaced_pred, pred_rows, token_count)
    for place in range(0, token_count, 128):
        predicted_turned[:, place : place + 128] = pred_rows[place : place + 128, :].T


def run_restore(lens, spaced_grad, spaced_pred, token_count):
    width, width_out = spaced_grad.shape[1], spaced_pred.shape[1]
    return pl.pallas_call(
        restore_kernel,
        out_shape=(shape(token_count, width), shape(width_out, token_count)),
        in_specs=[smem_spec()] + [vmem_spec()] * 2,
        out_specs=[vmem_spec()] * 2,
        scratch_shapes=[pltpu.VMEM((token_count, width_out), F32)],
        compiler_params=pltpu.CompilerParams(vmem_limit_bytes=VMEM_BYTES),
        name="restore",
    )(lens, spaced_grad, spaced_pred)


def gather_pack(mine, theirs, pack, sems):
    copies = [
        pltpu.make_async_copy(mine, pack.at[0], sems.at[0]),
        pltpu.make_async_copy(theirs, pack.at[1], sems.at[1]),
    ]
    for copy in copies:
        copy.start()
    for copy in copies:
        copy.wait()


def block_sums_kernel(
    devices, width_out, mine, theirs,
    reduce_out, head_out, lastnorm_gain, lastnorm_shift, reduce_shift, head_shift, loss_out, rms_out, scale_out,
    sum_reduce, small, pack, sems,
):
    gather_pack(mine, theirs, pack, sems)
    unpack_tiles(pack, [sum_reduce, head_out, small], devices, None)
    scale = 1.0 / jnp.sum(small[1:2, :], axis=1, keepdims=True)
    scale_out[...] = jnp.broadcast_to(scale, scale_out.shape)
    head_out[...] = head_out[...] * scale
    for row, target in ((5, lastnorm_gain), (6, lastnorm_shift), (7, reduce_shift)):
        target[...] = (small[row : row + 1, :] * scale)[0]
    head_shift[...] = (small[8:9, :] * scale)[0, : head_shift.shape[0]]
    loss_out[...] = jnp.broadcast_to(jnp.sum(small[0:1, :], axis=1, keepdims=True) * scale, loss_out.shape)
    counted = 1.0 / (jnp.sum(small[9:10, :], axis=1, keepdims=True) * small.shape[1])
    squares = jnp.sum(small[0:8, :], axis=1, keepdims=True)
    rms_out[...] = jnp.broadcast_to(jnp.sqrt(squares * counted), rms_out.shape)
    for place in range(0, reduce_out.shape[0], 128):
        reduce_out[place : place + 128, :] = sum_reduce[:, place : place + 128].T * scale


def mlp_sums_kernel(
    devices, scale, mine, theirs,
    expand_out, attention_out, expand_shift, midnorm_gain, midnorm_shift, attention_shift, small, pack, sems,
):
    gather_pack(mine, theirs, pack, sems)
    unpack_tiles(pack, [expand_out, attention_out, small], devices, scale[...])
    width = small.shape[1]
    for part in range(expand_shift.shape[0] // width):
        expand_shift[part * width : part * width + width] = small[part, :]
    for row, target in ((4, midnorm_gain), (5, midnorm_shift), (6, attention_shift)):
        target[...] = small[row, :]


def in_sums_kernel(devices, scale, mine, theirs, in_out, prenorm_gain, prenorm_shift, small, pack, sems):
    gather_pack(mine, theirs, pack, sems)
    unpack_tiles(pack, [in_out, small], devices, scale[...])
    prenorm_gain[...] = small[0, :]
    prenorm_shift[...] = small[1, :]


def run_sums(kernel, scale, mine, theirs, chunk, outs, keep, devices, name):
    scales = [] if scale is None else [scale]
    return pl.pallas_call(
        lambda *refs: kernel(devices, *refs),
        out_shape=tuple(shape(*dims) for dims in outs),
        in_specs=[vmem_spec()] * len(scales) + [any_spec()] * 2,
        out_specs=[vmem_spec()] * len(outs),
        scratch_shapes=[pltpu.VMEM(dims, F32) for dims in keep]
        + [
            pltpu.VMEM((2,) + slots_shape(chunk, devices), F32),
            pltpu.SemaphoreType.DMA((2,)),
        ],
        compiler_params=pltpu.CompilerParams(vmem_limit_bytes=VMEM_BYTES),
        name=name,
    )(*scales, mine, theirs)


def shards(
    tokens, cloud_lengths, owner_slot, targets, prenorm_gain, prenorm_shift, attention_in,
    attention_out, attention_shift, midnorm_gain, midnorm_shift, expand_weight, expand_shift,
    reduce_weight, reduce_shift, lastnorm_gain, lastnorm_shift, head_weight, head_shift,
):
    token_count, width = tokens.shape
    hidden_width = expand_weight.shape[1]
    devices = lax.axis_size("dp")
    slot_count, width_out = targets.shape
    capacity = slot_count // devices
    arrived = lax.all_to_all(
        targets.reshape(devices, capacity, width_out), "dp", split_axis=0, concat_axis=0, tiled=True
    ).reshape(slot_count, width_out)
    weights = dict(
        prenorm_gain=prenorm_gain, prenorm_shift=prenorm_shift, attention_in=attention_in,
        attention_out=attention_out, attention_shift=attention_shift,
        midnorm_gain=midnorm_gain, midnorm_shift=midnorm_shift,
        expand_weight=expand_weight, expand_shift=expand_shift, reduce_weight=reduce_weight,
        reduce_shift=reduce_shift, lastnorm_gain=lastnorm_gain,
        lastnorm_shift=lastnorm_shift, head_turned=head_weight.T,
        head_shift=head_shift,
    )
    spaced_tokens, joint, attended, owners, used = run_attend(
        tokens, cloud_lengths, owner_slot[None], weights["prenorm_gain"], weights["prenorm_shift"], attention_in
    )
    middle, slope, grad_stream, predicted, block_keep, block_send = run_block(
        used, cloud_lengths, attended, spaced_tokens, owners, arrived, weights, devices
    )
    block_sum = DeviceSum(block_keep, block_send, devices)
    grad_middle, grad_attended, mlp_keep, mlp_send = beside(
        [block_sum], run_mlp_back(used, grad_stream, slope, middle, attended, weights, devices)
    )
    mlp_sum = DeviceSum(mlp_keep, mlp_send, devices)
    clouds = cloud_lengths.shape[0]
    grad_joint = beside(
        [block_sum, mlp_sum], run_attention_back(0, clouds // 2, cloud_lengths, joint, grad_attended)
    )
    grad_joint = beside(
        [block_sum, mlp_sum],
        run_attention_back(clouds // 2, clouds, cloud_lengths, joint, grad_attended, grad_joint),
    )
    in_keep, in_send = beside(
        [block_sum, mlp_sum], run_in_back(used, cloud_lengths, grad_joint, spaced_tokens, weights, devices)
    )
    in_sum = DeviceSum(in_keep, in_send, devices)
    sums = [in_sum, block_sum, mlp_sum]
    beside(sums, ())
    spaced_grad = beside(sums, run_input(used, grad_joint, spaced_tokens, grad_middle, weights))
    input_grad, predicted_turned = beside(
        sums, run_restore(cloud_lengths, spaced_grad, predicted, token_count)
    )
    beside(sums, ())
    run_out([block_sum])
    chunk = block_chunk(width, hidden_width, width_out)
    (
        grad_reduce, grad_head_turned, grad_last_gain, grad_last_shift, grad_reduce_shift, grad_head_shift,
        loss, rms, scale,
    ) = beside(
        [in_sum, mlp_sum],
        run_sums(
            lambda devices, *refs: block_sums_kernel(devices, width_out, *refs), None,
            block_sum.total, block_sum.theirs, chunk,
            [
                (hidden_width, width), chunk[1], (width,), (width,), (width,), (width_out,),
                (8, 128), (8, 128), (8, 128),
            ],
            [chunk[0], chunk[2]], devices, "block_sums",
        ),
    )
    chunk = mlp_chunk(width, hidden_width)
    beside([in_sum], ())
    run_out([mlp_sum])
    grad_expand, grad_out, grad_expand_shift, grad_mid_gain, grad_mid_shift, grad_out_shift = beside(
        [in_sum],
        run_sums(
            mlp_sums_kernel, scale, mlp_sum.total, mlp_sum.theirs, chunk,
            [chunk[0], chunk[1], (hidden_width,), (width,), (width,), (width,)], [chunk[2]], devices, "mlp_sums",
        ),
    )
    run_out([in_sum])
    chunk = in_chunk(width)
    grad_in, grad_pre_gain, grad_pre_shift = run_sums(
        in_sums_kernel, scale, in_sum.total, in_sum.theirs, chunk,
        [chunk[0], (width,), (width,)], [chunk[1]], devices, "in_sums",
    )
    return (
        loss[0, 0],
        predicted_turned.T,
        input_grad,
        grad_pre_gain,
        grad_pre_shift,
        grad_in,
        grad_out,
        grad_out_shift,
        grad_mid_gain,
        grad_mid_shift,
        grad_expand,
        grad_expand_shift,
        grad_reduce,
        grad_reduce_shift,
        grad_last_gain,
        grad_last_shift,
        grad_head_turned.T,
        grad_head_shift,
        rms[2:5, 0],
    )


def solution(mesh):
    row = P("dp", None)
    return jax.shard_map(
        shards,
        mesh=mesh,
        in_specs=(row, P("dp"), P("dp"), row) + (P(),) * 15,
        out_specs=(P(), row, row) + (P(),) * 16,
        check_vma=False,
    )
```

```python
import math

import jax
import jax.numpy as jnp
from jax import lax
from jax.experimental import pallas as pl
from jax.experimental.pallas import tpu as pltpu
from jax.sharding import PartitionSpec as P

HEADS = 6
CLOUD_MAX = 128
TILE = 256
GROUP = 2
BACK_GROUP = 1
EPSILON = 1e-05
F32 = jnp.float32
BF16 = jnp.bfloat16
VMEM_BYTES = 60 * 1024 * 1024


def split(values):
    high = values.astype(BF16)
    low = (values - high.astype(F32)).astype(BF16)
    return high, low


def dot(left, right, left_dim=1, right_dim=0):
    return lax.dot_general(
        left, right, (((left_dim,), (right_dim,)), ((), ())), preferred_element_type=F32
    )


def dot3(left, right, left_dim=1, right_dim=0):
    left_high, left_low = left
    right_high, right_low = right
    return dot(left_high, right_high, left_dim, right_dim) + (
        dot(left_high, right_low, left_dim, right_dim)
        + dot(left_low, right_high, left_dim, right_dim)
    )


def norm_parts(values):
    average = jnp.mean(values, axis=-1, keepdims=True)
    centred = values - average
    spread = jnp.mean(centred * centred, axis=-1, keepdims=True)
    inverse = lax.rsqrt(spread + EPSILON)
    return centred * inverse, inverse


def norm_back(grad_out, unit_rows, inverse, scale_gain):
    scaled = grad_out * scale_gain
    average_grad = jnp.mean(scaled, axis=-1, keepdims=True)
    project_grad = jnp.mean(scaled * unit_rows, axis=-1, keepdims=True)
    return inverse * (scaled - average_grad - unit_rows * project_grad)


def any_spec():
    return pl.BlockSpec(memory_space=pl.ANY)


def vmem_spec():
    return pl.BlockSpec(memory_space=pltpu.VMEM)


def smem_spec():
    return pl.BlockSpec(memory_space=pltpu.SMEM)


def cost(microseconds):
    return pl.CostEstimate(flops=microseconds * 10**9, bytes_accessed=microseconds * 10**6, transcendentals=0)


def shape(*dims):
    return jax.ShapeDtypeStruct(dims, F32)


def row_of(vector):
    return vector[...][None, :]


def column_sum(values):
    return jnp.sum(values, axis=0, keepdims=True)


def split_weight(source, high, low, step=128):
    rows = source.shape[0]

    def body(index, carry):
        place = pl.ds(pl.multiple_of(index * step, step), step)
        high[place, :], low[place, :] = split(source[place, :])
        return carry

    lax.fori_loop(0, rows // step, body, 0)


def spaced(length):
    return (length + 7) // 8 * 8


def aligned_rows(token_count, cloud_count):
    return (token_count + 8 * cloud_count + TILE - 1) // TILE * TILE


def masked_of(length):
    return 3 * length // 5


def compact_rows(token_count, cloud_count):
    return (masked_of(token_count) + 8 * cloud_count + TILE - 1) // TILE * TILE


def cloud_totals(lens):
    spread, masked = jnp.int32(0), jnp.int32(0)
    for cloud in range(lens.shape[0]):
        spread = spread + spaced(lens[cloud])
        masked = masked + spaced(masked_of(lens[cloud]))
    return spread, masked


def cloud_windows(lens, token_count):
    start, spaced_start, compact_start = jnp.int32(0), jnp.int32(0), jnp.int32(0)
    windows = []
    for cloud in range(lens.shape[0]):
        length = lens[cloud]
        base = jnp.minimum(start // 128, token_count // 128 - 2) * 128
        windows.append((start, pl.multiple_of(base, 128), start_of(spaced_start), start_of(compact_start)))
        start = start + length
        spaced_start = spaced_start + spaced(length)
        compact_start = compact_start + spaced(masked_of(length))
    return windows


def earlier_table():
    rows = lax.broadcasted_iota(jnp.int32, (2 * CLOUD_MAX, 2 * CLOUD_MAX), 0)
    columns = lax.broadcasted_iota(jnp.int32, (2 * CLOUD_MAX, 2 * CLOUD_MAX), 1)
    return (rows < columns).astype(F32).astype(BF16)


def cloud_places(slots, offset, length, earlier):
    lanes = lax.broadcasted_iota(jnp.int32, (1, 2 * CLOUD_MAX), 1)
    inside = jnp.logical_and(lanes >= offset, lanes < offset + length)
    masked = jnp.logical_and(inside, slots >= 0)
    flags = jnp.broadcast_to(masked.astype(F32), (8, 2 * CLOUD_MAX)).astype(BF16)
    rank = dot(flags, earlier)[:1].astype(jnp.int32)
    visible = masked_of(length) + lanes - offset - rank
    return jnp.where(masked, rank, jnp.where(inside, visible, -1))


def start_of(place):
    return pl.multiple_of(place, 8)


def gelu_parts(pre_act):
    cumulative = 0.5 * (1.0 + lax.erf(pre_act * (1.0 / math.sqrt(2.0))))
    density = jnp.exp(-0.5 * pre_act * pre_act) * (1.0 / math.sqrt(2.0 * math.pi))
    return pre_act * cumulative, cumulative + pre_act * density


def slot_place(relative, part, devices):
    x, y, rest = (relative >> 1) & 1, (relative >> 2) & 1, relative >> 3
    major, minor = (x, y) if part == 0 else (y, x)
    return relative & 1, major * (devices // 4) + minor * (devices // 8) + rest


def tile_list(shapes):
    return [
        (which, row, column)
        for which, (rows, columns) in enumerate(shapes)
        for row in range(0, rows, 8)
        for column in range(0, columns, 128)
    ]


def atom_tiles(shapes, devices):
    return -(-len(tile_list(shapes)) // (2 * devices))


def slots_shape(shapes, devices):
    return (2, devices // 2, atom_tiles(shapes, devices) * 8, 128)


def pack_tiles(sources, pack, devices):
    me = lax.axis_index("dp")
    tiles = tile_list([source.shape for source in sources])
    each = atom_tiles([source.shape for source in sources], devices)
    for atom in range(-(-len(tiles) // each)):
        part, owner = atom // devices, atom % devices
        bit, place = slot_place(me ^ owner, part, devices)
        for number, (which, row, column) in enumerate(tiles[atom * each : atom * each + each]):
            pack[bit, part, place, number * 8 : number * 8 + 8, :] = sources[which][
                row : row + 8, column : column + 128
            ]


def unpack_tiles(pack, targets, devices, scale):
    me = lax.axis_index("dp")
    tiles = tile_list([target.shape for target in targets])
    each = atom_tiles([target.shape for target in targets], devices)
    for atom in range(-(-len(tiles) // each)):
        part, owner = atom // devices, atom % devices
        bit, place = slot_place(me ^ owner, part, devices)
        for number, (which, row, column) in enumerate(tiles[atom * each : atom * each + each]):
            piece = pack[bit, part, place, number * 8 : number * 8 + 8, :]
            targets[which][row : row + 8, column : column + 128] = (
                piece if scale is None else piece * scale
            )


def swap(values, bits, devices):
    return lax.ppermute(values, "dp", [(device, device ^ bits) for device in range(devices)])


def rest_groups(devices):
    count = (devices // 8).bit_length() - 1
    groups = []
    while count:
        step = 2 if count >= 2 else 1
        count -= step
        groups.append((3 + count, 1 << step))
    return groups


class DeviceSum:
    def __init__(self, keep, send, devices):
        self.devices = devices
        self.groups = rest_groups(devices)
        self.keep, self.send = keep, send
        self.stage = 0
        self.last = 5 + 2 * len(self.groups)

    def start(self):
        devices, stage, count = self.devices, self.stage, len(self.groups)
        if stage == 0:
            self.moving = [swap(self.send, 1, devices)]
        elif stage <= 2:
            size = devices // (4, 8)[stage - 1]
            bits = ((2, 4), (4, 2))[stage - 1]
            self.moving = [swap(half[size:], bit, devices) for half, bit in zip(self.halves, bits)]
            self.halves = [half[:size] for half in self.halves]
        elif stage < 3 + count:
            shift, size = self.groups[stage - 3]
            total = self.total.reshape((size, -1) + self.total.shape[1:])
            self.moving = [swap(total[slot], slot << shift, devices) for slot in range(1, size)]
            self.total = total[0]
        elif stage < 3 + 2 * count:
            shift, size = self.groups[3 + 2 * count - 1 - stage]
            self.moving = [swap(self.total, slot << shift, devices) for slot in range(1, size)]
        elif stage < 5 + 2 * count:
            bits = ((4, 2), (2, 4))[stage - 3 - 2 * count]
            self.moving = [swap(half, bit, devices) for half, bit in zip(self.halves, bits)]
        else:
            self.moving = [swap(self.total, 1, devices)]

    def finish(self):
        stage, count = self.stage, len(self.groups)
        if stage == 0:
            total = self.keep + self.moving[0]
            self.halves = [total[0], total[1]]
        elif stage <= 2:
            self.halves = [half + moved for half, moved in zip(self.halves, self.moving)]
            if stage == 2:
                self.total = jnp.stack(self.halves, axis=1)
        elif stage < 3 + count:
            self.total = sum(self.moving, self.total)
        elif stage < 3 + 2 * count:
            self.total = jnp.concatenate([self.total] + self.moving, axis=0)
            if stage == 2 + 2 * count:
                self.halves = [self.total[:, 0], self.total[:, 1]]
        elif stage < 5 + 2 * count:
            self.halves = [jnp.concatenate([half, moved]) for half, moved in zip(self.halves, self.moving)]
            if stage == 4 + 2 * count:
                self.total = jnp.stack(self.halves)
        else:
            self.theirs = self.moving[0]
        self.stage += 1

    def done(self):
        return self.stage > self.last

    def state(self):
        if hasattr(self, "total") and (3 <= self.stage < 3 + 2 * len(self.groups) or self.stage >= self.last):
            return self.total
        return self.halves

    def set_state(self, state):
        if hasattr(self, "total") and (3 <= self.stage < 3 + 2 * len(self.groups) or self.stage >= self.last):
            self.total = state
        else:
            self.halves = state


def beside(sums, outs):
    sums = [one for one in sums if not one.done()]
    for one in sums:
        one.start()
    moving, outs = lax.optimization_barrier(([one.moving for one in sums], outs))
    for one, moved in zip(sums, moving):
        one.moving = moved
        one.finish()
    going = [one for one in sums if not one.done()]
    states, outs = lax.optimization_barrier(([one.state() for one in going], outs))
    for one, state in zip(going, states):
        one.set_state(state)
    return outs


def run_stage(one):
    one.start()
    one.finish()


def run_out(sums):
    while not all(one.done() for one in sums):
        for one in sums:
            if not one.done():
                run_stage(one)


def attend_kernel(
    lens, tokens_hbm, owner, prenorm_gain, prenorm_shift, attention_in,
    tokens_out, joint_out, attended_out, owners, valid, used_out, groups_out,
    raw, tokens, joint, attended, in_high, in_low, token_sem, joint_sem, out_sems,
):
    token_count = owner.shape[1]
    tiles = tokens.shape[0] // TILE
    width = tokens.shape[1]
    spread, compact = cloud_totals(lens)
    used = (spread + TILE - 1) // TILE
    used_out[0] = used
    used_out[1] = (compact + TILE - 1) // TILE

    def tile_rows(index):
        return pl.ds(pl.multiple_of(index * TILE, TILE), TILE)

    token_copy = pltpu.make_async_copy(tokens_hbm, raw, token_sem)
    token_copy.start()
    split_weight(attention_in, in_high, in_low)
    owners[...] = jnp.full(owners.shape, -1, jnp.int32)
    valid[...] = jnp.zeros(valid.shape, F32)
    tokens[tile_rows(used - 1), :] = jnp.zeros((TILE, width), F32)

    def no_group(index, carry):
        groups_out[index] = -1
        return carry

    lax.fori_loop(0, groups_out.shape[0], no_group, 0, unroll=8)

    def cloud_groups(cloud, carry):
        spaced_group, compact_group = carry
        count = spaced(masked_of(lens[cloud])) // 8

        def group(index, carry):
            groups_out[spaced_group + index] = compact_group + index
            return carry

        lax.fori_loop(0, count, group, 0)
        return spaced_group + spaced(lens[cloud]) // 8, compact_group + count

    lax.fori_loop(0, lens.shape[0], cloud_groups, (jnp.int32(0), jnp.int32(0)))
    windows = cloud_windows(lens, token_count)
    earlier = earlier_table()
    wide = lax.broadcasted_iota(jnp.int32, (1, 2 * CLOUD_MAX), 1)
    order = lax.broadcasted_iota(jnp.int32, (CLOUD_MAX, 2 * CLOUD_MAX), 0)
    token_copy.wait()
    for first in range(0, lens.shape[0], 4):
        clouds = range(first, min(first + 4, lens.shape[0]))
        slots = [owner[:, pl.ds(windows[cloud][1], 2 * CLOUD_MAX)] for cloud in clouds]
        places = [
            cloud_places(slot, windows[cloud][0] - windows[cloud][1], lens[cloud], earlier)
            for slot, cloud in zip(slots, clouds)
        ]
        picks = [(order == place).astype(F32).astype(BF16) for place in places]
        for pick, slot, cloud in zip(picks, slots, clouds):
            _, base, spaced_start, compact_start = windows[cloud]
            rows = raw[pl.ds(base, 2 * CLOUD_MAX), :]
            high = rows.astype(BF16)
            rest = rows - high.astype(F32)
            mid, low = split(rest)
            tokens[pl.ds(spaced_start, CLOUD_MAX), :] = (dot(pick, high) + dot(pick, mid)) + dot(pick, low)
            parts = jnp.concatenate(
                [(slot >> 6).astype(F32), (slot & 63).astype(F32), jnp.zeros((6, 2 * CLOUD_MAX), F32)], axis=0
            )
            parts = dot(parts.astype(BF16), pick, 1, 1)
            moved = (parts[0:1] * 64.0 + parts[1:2]).astype(jnp.int32)
            moved = jnp.concatenate([moved, jnp.zeros((1, CLOUD_MAX), jnp.int32)], axis=1)
            length, masked = lens[cloud], masked_of(lens[cloud])
            offset = compact_start % 128
            lanes = pl.ds(pl.multiple_of(compact_start // 128 * 128, 128), 2 * CLOUD_MAX)
            inside = jnp.logical_and(wide >= offset, wide < offset + masked)
            owners[:, lanes] = jnp.where(inside, pltpu.roll(moved, offset, 1), owners[:, lanes])
            offset = spaced_start % 128
            lanes = pl.ds(pl.multiple_of(spaced_start // 128 * 128, 128), 2 * CLOUD_MAX)
            inside = jnp.logical_and(wide >= offset, wide < offset + length)
            valid[:, lanes] = jnp.where(inside, 1.0, valid[:, lanes])

    def joint_copies(index):
        rows = tile_rows(index)
        return [
            pltpu.make_async_copy(joint.at[rows], joint_out.at[rows], joint_sem.at[index]),
            pltpu.make_async_copy(tokens.at[rows], tokens_out.at[rows], out_sems.at[0, index]),
        ]

    def joint_tile(index, carry):
        rows = tile_rows(index)
        unit, _ = norm_parts(tokens[rows, :])
        normed = split(unit * row_of(prenorm_gain) + row_of(prenorm_shift))
        joint[rows, :] = dot3(normed, (in_high[...], in_low[...]))
        for copy in joint_copies(index):
            copy.start()
        return carry

    lax.fori_loop(0, used, joint_tile, 0)
    tail = pl.ds(pl.multiple_of(used * TILE, TILE), CLOUD_MAX)
    joint[tail, :] = jnp.zeros((CLOUD_MAX, joint.shape[1]), F32)
    tail_copy = pltpu.make_async_copy(joint.at[tail], joint_out.at[tail], joint_sem.at[tiles])
    tail_copy.start()
    attended[tile_rows(used - 1), :] = jnp.zeros((TILE, width), F32)

    lane = lax.broadcasted_iota(jnp.int32, (CLOUD_MAX, 128), 1)
    first_head = lane < 64
    wide_lane = lax.broadcasted_iota(jnp.int32, (2 * CLOUD_MAX, CLOUD_MAX), 1)
    empty = jnp.zeros((CLOUD_MAX, 128), BF16)

    def clouds(index, start):
        lengths = [lens[GROUP * index + number] for number in range(GROUP)]
        places = []
        for length in lengths:
            places.append(pl.ds(start_of(start), CLOUD_MAX))
            start = start + spaced(length)
        insides = [wide_lane < length for length in lengths]
        work = [(number, pair) for number in range(GROUP) for pair in range(HEADS // 2)]
        lefts, rights = [], []
        for number, pair in work:
            rows = places[number]
            query = joint[rows, pair * 128 : pair * 128 + 128] * 0.125
            key_high, key_low = split(joint[rows, width + pair * 128 : width + pair * 128 + 128])
            both = jnp.concatenate(
                [jnp.where(first_head, query, 0.0), jnp.where(first_head, 0.0, query)], axis=0
            )
            lefts.append(jnp.concatenate(split(both), axis=1))
            rights.append(
                jnp.concatenate(
                    [
                        jnp.concatenate([key_high, key_high], axis=1),
                        jnp.concatenate([key_low, empty], axis=1),
                    ],
                    axis=0,
                )
            )
        scores = [dot(left, right, 1, 1) for left, right in zip(lefts, rights)]
        scores = [
            jnp.where(insides[number], score[:, :128] + score[:, 128:], -1e30)
            for (number, _), score in zip(work, scores)
        ]
        peaks = [jnp.max(score, axis=-1, keepdims=True) for score in scores]
        weights = [jnp.exp(score - peak) for score, peak in zip(scores, peaks)]
        scales = [1.0 / jnp.sum(weight, axis=-1, keepdims=True) for weight in weights]
        lefts = [jnp.concatenate(split(weight * scale), axis=1) for weight, scale in zip(weights, scales)]
        rights = []
        for number, pair in work:
            value_high, value_low = split(
                joint[places[number], 2 * width + pair * 128 : 2 * width + pair * 128 + 128]
            )
            rights.append(
                jnp.concatenate(
                    [
                        jnp.concatenate([value_high, value_low], axis=1),
                        jnp.concatenate([value_high, empty], axis=1),
                    ],
                    axis=0,
                )
            )
        mixed = [dot(left, right) for left, right in zip(lefts, rights)]
        for (number, pair), both in zip(work, mixed):
            both = both[:, :128] + both[:, 128:]
            attended[places[number], pair * 128 : pair * 128 + 128] = jnp.where(
                first_head, both[:CLOUD_MAX], both[CLOUD_MAX:]
            )
        return start

    lax.fori_loop(0, lens.shape[0] // GROUP, clouds, jnp.int32(0))

    def attended_copy(index):
        rows = tile_rows(index)
        return pltpu.make_async_copy(attended.at[rows], attended_out.at[rows], out_sems.at[1, index])

    def begin(index, carry):
        attended_copy(index).start()
        return carry

    def finish(index, carry):
        attended_copy(index).wait()
        for copy in joint_copies(index):
            copy.wait()
        return carry

    lax.fori_loop(0, used, begin, 0)
    tail_copy.wait()
    lax.fori_loop(0, used, finish, 0)


def run_attend(tokens, lens, owner, prenorm_gain, prenorm_shift, attention_in):
    token_count, width = tokens.shape
    joint_width = attention_in.shape[1]
    spaced_count = aligned_rows(token_count, lens.shape[0])
    tiles = spaced_count // TILE
    return pl.pallas_call(
        attend_kernel,
        out_shape=(
            shape(spaced_count, width),
            shape(spaced_count + CLOUD_MAX, joint_width),
            shape(spaced_count, width),
            jax.ShapeDtypeStruct((1, compact_rows(token_count, lens.shape[0]) + 256), jnp.int32),
            shape(1, spaced_count + 256),
            jax.ShapeDtypeStruct((2,), jnp.int32),
            jax.ShapeDtypeStruct((spaced_count // 8,), jnp.int32),
        ),
        in_specs=[smem_spec(), any_spec()] + [vmem_spec()] * 4,
        out_specs=[any_spec()] * 3 + [vmem_spec()] * 2 + [smem_spec()] * 2,
        scratch_shapes=[
            pltpu.VMEM((token_count, width), F32),
            pltpu.VMEM((spaced_count, width), F32),
            pltpu.VMEM((spaced_count + CLOUD_MAX, joint_width), F32),
            pltpu.VMEM((spaced_count + CLOUD_MAX, width), F32),
            pltpu.VMEM(attention_in.shape, BF16),
            pltpu.VMEM(attention_in.shape, BF16),
            pltpu.SemaphoreType.DMA,
            pltpu.SemaphoreType.DMA((tiles + 1,)),
            pltpu.SemaphoreType.DMA((2, tiles)),
        ],
        compiler_params=pltpu.CompilerParams(vmem_limit_bytes=VMEM_BYTES),
        cost_estimate=cost(30),
        name="attend",
    )(lens, tokens, owner, prenorm_gain, prenorm_shift, attention_in)


def block_kernel(
    devices, used_ref, groups, attended, tokens, valid, owners, targets, attention_out,
    attention_shift, midnorm_gain, midnorm_shift, expand_weight, expand_shift, reduce_weight,
    reduce_shift, lastnorm_gain, lastnorm_shift, head_turned, head_shift,
    predicted, grad_middle_out, grad_attended_out, keep_out, send_out,
    sum_reduce, sum_expand, sum_out, sum_head, small, pack,
    middle, attended_kept, slope, hidden, stream, blank,
    hidden_tile, slope_tile, middle_tile, stream_tile,
    out_high, out_low, expand_high, expand_low, reduce_high, reduce_low,
    head_high, head_low, turned_high, turned_low, target_parts, pred_rows, true_rows, distance, second,
    col_low, col_sum, shift_column, pack_sem, out_sems, weight_sems, blank_sem,
):
    index = pl.program_id(0)
    used, compact_used = used_ref[0], used_ref[1]
    slot_count, width_out = targets.shape
    points = width_out // 3
    width = middle.shape[1]
    spare = middle.shape[0] // 8 - 1
    copies = [
        pltpu.make_async_copy(pack.at[0], keep_out, pack_sem.at[0]),
        pltpu.make_async_copy(pack.at[1], send_out, pack_sem.at[1]),
    ]

    def tile_rows(index):
        return pl.ds(pl.multiple_of(index * TILE, TILE), TILE)

    def out_copies(index):
        rows = tile_rows(index)
        return [
            pltpu.make_async_copy(middle.at[rows], grad_middle_out.at[rows], out_sems.at[0, index]),
            pltpu.make_async_copy(attended_kept.at[rows], grad_attended_out.at[rows], out_sems.at[1, index]),
        ]

    blank_copy = pltpu.make_async_copy(
        blank,
        grad_attended_out.at[pl.ds(pl.multiple_of(compact_used * TILE, TILE), CLOUD_MAX)],
        blank_sem,
    )

    @pl.when(index == 0)
    def _():
        staged = [
            (attention_out, middle.at[pl.ds(0, attention_out.shape[0])], out_high, out_low),
            (expand_weight, slope.at[pl.ds(0, expand_weight.shape[0])], expand_high, expand_low),
            (reduce_weight, stream.at[pl.ds(0, reduce_weight.shape[0])], reduce_high, reduce_low),
        ]
        copies = [
            pltpu.make_async_copy(weight, place, weight_sems.at[number])
            for number, (weight, place, _, _) in enumerate(staged)
        ]
        for copy in copies:
            copy.start()
        shift_column[...] = jnp.broadcast_to(row_of(head_shift), (8, width_out)).T[:, :1]
        turned_high[...], turned_low[...] = split(head_turned[...])
        head_high[...], head_low[...] = split(head_turned[...].T)
        high, low = split(targets[...].T)
        target_parts[:width_out, :] = high
        target_parts[width_out:, :] = low
        for total in (small, sum_reduce, sum_head, sum_expand, sum_out, blank):
            total[...] = jnp.zeros_like(total)
        for copy, (_, place, high_part, low_part) in zip(copies, staged):
            copy.wait()
            split_weight(place, high_part, low_part)
        for kept in (middle, attended_kept, slope, hidden, stream):
            kept[tile_rows(compact_used - 1), :] = jnp.zeros((TILE, kept.shape[1]), F32)
        blank_copy.start()

    def chamfer_half(half):
        xs = [pred_rows[half, pl.ds(c, points, stride=3), :] for c in range(3)]

        def first(j, row_low):
            gap = [xs[c] - true_rows[half, pl.ds(3 * j + c, 1), :] for c in range(3)]
            apart = gap[0] * gap[0] + gap[1] * gap[1] + gap[2] * gap[2]
            distance[j] = apart
            lowest = jnp.min(apart, axis=0, keepdims=True)
            weight = jnp.exp(lowest - apart)
            inside = column_sum(weight)
            col_low[pl.ds(j, 1), :] = lowest
            col_sum[pl.ds(j, 1), :] = inside
            second[j] = weight * (1.0 / (points * inside))
            return jnp.minimum(row_low, apart)

        row_low = lax.fori_loop(
            0, points, first, jnp.full((points, 128), jnp.inf, F32), unroll=8
        )

        def middle_pass(j, row_sum):
            weight = jnp.exp(row_low - distance[j])
            distance[j] = weight
            return row_sum + weight

        row_sum = lax.fori_loop(0, points, middle_pass, jnp.zeros((points, 128), F32), unroll=8)
        row_scale = 1.0 / (points * row_sum)

        def last(j, carry):
            weight = second[j] + distance[j] * row_scale
            return (carry[0] + weight,) + tuple(
                carry[1 + c] + weight * true_rows[half, pl.ds(3 * j + c, 1), :] for c in range(3)
            )

        zero = jnp.zeros((points, 128), F32)
        sums = lax.fori_loop(0, points, last, (zero,) * 4, unroll=8)
        terms = column_sum(row_low - jnp.log(row_sum * (1.0 / points))) + column_sum(
            col_low[...] - jnp.log(col_sum[...] * (1.0 / points))
        )
        grads = [2.0 * (sums[0] * xs[c] - sums[1 + c]) for c in range(3)]
        return terms * (1.0 / points), grads

    def back_tile(index, carry):
        rows = tile_rows(index)
        slots = lax.broadcasted_iota(jnp.int32, (slot_count, TILE), 0)
        slot_row = owners[:, rows]
        unit, inverse = norm_parts(stream[rows, :])
        normed = split(unit * row_of(lastnorm_gain) + row_of(lastnorm_shift))
        pred = dot3((turned_high[...], turned_low[...]), normed, 1, 1) + shift_column[...]
        for half in range(TILE // 128):
            pred_rows[half] = pred[:, half * 128 : half * 128 + 128]
        chosen = (slots == slot_row).astype(F32).astype(BF16)
        true_points = dot(target_parts[...], chosen)
        true_points = true_points[:width_out] + true_points[width_out:]
        for half in range(TILE // 128):
            true_rows[half] = true_points[:, half * 128 : half * 128 + 128]
        masked = slot_row >= 0
        losses = []
        for half in range(TILE // 128):
            terms, grads = chamfer_half(half)
            losses.append(terms)
            for c in range(3):
                pred_rows[half, pl.ds(c, points, stride=3), :] = grads[c]
        grad_turned = jnp.concatenate([pred_rows[half] for half in range(TILE // 128)], axis=1)
        grad_turned = jnp.where(masked, grad_turned, 0.0)
        loss = jnp.where(masked, jnp.concatenate(losses, axis=1), 0.0)
        grad_pred = grad_turned.T
        sum_head[...] += dot3(split(grad_turned), normed)
        grad_last = dot3(split(grad_pred), (head_high[...], head_low[...]), 1, 1)
        grad_str = norm_back(grad_last, unit, inverse, row_of(lastnorm_gain))
        sum_reduce[...] += dot3(split(grad_str.T), split(hidden[rows, :]))
        small[0:1, :TILE] += loss
        small[1:2, :TILE] += masked.astype(F32)
        small[5:6, :] += column_sum(grad_last * unit)
        small[6:7, :] += column_sum(grad_last)
        small[7:8, :] += column_sum(grad_str)
        small[8:9, :width_out] += column_sum(grad_pred)
        unit, inverse = norm_parts(middle[rows, :])
        normed = unit * row_of(midnorm_gain) + row_of(midnorm_shift)
        grad_pre = dot3(split(grad_str), (reduce_high[...], reduce_low[...]), 1, 1) * slope[rows, :]
        parts = split(grad_pre)
        sum_expand[...] += dot3(split(normed.T), parts)
        grad_normed = dot3(parts, (expand_high[...], expand_low[...]), 1, 1)
        grad_mid = grad_str + norm_back(grad_normed, unit, inverse, row_of(midnorm_gain))
        shift_sum = column_sum(grad_pre)
        for part in range(shift_sum.shape[1] // width):
            small[16 + part : 17 + part, :] += shift_sum[:, part * width : part * width + width]
        small[20:21, :] += column_sum(grad_normed * unit)
        small[21:22, :] += column_sum(grad_normed)
        small[22:23, :] += column_sum(grad_mid)
        parts = split(grad_mid)
        sum_out[...] += dot3(split(attended_kept[rows, :].T), parts)
        middle[rows, :] = grad_mid
        attended_kept[rows, :] = dot3(parts, (out_high[...], out_low[...]), 1, 1)
        for copy in out_copies(index):
            copy.start()
        return carry

    @pl.when(index < used)
    def _():
        valid_row = jnp.broadcast_to(valid[...], (8, TILE)).T[:, :1] > 0.5
        mixed = dot3(split(attended[...]), (out_high[...], out_low[...])) + row_of(attention_shift)
        mid = tokens[...] + mixed
        unit, _ = norm_parts(mid)
        normed = split(unit * row_of(midnorm_gain) + row_of(midnorm_shift))
        pre_act = dot3(normed, (expand_high[...], expand_low[...])) + row_of(expand_shift)
        active, steep = gelu_parts(pre_act)
        hidden_tile[...] = active
        slope_tile[...] = steep
        branch = dot3(split(active), (reduce_high[...], reduce_low[...])) + row_of(reduce_shift)
        after = mid + branch
        unit, _ = norm_parts(after)
        normed = split(unit * row_of(lastnorm_gain) + row_of(lastnorm_shift))
        predicted[...] = dot3(normed, (head_high[...], head_low[...])) + row_of(head_shift)
        small[2:3, :] += column_sum(jnp.where(valid_row, after * after, 0.0))
        small[3:4, :] += column_sum(jnp.where(valid_row, mixed * mixed, 0.0))
        small[4:5, :] += column_sum(jnp.where(valid_row, branch * branch, 0.0))
        small[9:10, :TILE] += valid[...]
        middle_tile[...] = mid
        stream_tile[...] = after

        pairs = (
            (hidden_tile, hidden), (slope_tile, slope), (middle_tile, middle), (stream_tile, stream),
            (attended, attended_kept),
        )

        def keep_group(group, carry):
            target = groups[index * (TILE // 8) + group]
            target = jnp.where(target >= 0, target, spare)
            rows = pl.ds(start_of(target * 8), 8)
            values = [source[pl.ds(start_of(group * 8), 8), :] for source, _ in pairs]
            for (_, kept), value in zip(pairs, values):
                kept[rows, :] = value
            return carry

        lax.fori_loop(0, TILE // 8, keep_group, 0, unroll=4)

    @pl.when(index == pl.num_programs(0) - 1)
    def _():
        lax.fori_loop(0, compact_used, back_tile, 0)
        pack_tiles([sum_reduce, sum_expand, sum_out, sum_head, small], pack, devices)
        for copy in copies:
            copy.start()
        blank_copy.wait()

        def finish(index, carry):
            for copy in out_copies(index):
                copy.wait()
            return carry

        lax.fori_loop(0, compact_used, finish, 0)
        for copy in copies:
            copy.wait()


def row_map(index, used):
    return (jnp.minimum(index, used[0] - 1), 0)


def rows_spec(columns):
    return pl.BlockSpec((TILE, columns), row_map)


def whole_spec(array):
    return pl.BlockSpec(array.shape, lambda index, used: (0,) * len(array.shape))


def run_block(used, groups, attended, tokens, valid, owners, targets, weights, devices):
    spaced_count, width = tokens.shape
    compact_count = owners.shape[1] - 256
    hidden_width = weights["expand_weight"].shape[1]
    slot_count, width_out = targets.shape
    points = width_out // 3
    names = (
        "attention_out", "attention_shift",
        "midnorm_gain", "midnorm_shift", "expand_weight", "expand_shift", "reduce_weight",
        "reduce_shift", "lastnorm_gain", "lastnorm_shift", "head_turned", "head_shift",
    )
    extra = [owners, targets] + [weights[name] for name in names]
    staged = ("attention_out", "expand_weight", "reduce_weight")
    extra_specs = [whole_spec(array) for array in extra[:2]] + [
        any_spec() if name in staged else whole_spec(weights[name]) for name in names
    ]
    pairs = []
    for name in ("attention_out", "expand_weight", "reduce_weight"):
        pairs += [pltpu.VMEM(weights[name].shape, BF16)] * 2
    pairs += [pltpu.VMEM((width, width_out), BF16)] * 2 + [pltpu.VMEM((width_out, width), BF16)] * 2
    chunk = block_chunk(width, hidden_width, width_out)
    slots = slots_shape(chunk, devices)
    return pl.pallas_call(
        lambda *refs: block_kernel(devices, *refs),
        out_shape=(
            shape(spaced_count, width_out),
            shape(compact_count, width),
            shape(compact_count + CLOUD_MAX, width),
            shape(*slots),
            shape(*slots),
        ),
        grid_spec=pltpu.PrefetchScalarGridSpec(
            num_scalar_prefetch=1,
            grid=(spaced_count // TILE,),
            in_specs=[
                smem_spec(),
                rows_spec(width),
                rows_spec(width),
                pl.BlockSpec((1, TILE), lambda index, used: (0, jnp.minimum(index, used[0] - 1))),
            ]
            + extra_specs,
            out_specs=[rows_spec(width_out)] + [any_spec()] * 4,
            scratch_shapes=[pltpu.VMEM(dims, F32) for dims in chunk]
            + [pltpu.VMEM((2,) + slots, F32)]
            + [
                pltpu.VMEM((compact_count + 8, columns), F32)
                for columns in (width, width, hidden_width, hidden_width, width)
            ]
            + [pltpu.VMEM((CLOUD_MAX, width), F32)]
            + [pltpu.VMEM((TILE, columns), F32) for columns in (hidden_width, hidden_width, width, width)]
            + pairs
            + [
                pltpu.VMEM((2 * width_out, slot_count), BF16),
                pltpu.VMEM((TILE // 128, width_out, 128), F32),
                pltpu.VMEM((TILE // 128, width_out, 128), F32),
                pltpu.VMEM((points, points, 128), F32),
                pltpu.VMEM((points, points, 128), F32),
                pltpu.VMEM((points, 128), F32),
                pltpu.VMEM((points, 128), F32),
                pltpu.VMEM((width_out, 1), F32),
                pltpu.SemaphoreType.DMA((2,)),
                pltpu.SemaphoreType.DMA((2, compact_count // TILE)),
                pltpu.SemaphoreType.DMA((3,)),
                pltpu.SemaphoreType.DMA,
            ],
        ),
        compiler_params=pltpu.CompilerParams(vmem_limit_bytes=VMEM_BYTES),
        cost_estimate=cost(55),
        name="block",
    )(used, groups, attended, tokens, valid, *extra)


def block_chunk(width, hidden_width, width_out):
    return [(width, hidden_width), (width, hidden_width), (width, width), (width_out, width), (24, width)]


def in_chunk(width):
    return [(width, 3 * width), (8, width)]


def attention_back_kernel(
    lens, joint_hbm, grad_hbm, joint_grad_out, joint, grad_rows, joint_grad, in_sems, out_sem,
):
    width = grad_rows.shape[2]
    lane = lax.broadcasted_iota(jnp.int32, (CLOUD_MAX, 128), 1)
    first_head = lane < 64
    key_place = lax.broadcasted_iota(jnp.int32, (CLOUD_MAX, 2 * CLOUD_MAX), 0)
    query_place = lax.broadcasted_iota(jnp.int32, (CLOUD_MAX, 2 * CLOUD_MAX), 1) % CLOUD_MAX
    empty = jnp.zeros((CLOUD_MAX, 128), BF16)

    def both_heads(values):
        return jnp.concatenate(
            [jnp.where(first_head, values, 0.0), jnp.where(first_head, 0.0, values)], axis=0
        )

    def fetch(starts, half):
        copies = []
        for number, (start, masked_start) in enumerate(starts):
            rows = pl.ds(start_of(start), CLOUD_MAX)
            masked_rows = pl.ds(start_of(masked_start), CLOUD_MAX)
            slot = half * BACK_GROUP + number
            copies += [
                pltpu.make_async_copy(joint_hbm.at[rows], joint.at[slot], in_sems.at[0, slot]),
                pltpu.make_async_copy(grad_hbm.at[masked_rows], grad_rows.at[slot], in_sems.at[1, slot]),
            ]
        return copies

    def store(start, slot):
        rows = pl.ds(start_of(start), CLOUD_MAX)
        return pltpu.make_async_copy(joint_grad.at[slot], joint_grad_out.at[rows], out_sem)

    def starts_of(index, start, masked_start):
        starts = []
        for number in range(BACK_GROUP):
            starts.append((start, masked_start))
            length = lens[jnp.minimum(index * BACK_GROUP + number, lens.shape[0] - 1)]
            start = start + spaced(length)
            masked_start = masked_start + spaced(masked_of(length))
        return starts, start, masked_start

    groups = lens.shape[0] // BACK_GROUP
    starts, _, _ = starts_of(0, jnp.int32(0), jnp.int32(0))
    for copy in fetch(starts, 0):
        copy.start()
    work = [(number, pair) for number in range(BACK_GROUP) for pair in range(HEADS // 2)]

    def clouds(index, carry):
        before, start, masked_start = carry
        half = lax.rem(index, 2)
        starts, following, masked_following = starts_of(index, start, masked_start)

        @pl.when(index + 1 < groups)
        def _():
            after, _, _ = starts_of(index + 1, following, masked_following)
            for copy in fetch(after, 1 - half):
                copy.start()

        @pl.when(index > 0)
        def _():
            for number in range(1, BACK_GROUP):
                store(before[number - 1], (1 - half) * BACK_GROUP + number - 1).wait()
                store(before[number], (1 - half) * BACK_GROUP + number).start()

        for copy in fetch(starts, half):
            copy.wait()
        lengths = [lens[index * BACK_GROUP + number] for number in range(BACK_GROUP)]
        insides = [key_place < length for length in lengths]
        lives = [
            jnp.logical_and(inside, query_place < masked_of(length)) for inside, length in zip(insides, lengths)
        ]
        slots = [half * BACK_GROUP + number for number, _ in work]
        at = [
            [slice(part * width + pair * 128, part * width + pair * 128 + 128) for part in range(3)]
            for _, pair in work
        ]
        each = range(len(work))
        query = [split(both_heads(joint[slots[one], :, at[one][0]] * 0.125)) for one in each]
        key = [split(joint[slots[one], :, at[one][1]]) for one in each]
        value = [split(joint[slots[one], :, at[one][2]]) for one in each]
        grad = [split(both_heads(grad_rows[slots[one], :, at[one][0]])) for one in each]
        scores = [dot3(key[one], query[one], 1, 1) for one in each]
        grad_probs = [dot3(value[one], grad[one], 1, 1) for one in each]
        scores = [jnp.where(insides[number], score, -1e30) for (number, _), score in zip(work, scores)]
        peaks = [jnp.max(score, axis=0, keepdims=True) for score in scores]
        weights = [jnp.exp(score - peak) for score, peak in zip(scores, peaks)]
        scales = [1.0 / column_sum(weight) for weight in weights]
        probs = [
            jnp.where(lives[number], weight * scale, 0.0)
            for (number, _), weight, scale in zip(work, weights, scales)
        ]
        shared = [column_sum(prob * grad_prob) for prob, grad_prob in zip(probs, grad_probs)]
        grad_scores = [probs[one] * (grad_probs[one] - shared[one]) for one in each]
        turned = [grad_score.T for grad_score in grad_scores]
        for one in each:
            joint_grad[slots[one], :, at[one][2]] = dot3(split(probs[one]), grad[one])
        for one in each:
            joint_grad[slots[one], :, at[one][1]] = dot3(split(grad_scores[one]), query[one])
        for one in each:
            left = jnp.concatenate(split(turned[one]), axis=1)
            right = jnp.concatenate(
                [
                    jnp.concatenate([key[one][0], key[one][1]], axis=1),
                    jnp.concatenate([key[one][0], empty], axis=1),
                ],
                axis=0,
            )
            grad_query = dot(left, right)
            grad_query = (grad_query[:, :128] + grad_query[:, 128:]) * 0.125
            joint_grad[slots[one], :, at[one][0]] = jnp.where(
                first_head, grad_query[:CLOUD_MAX], grad_query[CLOUD_MAX:]
            )

        @pl.when(index > 0)
        def _():
            store(before[BACK_GROUP - 1], (1 - half) * BACK_GROUP + BACK_GROUP - 1).wait()

        store(starts[0][0], half * BACK_GROUP).start()
        return tuple(start for start, _ in starts), following, masked_following

    zero = jnp.int32(0)
    before, _, _ = lax.fori_loop(0, groups, clouds, ((zero,) * BACK_GROUP, zero, zero))
    half = (groups - 1) % 2
    for number in range(BACK_GROUP):
        store(before[number], half * BACK_GROUP + number).wait()
        if number + 1 < BACK_GROUP:
            store(before[number + 1], half * BACK_GROUP + number + 1).start()


def run_attention_back(lens, joint, grad_attended):
    width = grad_attended.shape[1]
    joint_width = joint.shape[1]
    return pl.pallas_call(
        attention_back_kernel,
        out_shape=shape(*joint.shape),
        in_specs=[smem_spec()] + [any_spec()] * 2,
        out_specs=any_spec(),
        scratch_shapes=[
            pltpu.VMEM((2 * BACK_GROUP, CLOUD_MAX, joint_width), F32),
            pltpu.VMEM((2 * BACK_GROUP, CLOUD_MAX, width), F32),
            pltpu.VMEM((2 * BACK_GROUP, CLOUD_MAX, joint_width), F32),
            pltpu.SemaphoreType.DMA((2, 2 * BACK_GROUP)),
            pltpu.SemaphoreType.DMA,
        ],
        compiler_params=pltpu.CompilerParams(vmem_limit_bytes=VMEM_BYTES),
        cost_estimate=cost(18),
        name="attention_back",
    )(lens, joint, grad_attended)


def in_back_kernel(
    devices, used_ref, lens, grad_joint, tokens, prenorm_gain, prenorm_shift, attention_in,
    keep_out, send_out,
    sum_in, small, joint_sum, pack, pack_sem,
):
    index = pl.program_id(0)
    used = used_ref[0]
    width = tokens.shape[1]
    copies = [
        pltpu.make_async_copy(pack.at[0], keep_out, pack_sem.at[0]),
        pltpu.make_async_copy(pack.at[1], send_out, pack_sem.at[1]),
    ]

    @pl.when(index == 0)
    def _():
        sum_in[...] = jnp.zeros_like(sum_in)
        joint_sum[...] = jnp.zeros_like(joint_sum)

    @pl.when(index < used)
    def _():
        spread, _ = cloud_totals(lens)
        live = lax.broadcasted_iota(jnp.int32, (TILE, 1), 0) + index * TILE < spread
        unit, _ = norm_parts(tokens[...])
        grads = jnp.where(live, grad_joint[...], 0.0)
        joint_sum[...] += column_sum(grads)
        sum_in[...] += dot3(split(unit.T), split(grads))

    @pl.when(index == used - 1)
    def _():
        weighted = split(sum_in[...] * attention_in[...])
        ones = jnp.ones((8, joint_sum.shape[1]), BF16)
        small[...] = jnp.zeros_like(small)
        small[0:1, :] = (dot(ones, weighted[0], 1, 1) + dot(ones, weighted[1], 1, 1))[:1]
        columns = split(jnp.broadcast_to(joint_sum[...], (8, joint_sum.shape[1])))
        small[1:2, :] = dot3(columns, split(attention_in[...]), 1, 1)[:1]
        gains = jnp.broadcast_to(row_of(prenorm_gain), (8, width)).T[:, :1]
        shifts = jnp.broadcast_to(row_of(prenorm_shift), (8, width)).T[:, :1]
        sum_in[...] = sum_in[...] * gains + shifts * joint_sum[...]
        pack_tiles([sum_in, small], pack, devices)
        for copy in copies:
            copy.start()

    @pl.when(index == pl.num_programs(0) - 1)
    def _():
        for copy in copies:
            copy.wait()


def run_in_back(used, lens, grad_joint, tokens, weights, devices):
    spaced_count, width = tokens.shape
    joint_width = grad_joint.shape[1]
    extra = [weights[name] for name in ("prenorm_gain", "prenorm_shift", "attention_in")]
    chunk = in_chunk(width)
    slots = slots_shape(chunk, devices)
    return pl.pallas_call(
        lambda used, lens, *refs: in_back_kernel(devices, used, lens, *refs),
        out_shape=(shape(*slots), shape(*slots)),
        grid_spec=pltpu.PrefetchScalarGridSpec(
            num_scalar_prefetch=1,
            grid=(spaced_count // TILE,),
            in_specs=[smem_spec(), rows_spec(joint_width), rows_spec(width)]
            + [whole_spec(array) for array in extra],
            out_specs=[any_spec()] * 2,
            scratch_shapes=[pltpu.VMEM(dims, F32) for dims in chunk]
            + [
                pltpu.VMEM((1, joint_width), F32),
                pltpu.VMEM((2,) + slots, F32),
                pltpu.SemaphoreType.DMA((2,)),
            ],
        ),
        compiler_params=pltpu.CompilerParams(vmem_limit_bytes=VMEM_BYTES),
        cost_estimate=cost(14),
        name="in_back",
    )(used, lens, grad_joint, tokens, *extra)


def input_kernel(
    used_ref, groups, grad_joint, tokens, grad_middle, prenorm_gain, attention_in, spaced_grad, in_high, in_low,
):
    index = pl.program_id(0)

    @pl.when(index == 0)
    def _():
        split_weight(attention_in, in_high, in_low)

    @pl.when(index < used_ref[0])
    def _():
        unit, inverse = norm_parts(tokens[...])
        grad_normed = dot3(split(grad_joint[...]), (in_high[...], in_low[...]), 1, 1)
        spaced_grad[...] = norm_back(grad_normed, unit, inverse, row_of(prenorm_gain))

        def add_group(group, carry):
            source = groups[index * (TILE // 8) + group]
            rows = pl.ds(start_of(group * 8), 8)
            added = grad_middle[pl.ds(start_of(jnp.maximum(source, 0) * 8), 8), :]
            spaced_grad[rows, :] += jnp.where(source >= 0, added, 0.0)
            return carry

        lax.fori_loop(0, TILE // 8, add_group, 0, unroll=8)


def run_input(used, groups, grad_joint, tokens, grad_middle, weights):
    spaced_count, width = tokens.shape
    extra = [weights["prenorm_gain"], weights["attention_in"]]
    return pl.pallas_call(
        input_kernel,
        out_shape=shape(spaced_count, width),
        grid_spec=pltpu.PrefetchScalarGridSpec(
            num_scalar_prefetch=1,
            grid=(spaced_count // TILE,),
            in_specs=[smem_spec(), rows_spec(grad_joint.shape[1]), rows_spec(width), whole_spec(grad_middle)]
            + [whole_spec(array) for array in extra],
            out_specs=rows_spec(width),
            scratch_shapes=[pltpu.VMEM(weights["attention_in"].shape, BF16)] * 2,
        ),
        compiler_params=pltpu.CompilerParams(vmem_limit_bytes=VMEM_BYTES),
        cost_estimate=cost(14),
        name="input_grad",
    )(used, groups, grad_joint, tokens, grad_middle, *extra)


def restore_kernel(lens, owner, spaced_grad, spaced_pred, input_grad, predicted_turned, pred_rows):
    token_count, width = input_grad.shape
    width_out = pred_rows.shape[1]
    input_grad[...] = jnp.zeros_like(input_grad)
    pred_rows[...] = jnp.zeros_like(pred_rows)
    windows = cloud_windows(lens, token_count)
    earlier = earlier_table()
    order = lax.broadcasted_iota(jnp.int32, (2 * CLOUD_MAX, CLOUD_MAX), 1)
    for first in range(0, lens.shape[0], 4):
        clouds = range(first, min(first + 4, lens.shape[0]))
        places = [
            cloud_places(
                owner[:, pl.ds(windows[cloud][1], 2 * CLOUD_MAX)],
                windows[cloud][0] - windows[cloud][1], lens[cloud], earlier,
            )
            for cloud in clouds
        ]
        columns = [jnp.broadcast_to(place.astype(F32), (8, 2 * CLOUD_MAX)).T[:, :1].astype(jnp.int32) for place in places]
        picks = [(order == column).astype(F32).astype(BF16) for column in columns]
        for pick, cloud in zip(picks, clouds):
            _, base, spaced_start, _ = windows[cloud]
            rows, source = pl.ds(base, 2 * CLOUD_MAX), pl.ds(spaced_start, CLOUD_MAX)
            kept = lax.broadcasted_iota(jnp.int32, (CLOUD_MAX, 1), 0) < lens[cloud]
            for values, target in ((spaced_grad, input_grad), (spaced_pred, pred_rows)):
                high, low = split(jnp.where(kept, values[source, :], 0.0))
                target[rows, :] += dot(pick, high) + dot(pick, low)
    for place in range(0, token_count, 128):
        predicted_turned[:, place : place + 128] = pred_rows[place : place + 128, :].T


def run_restore(lens, owner, spaced_grad, spaced_pred):
    token_count = owner.shape[1]
    width, width_out = spaced_grad.shape[1], spaced_pred.shape[1]
    return pl.pallas_call(
        restore_kernel,
        out_shape=(shape(token_count, width), shape(width_out, token_count)),
        in_specs=[smem_spec()] + [vmem_spec()] * 3,
        out_specs=[vmem_spec()] * 2,
        scratch_shapes=[pltpu.VMEM((token_count, width_out), F32)],
        compiler_params=pltpu.CompilerParams(vmem_limit_bytes=VMEM_BYTES),
        cost_estimate=cost(8),
        name="restore",
    )(lens, owner, spaced_grad, spaced_pred)


def gather_pack(mine, theirs, pack, sems):
    copies = [
        pltpu.make_async_copy(mine, pack.at[0], sems.at[0]),
        pltpu.make_async_copy(theirs, pack.at[1], sems.at[1]),
    ]
    for copy in copies:
        copy.start()
    for copy in copies:
        copy.wait()


def block_sums_kernel(
    devices, mine, theirs,
    reduce_out, expand_out, attention_out, head_out, lastnorm_gain, lastnorm_shift, reduce_shift, head_shift,
    expand_shift, midnorm_gain, midnorm_shift, attention_shift, loss_out, rms_out, scale_out,
    sum_reduce, small, pack, sems,
):
    gather_pack(mine, theirs, pack, sems)
    unpack_tiles(pack, [sum_reduce, expand_out, attention_out, head_out, small], devices, None)
    width = small.shape[1]
    scale = 1.0 / jnp.sum(small[1:2, :], axis=1, keepdims=True)
    scale_out[...] = jnp.broadcast_to(scale, scale_out.shape)
    for target in (expand_out, attention_out, head_out):
        target[...] = target[...] * scale
    for row, target in (
        (5, lastnorm_gain), (6, lastnorm_shift), (7, reduce_shift),
        (20, midnorm_gain), (21, midnorm_shift), (22, attention_shift),
    ):
        target[...] = (small[row : row + 1, :] * scale)[0]
    for part in range(expand_shift.shape[0] // width):
        expand_shift[part * width : part * width + width] = (small[16 + part : 17 + part, :] * scale)[0]
    head_shift[...] = (small[8:9, :] * scale)[0, : head_shift.shape[0]]
    loss_out[...] = jnp.broadcast_to(jnp.sum(small[0:1, :], axis=1, keepdims=True) * scale, loss_out.shape)
    counted = 1.0 / (jnp.sum(small[9:10, :], axis=1, keepdims=True) * width)
    squares = jnp.sum(small[0:8, :], axis=1, keepdims=True)
    rms_out[...] = jnp.broadcast_to(jnp.sqrt(squares * counted), rms_out.shape)
    for place in range(0, reduce_out.shape[0], 128):
        reduce_out[place : place + 128, :] = sum_reduce[:, place : place + 128].T * scale


def in_sums_kernel(devices, scale, mine, theirs, in_out, prenorm_gain, prenorm_shift, small, pack, sems):
    gather_pack(mine, theirs, pack, sems)
    unpack_tiles(pack, [in_out, small], devices, scale[...])
    prenorm_gain[...] = small[0, :]
    prenorm_shift[...] = small[1, :]


def run_sums(kernel, scale, mine, theirs, chunk, outs, keep, devices, name):
    scales = [] if scale is None else [scale]
    return pl.pallas_call(
        lambda *refs: kernel(devices, *refs),
        out_shape=tuple(shape(*dims) for dims in outs),
        in_specs=[vmem_spec()] * len(scales) + [any_spec()] * 2,
        out_specs=[vmem_spec()] * len(outs),
        scratch_shapes=[pltpu.VMEM(dims, F32) for dims in keep]
        + [
            pltpu.VMEM((2,) + slots_shape(chunk, devices), F32),
            pltpu.SemaphoreType.DMA((2,)),
        ],
        compiler_params=pltpu.CompilerParams(vmem_limit_bytes=VMEM_BYTES),
        cost_estimate=cost(4),
        name=name,
    )(*scales, mine, theirs)


def shards(
    tokens, cloud_lengths, owner_slot, targets, prenorm_gain, prenorm_shift, attention_in,
    attention_out, attention_shift, midnorm_gain, midnorm_shift, expand_weight, expand_shift,
    reduce_weight, reduce_shift, lastnorm_gain, lastnorm_shift, head_weight, head_shift,
):
    token_count, width = tokens.shape
    hidden_width = expand_weight.shape[1]
    devices = lax.axis_size("dp")
    slot_count, width_out = targets.shape
    capacity = slot_count // devices
    arrived = lax.all_to_all(
        targets.reshape(devices, capacity, width_out), "dp", split_axis=0, concat_axis=0, tiled=True
    ).reshape(slot_count, width_out)
    weights = dict(
        prenorm_gain=prenorm_gain, prenorm_shift=prenorm_shift, attention_in=attention_in,
        attention_out=attention_out, attention_shift=attention_shift,
        midnorm_gain=midnorm_gain, midnorm_shift=midnorm_shift,
        expand_weight=expand_weight, expand_shift=expand_shift, reduce_weight=reduce_weight,
        reduce_shift=reduce_shift, lastnorm_gain=lastnorm_gain,
        lastnorm_shift=lastnorm_shift, head_turned=head_weight.T,
        head_shift=head_shift,
    )
    owner = owner_slot[None]
    spaced_tokens, joint, attended, owners, valid, used, groups = run_attend(
        tokens, cloud_lengths, owner, weights["prenorm_gain"], weights["prenorm_shift"], attention_in
    )
    predicted, grad_middle, grad_attended, block_keep, block_send = run_block(
        used, groups, attended, spaced_tokens, valid, owners, arrived, weights, devices
    )
    block_sum = DeviceSum(block_keep, block_send, devices)
    beside([block_sum], ())
    grad_joint = beside(
        [block_sum], run_attention_back(cloud_lengths, joint, grad_attended)
    )
    in_keep, in_send = beside(
        [block_sum], run_in_back(used, cloud_lengths, grad_joint, spaced_tokens, weights, devices)
    )
    in_sum = DeviceSum(in_keep, in_send, devices)
    sums = [in_sum, block_sum]
    grad_joint = beside([in_sum], grad_joint)
    spaced_grad = beside(sums, run_input(used, groups, grad_joint, spaced_tokens, grad_middle, weights))
    input_grad, predicted_turned = beside(
        sums, run_restore(cloud_lengths, owner, spaced_grad, predicted)
    )
    while not block_sum.done():
        beside(sums, ())
    chunk = block_chunk(width, hidden_width, width_out)
    vector = (width,)
    (
        grad_reduce, grad_expand, grad_out, grad_head_turned, grad_last_gain, grad_last_shift, grad_reduce_shift,
        grad_head_shift, grad_expand_shift, grad_mid_gain, grad_mid_shift, grad_out_shift, loss, rms, scale,
    ) = beside(
        [in_sum],
        run_sums(
            block_sums_kernel, None, block_sum.total, block_sum.theirs, chunk,
            [
                (hidden_width, width), chunk[1], chunk[2], chunk[3], vector, vector, vector,
                (width_out,), (hidden_width,), vector, vector, vector, (8, 128), (8, 128), (8, 128),
            ],
            [chunk[0], chunk[4]], devices, "block_sums",
        ),
    )
    run_out([in_sum])
    chunk = in_chunk(width)
    grad_in, grad_pre_gain, grad_pre_shift = run_sums(
        in_sums_kernel, scale, in_sum.total, in_sum.theirs, chunk,
        [chunk[0], (width,), (width,)], [chunk[1]], devices, "in_sums",
    )
    return (
        loss[0, 0],
        predicted_turned.T,
        input_grad,
        grad_pre_gain,
        grad_pre_shift,
        grad_in,
        grad_out,
        grad_out_shift,
        grad_mid_gain,
        grad_mid_shift,
        grad_expand,
        grad_expand_shift,
        grad_reduce,
        grad_reduce_shift,
        grad_last_gain,
        grad_last_shift,
        grad_head_turned.T,
        grad_head_shift,
        rms[2:5, 0],
    )


def solution(mesh):
    row = P("dp", None)
    return jax.shard_map(
        shards,
        mesh=mesh,
        in_specs=(row, P("dp"), P("dp"), row) + (P(),) * 15,
        out_specs=(P(), row, row) + (P(),) * 16,
        check_vma=False,
    )
```

```python
import math

import jax
import jax.numpy as jnp
from jax import lax
from jax.experimental import pallas as pl
from jax.experimental.pallas import tpu as pltpu
from jax.sharding import PartitionSpec as P

HEADS = 6
CLOUD_MAX = 128
TILE = 256
GROUP = 2
BACK_GROUP = 1
MASKED_TILE = 512
VISIBLE_MAX = 64
EPSILON = 1e-05
F32 = jnp.float32
BF16 = jnp.bfloat16
VMEM_BYTES = 60 * 1024 * 1024


def split(values):
    high = values.astype(BF16)
    low = (values - high.astype(F32)).astype(BF16)
    return high, low


def dot(left, right, left_dim=1, right_dim=0):
    return lax.dot_general(
        left, right, (((left_dim,), (right_dim,)), ((), ())), preferred_element_type=F32
    )


def dot3(left, right, left_dim=1, right_dim=0):
    left_high, left_low = left
    right_high, right_low = right
    return dot(left_high, right_high, left_dim, right_dim) + (
        dot(left_high, right_low, left_dim, right_dim)
        + dot(left_low, right_high, left_dim, right_dim)
    )


def dot_deep(left, triple, right_dim=0):
    left_high, left_low = left
    return dot(jnp.concatenate([left_high, left_high, left_low], axis=1), triple, 1, right_dim)


def dot_wide(left, pair, right_dim=0):
    left_high, left_low = left
    columns = pair.shape[1 - right_dim] // 2
    both = dot(left_high, pair, 1, right_dim)
    high = pair[:columns, :] if right_dim else pair[:, :columns]
    return both[:, :columns] + (both[:, columns:] + dot(left_low, high, 1, right_dim))


def dot_pair(left, right):
    right_high, right_low = right
    return dot(jnp.concatenate(left, axis=1), jnp.concatenate([right_high, right_high], axis=1), 1, 1) + dot(
        left[0], right_low, 1, 1
    )


def norm_parts(values):
    average = jnp.mean(values, axis=-1, keepdims=True)
    centred = values - average
    spread = jnp.mean(centred * centred, axis=-1, keepdims=True)
    inverse = lax.rsqrt(spread + EPSILON)
    return centred * inverse, inverse


def norm_back(grad_out, unit_rows, inverse, scale_gain):
    scaled = grad_out * scale_gain
    average_grad = jnp.mean(scaled, axis=-1, keepdims=True)
    project_grad = jnp.mean(scaled * unit_rows, axis=-1, keepdims=True)
    return inverse * (scaled - average_grad - unit_rows * project_grad)


def any_spec():
    return pl.BlockSpec(memory_space=pltpu.HBM)


def vmem_spec():
    return pl.BlockSpec(memory_space=pltpu.VMEM)


def smem_spec():
    return pl.BlockSpec(memory_space=pltpu.SMEM)


def cost(microseconds):
    return pl.CostEstimate(flops=microseconds * 10**9, bytes_accessed=microseconds * 10**6, transcendentals=0)


def shape(*dims):
    return jax.ShapeDtypeStruct(dims, F32)


def row_of(vector):
    return vector[...][None, :]


def column_sum(values):
    return jnp.sum(values, axis=0, keepdims=True)


def split_weight(source, target, axis, step=128):
    rows, columns = source.shape

    def body(index, carry):
        start = pl.multiple_of(index * step, step)
        for part, values in enumerate(split_three(source[pl.ds(start, step), :])):
            if axis == 0:
                target[pl.ds(start + part * rows, step), :] = values
            else:
                target[pl.ds(start, step), part * columns : part * columns + columns] = values
        return carry

    lax.fori_loop(0, rows // step, body, 0)


def split_three(values):
    high, low = split(values)
    return high, low, high


def spaced(length):
    return (length + 7) // 8 * 8


def aligned_rows(token_count, cloud_count):
    return (token_count + 8 * cloud_count + TILE - 1) // TILE * TILE


def masked_of(length):
    return 3 * length // 5


def tiles_of(rows, tile=TILE):
    return (rows + tile - 1) // tile


def compact_rows(token_count, cloud_count):
    return tiles_of(masked_of(token_count) + 8 * cloud_count, MASKED_TILE) * MASKED_TILE


def visible_rows(token_count, cloud_count):
    return tiles_of(token_count - masked_of(token_count) + 9 * cloud_count) * TILE


def cloud_totals(lens):
    spread, masked, visible = jnp.int32(0), jnp.int32(0), jnp.int32(0)
    for cloud in range(lens.shape[0]):
        length = lens[cloud]
        spread = spread + spaced(length)
        masked = masked + spaced(masked_of(length))
        visible = visible + spaced(length - masked_of(length))
    return spread, masked, visible


def cloud_windows(lens, token_count):
    start, spaced_start, masked_start, visible_start = (jnp.int32(0),) * 4
    windows = []
    for cloud in range(lens.shape[0]):
        length = lens[cloud]
        base = jnp.minimum(start // 128, token_count // 128 - 2) * 128
        windows.append(
            (start, pl.multiple_of(base, 128), start_of(spaced_start), start_of(masked_start), start_of(visible_start))
        )
        start = start + length
        spaced_start = spaced_start + spaced(length)
        masked_start = masked_start + spaced(masked_of(length))
        visible_start = visible_start + spaced(length - masked_of(length))
    return windows


def earlier_table():
    rows = lax.broadcasted_iota(jnp.int32, (2 * CLOUD_MAX, 2 * CLOUD_MAX), 0)
    columns = lax.broadcasted_iota(jnp.int32, (2 * CLOUD_MAX, 2 * CLOUD_MAX), 1)
    return (rows < columns).astype(F32).astype(BF16)


def cloud_places(slots, offset, length, earlier):
    lanes = lax.broadcasted_iota(jnp.int32, (1, 2 * CLOUD_MAX), 1)
    inside = jnp.logical_and(lanes >= offset, lanes < offset + length)
    masked = jnp.logical_and(inside, slots >= 0)
    flags = jnp.broadcast_to(masked.astype(F32), (8, 2 * CLOUD_MAX)).astype(BF16)
    rank = dot(flags, earlier)[:1].astype(jnp.int32)
    visible = masked_of(length) + lanes - offset - rank
    return jnp.where(masked, rank, jnp.where(inside, visible, -1))


def start_of(place):
    return pl.multiple_of(place, 8)


def gelu_parts(pre_act):
    cumulative = 0.5 * (1.0 + lax.erf(pre_act * (1.0 / math.sqrt(2.0))))
    density = jnp.exp(-0.5 * pre_act * pre_act) * (1.0 / math.sqrt(2.0 * math.pi))
    return pre_act * cumulative, cumulative + pre_act * density


def slot_place(relative, part, devices):
    x, y, rest = (relative >> 1) & 1, (relative >> 2) & 1, relative >> 3
    major, minor = (x, y) if part == 0 else (y, x)
    return relative & 1, major * (devices // 4) + minor * (devices // 8) + rest


def tile_list(shapes):
    return [
        (which, row, column)
        for which, (rows, columns) in enumerate(shapes)
        for row in range(0, rows, 8)
        for column in range(0, columns, 128)
    ]


def atom_tiles(shapes, devices):
    return -(-len(tile_list(shapes)) // (2 * devices))


def slots_shape(shapes, devices):
    return (2, devices // 2, atom_tiles(shapes, devices) * 8, 128)


def pack_tiles(sources, pack, devices):
    me = lax.axis_index("dp")
    tiles = tile_list([source.shape for source in sources])
    each = atom_tiles([source.shape for source in sources], devices)
    for atom in range(-(-len(tiles) // each)):
        part, owner = atom // devices, atom % devices
        bit, place = slot_place(me ^ owner, part, devices)
        for number, (which, row, column) in enumerate(tiles[atom * each : atom * each + each]):
            pack[bit, part, place, number * 8 : number * 8 + 8, :] = sources[which][
                row : row + 8, column : column + 128
            ]


def unpack_tiles(pack, targets, devices, scale):
    me = lax.axis_index("dp")
    tiles = tile_list([target.shape for target in targets])
    each = atom_tiles([target.shape for target in targets], devices)
    for atom in range(-(-len(tiles) // each)):
        part, owner = atom // devices, atom % devices
        bit, place = slot_place(me ^ owner, part, devices)
        for number, (which, row, column) in enumerate(tiles[atom * each : atom * each + each]):
            piece = pack[bit, part, place, number * 8 : number * 8 + 8, :]
            targets[which][row : row + 8, column : column + 128] = (
                piece if scale is None else piece * scale
            )


def swap(values, bits, devices):
    return lax.ppermute(values, "dp", [(device, device ^ bits) for device in range(devices)])


def rest_groups(devices):
    count = (devices // 8).bit_length() - 1
    groups = []
    while count:
        step = 2 if count >= 2 else 1
        count -= step
        groups.append((3 + count, 1 << step))
    return groups


class DeviceSum:
    def __init__(self, keep, send, devices):
        self.devices = devices
        self.groups = rest_groups(devices)
        self.keep, self.send = keep, send
        self.stage = 0
        self.last = 5 + 2 * len(self.groups)

    def start(self):
        devices, stage, count = self.devices, self.stage, len(self.groups)
        if stage == 0:
            self.moving = [swap(self.send, 1, devices)]
        elif stage <= 2:
            size = devices // (4, 8)[stage - 1]
            bits = ((2, 4), (4, 2))[stage - 1]
            self.moving = [swap(half[size:], bit, devices) for half, bit in zip(self.halves, bits)]
            self.halves = [half[:size] for half in self.halves]
        elif stage < 3 + count:
            shift, size = self.groups[stage - 3]
            total = self.total.reshape((size, -1) + self.total.shape[1:])
            self.moving = [swap(total[slot], slot << shift, devices) for slot in range(1, size)]
            self.total = total[0]
        elif stage < 3 + 2 * count:
            shift, size = self.groups[3 + 2 * count - 1 - stage]
            self.moving = [swap(self.total, slot << shift, devices) for slot in range(1, size)]
        elif stage < 5 + 2 * count:
            bits = ((4, 2), (2, 4))[stage - 3 - 2 * count]
            self.moving = [swap(half, bit, devices) for half, bit in zip(self.halves, bits)]
        else:
            self.moving = [swap(self.total, 1, devices)]

    def finish(self):
        stage, count = self.stage, len(self.groups)
        if stage == 0:
            total = self.keep + self.moving[0]
            self.halves = [total[0], total[1]]
        elif stage <= 2:
            self.halves = [half + moved for half, moved in zip(self.halves, self.moving)]
            if stage == 2:
                self.total = jnp.stack(self.halves, axis=1)
        elif stage < 3 + count:
            self.total = sum(self.moving, self.total)
        elif stage < 3 + 2 * count:
            self.total = jnp.concatenate([self.total] + self.moving, axis=0)
            if stage == 2 + 2 * count:
                self.halves = [self.total[:, 0], self.total[:, 1]]
        elif stage < 5 + 2 * count:
            self.halves = [jnp.concatenate([half, moved]) for half, moved in zip(self.halves, self.moving)]
            if stage == 4 + 2 * count:
                self.total = jnp.stack(self.halves)
        else:
            self.theirs = self.moving[0]
        self.stage += 1

    def done(self):
        return self.stage > self.last

    def state(self):
        if hasattr(self, "total") and (3 <= self.stage < 3 + 2 * len(self.groups) or self.stage >= self.last):
            return self.total
        return self.halves

    def set_state(self, state):
        if hasattr(self, "total") and (3 <= self.stage < 3 + 2 * len(self.groups) or self.stage >= self.last):
            self.total = state
        else:
            self.halves = state


def beside(sums, outs):
    sums = [one for one in sums if not one.done()]
    for one in sums:
        one.start()
    moving, outs = lax.optimization_barrier(([one.moving for one in sums], outs))
    for one, moved in zip(sums, moving):
        one.moving = moved
        one.finish()
    going = [one for one in sums if not one.done()]
    states, outs = lax.optimization_barrier(([one.state() for one in going], outs))
    for one, state in zip(going, states):
        one.set_state(state)
    return outs


def run_stage(one):
    one.start()
    one.finish()


def run_out(sums):
    while not all(one.done() for one in sums):
        for one in sums:
            if not one.done():
                run_stage(one)


def attend_kernel(
    lens, tokens_hbm, owner, prenorm_gain, prenorm_shift, attention_in,
    tokens_out, joint_out, masked_tokens_out, masked_attended_out, visible_tokens_out, visible_attended_out,
    owners, valid, used_out, groups_out,
    raw, tokens, joint, masked_tokens, masked_attended, visible_tokens, visible_attended, in_parts,
    token_sem, joint_sem, out_sems,
):
    token_count = owner.shape[1]
    tiles = tokens.shape[0] // TILE
    width = tokens.shape[1]
    spread, masked_total, visible_total = cloud_totals(lens)
    used, visible_used = tiles_of(spread), tiles_of(visible_total)
    masked_used = tiles_of(masked_total, MASKED_TILE)
    used_out[0] = used
    used_out[1] = masked_used
    used_out[2] = visible_used

    def tile_rows(index, tile=TILE):
        return pl.ds(pl.multiple_of(index * tile, tile), tile)

    token_copy = pltpu.make_async_copy(tokens_hbm, raw, token_sem)
    token_copy.start()
    split_weight(attention_in, in_parts, 0)
    owners[...] = jnp.full(owners.shape, -1, jnp.int32)
    valid[...] = jnp.zeros(valid.shape, F32)
    blank = jnp.zeros((TILE, width), F32)
    tokens[tile_rows(used - 1), :] = blank
    for kept in (masked_tokens, masked_attended):
        kept[tile_rows(masked_used - 1, MASKED_TILE), :] = jnp.zeros((MASKED_TILE, width), F32)
    for kept in (visible_tokens, visible_attended):
        kept[tile_rows(visible_used - 1), :] = blank

    def no_group(index, carry):
        groups_out[index] = -1
        return carry

    lax.fori_loop(0, groups_out.shape[0], no_group, 0, unroll=8)

    def cloud_groups(cloud, carry):
        spaced_group, masked_group = carry
        count = spaced(masked_of(lens[cloud])) // 8

        def group(index, carry):
            groups_out[spaced_group + index] = masked_group + index
            return carry

        lax.fori_loop(0, count, group, 0)
        return spaced_group + spaced(lens[cloud]) // 8, masked_group + count

    lax.fori_loop(0, lens.shape[0], cloud_groups, (jnp.int32(0), jnp.int32(0)))
    windows = cloud_windows(lens, token_count)
    earlier = earlier_table()
    wide = lax.broadcasted_iota(jnp.int32, (1, 2 * CLOUD_MAX), 1)
    order = lax.broadcasted_iota(jnp.int32, (CLOUD_MAX + VISIBLE_MAX, 2 * CLOUD_MAX), 0)
    token_copy.wait()
    for first in range(0, lens.shape[0], 4):
        clouds = range(first, min(first + 4, lens.shape[0]))
        slots = [owner[:, pl.ds(windows[cloud][1], 2 * CLOUD_MAX)] for cloud in clouds]
        places = [
            cloud_places(slot, windows[cloud][0] - windows[cloud][1], lens[cloud], earlier)
            for slot, cloud in zip(slots, clouds)
        ]
        rows_of = [
            jnp.where(order < CLOUD_MAX, order, order - CLOUD_MAX + masked_of(lens[cloud])) for cloud in clouds
        ]
        picks = [(row == place).astype(F32).astype(BF16) for row, place in zip(rows_of, places)]
        for pick, slot, cloud in zip(picks, slots, clouds):
            _, base, spaced_start, masked_start, visible_start = windows[cloud]
            rows = raw[pl.ds(base, 2 * CLOUD_MAX), :]
            high = rows.astype(BF16)
            rest = rows - high.astype(F32)
            mid, low = split(rest)
            moved = (dot(pick, high) + dot(pick, mid)) + dot(pick, low)
            tokens[pl.ds(spaced_start, CLOUD_MAX), :] = moved[:CLOUD_MAX]
            masked_tokens[pl.ds(masked_start, CLOUD_MAX), :] = moved[:CLOUD_MAX]
            visible_tokens[pl.ds(visible_start, VISIBLE_MAX), :] = moved[CLOUD_MAX:]
            parts = jnp.concatenate(
                [(slot >> 6).astype(F32), (slot & 63).astype(F32), jnp.zeros((6, 2 * CLOUD_MAX), F32)], axis=0
            )
            parts = dot(parts.astype(BF16), pick[:CLOUD_MAX], 1, 1)
            moved = (parts[0:1] * 64.0 + parts[1:2]).astype(jnp.int32)
            moved = jnp.concatenate([moved, jnp.zeros((1, CLOUD_MAX), jnp.int32)], axis=1)
            masked, visible = masked_of(lens[cloud]), lens[cloud] - masked_of(lens[cloud])
            offset = masked_start % 128
            lanes = pl.ds(pl.multiple_of(masked_start // 128 * 128, 128), 2 * CLOUD_MAX)
            inside = jnp.logical_and(wide >= offset, wide < offset + masked)
            owners[:, lanes] = jnp.where(inside, pltpu.roll(moved, offset, 1), owners[:, lanes])
            offset = visible_start % 128
            lanes = pl.ds(pl.multiple_of(visible_start // 128 * 128, 128), 2 * CLOUD_MAX)
            inside = jnp.logical_and(wide >= offset, wide < offset + visible)
            valid[:, lanes] = jnp.where(inside, 1.0, valid[:, lanes])

    def joint_copies(index):
        rows = tile_rows(index)
        return [
            pltpu.make_async_copy(joint.at[rows], joint_out.at[rows], joint_sem.at[index]),
            pltpu.make_async_copy(tokens.at[rows], tokens_out.at[rows], out_sems.at[0, index]),
        ]

    def joint_tile(index, carry):
        rows = tile_rows(index)
        unit, _ = norm_parts(tokens[rows, :])
        normed = split(unit * row_of(prenorm_gain) + row_of(prenorm_shift))
        joint[rows, :] = dot_deep(normed, in_parts[...])
        for copy in joint_copies(index):
            copy.start()
        return carry

    lax.fori_loop(0, used, joint_tile, 0)
    tail = pl.ds(pl.multiple_of(used * TILE, TILE), CLOUD_MAX)
    joint[tail, :] = jnp.zeros((CLOUD_MAX, joint.shape[1]), F32)
    tail_copy = pltpu.make_async_copy(joint.at[tail], joint_out.at[tail], joint_sem.at[tiles])
    tail_copy.start()

    lane = lax.broadcasted_iota(jnp.int32, (CLOUD_MAX, 128), 1)
    first_head = lane < 64
    wide_lane = lax.broadcasted_iota(jnp.int32, (2 * CLOUD_MAX, CLOUD_MAX), 1)
    empty = jnp.zeros((CLOUD_MAX, 128), BF16)

    visible_order = lax.broadcasted_iota(jnp.int32, (VISIBLE_MAX, CLOUD_MAX), 0)
    visible_column = lax.broadcasted_iota(jnp.int32, (VISIBLE_MAX, CLOUD_MAX), 1)

    def clouds(index, carry):
        start, masked_start, visible_start = carry
        lengths = [lens[GROUP * index + number] for number in range(GROUP)]
        places, masked_places, visible_places = [], [], []
        for length in lengths:
            places.append(pl.ds(start_of(start), CLOUD_MAX))
            masked_places.append(pl.ds(start_of(masked_start), CLOUD_MAX))
            visible_places.append(pl.ds(start_of(visible_start), VISIBLE_MAX))
            start = start + spaced(length)
            masked_start = masked_start + spaced(masked_of(length))
            visible_start = visible_start + spaced(length - masked_of(length))
        picks = [
            jnp.logical_and(visible_column == visible_order + masked_of(length), visible_column < length)
            .astype(F32)
            .astype(BF16)
            for length in lengths
        ]
        insides = [wide_lane < length for length in lengths]
        work = [(number, pair) for number in range(GROUP) for pair in range(HEADS // 2)]
        lefts, rights = [], []
        for number, pair in work:
            rows = places[number]
            query = joint[rows, pair * 128 : pair * 128 + 128] * 0.125
            key_high, key_low = split(joint[rows, width + pair * 128 : width + pair * 128 + 128])
            both = jnp.concatenate(
                [jnp.where(first_head, query, 0.0), jnp.where(first_head, 0.0, query)], axis=0
            )
            lefts.append(jnp.concatenate(split(both), axis=1))
            rights.append(
                jnp.concatenate(
                    [
                        jnp.concatenate([key_high, key_high], axis=1),
                        jnp.concatenate([key_low, empty], axis=1),
                    ],
                    axis=0,
                )
            )
        scores = [dot(left, right, 1, 1) for left, right in zip(lefts, rights)]
        scores = [
            jnp.where(insides[number], score[:, :128] + score[:, 128:], -1e30)
            for (number, _), score in zip(work, scores)
        ]
        peaks = [jnp.max(score, axis=-1, keepdims=True) for score in scores]
        weights = [jnp.exp(score - peak) for score, peak in zip(scores, peaks)]
        scales = [1.0 / jnp.sum(weight, axis=-1, keepdims=True) for weight in weights]
        lefts = [jnp.concatenate(split(weight * scale), axis=1) for weight, scale in zip(weights, scales)]
        rights = []
        for number, pair in work:
            value_high, value_low = split(
                joint[places[number], 2 * width + pair * 128 : 2 * width + pair * 128 + 128]
            )
            rights.append(
                jnp.concatenate(
                    [
                        jnp.concatenate([value_high, value_low], axis=1),
                        jnp.concatenate([value_high, empty], axis=1),
                    ],
                    axis=0,
                )
            )
        mixed = [dot(left, right) for left, right in zip(lefts, rights)]
        for (number, pair), both in zip(work, mixed):
            both = both[:, :128] + both[:, 128:]
            both = jnp.where(first_head, both[:CLOUD_MAX], both[CLOUD_MAX:])
            columns = slice(pair * 128, pair * 128 + 128)
            masked_attended[masked_places[number], columns] = both
            moved = dot(picks[number], jnp.concatenate(split(both), axis=1))
            visible_attended[visible_places[number], columns] = moved[:, :128] + moved[:, 128:]
        return start, masked_start, visible_start

    zero = jnp.int32(0)
    lax.fori_loop(0, lens.shape[0] // GROUP, clouds, (zero, zero, zero))

    def masked_copies(index):
        rows = tile_rows(index, MASKED_TILE)
        return [
            pltpu.make_async_copy(masked_tokens.at[rows], masked_tokens_out.at[rows], out_sems.at[1, index]),
            pltpu.make_async_copy(masked_attended.at[rows], masked_attended_out.at[rows], out_sems.at[2, index]),
        ]

    def visible_copies(index):
        rows = tile_rows(index)
        return [
            pltpu.make_async_copy(visible_tokens.at[rows], visible_tokens_out.at[rows], out_sems.at[3, index]),
            pltpu.make_async_copy(visible_attended.at[rows], visible_attended_out.at[rows], out_sems.at[4, index]),
        ]

    def begin(copies_of):
        def body(index, carry):
            for copy in copies_of(index):
                copy.start()
            return carry

        return body

    def finish(copies_of):
        def body(index, carry):
            for copy in copies_of(index):
                copy.wait()
            return carry

        return body

    lax.fori_loop(0, masked_used, begin(masked_copies), 0)
    lax.fori_loop(0, visible_used, begin(visible_copies), 0)
    tail_copy.wait()
    lax.fori_loop(0, used, finish(joint_copies), 0)
    lax.fori_loop(0, masked_used, finish(masked_copies), 0)
    lax.fori_loop(0, visible_used, finish(visible_copies), 0)


def run_attend(tokens, lens, owner, prenorm_gain, prenorm_shift, attention_in):
    token_count, width = tokens.shape
    joint_width = attention_in.shape[1]
    spaced_count = aligned_rows(token_count, lens.shape[0])
    masked_count = compact_rows(token_count, lens.shape[0])
    visible_count = visible_rows(token_count, lens.shape[0])
    tiles = spaced_count // TILE
    return pl.pallas_call(
        attend_kernel,
        out_shape=(
            shape(spaced_count, width),
            shape(spaced_count + CLOUD_MAX, joint_width),
            shape(masked_count, width),
            shape(masked_count, width),
            shape(visible_count, width),
            shape(visible_count, width),
            jax.ShapeDtypeStruct((1, masked_count + 256), jnp.int32),
            shape(1, visible_count + 256),
            jax.ShapeDtypeStruct((3,), jnp.int32),
            jax.ShapeDtypeStruct((spaced_count // 8,), jnp.int32),
        ),
        in_specs=[smem_spec(), any_spec()] + [vmem_spec()] * 4,
        out_specs=[any_spec()] * 6 + [vmem_spec()] * 2 + [smem_spec()] * 2,
        scratch_shapes=[
            pltpu.VMEM((token_count, width), F32),
            pltpu.VMEM((spaced_count, width), F32),
            pltpu.VMEM((spaced_count + CLOUD_MAX, joint_width), F32),
            pltpu.VMEM((masked_count + CLOUD_MAX, width), F32),
            pltpu.VMEM((masked_count + CLOUD_MAX, width), F32),
            pltpu.VMEM((visible_count + VISIBLE_MAX, width), F32),
            pltpu.VMEM((visible_count + VISIBLE_MAX, width), F32),
            pltpu.VMEM((3 * width, joint_width), BF16),
            pltpu.SemaphoreType.DMA,
            pltpu.SemaphoreType.DMA((tiles + 1,)),
            pltpu.SemaphoreType.DMA((5, tiles)),
        ],
        compiler_params=pltpu.CompilerParams(vmem_limit_bytes=48 * 2**20),
        cost_estimate=cost(26),
        name="attend",
    )(lens, tokens, owner, prenorm_gain, prenorm_shift, attention_in)


def stage_weights(staged, sems):
    copies = [
        pltpu.make_async_copy(weight, place, sems.at[number])
        for number, (weight, place, _, _) in enumerate(staged)
    ]
    for copy in copies:
        copy.start()
    return copies


def split_staged(copies, staged):
    for copy, (_, place, parts, axis) in zip(copies, staged):
        copy.wait()
        split_weight(place, parts, axis)


def block_rows(
    attended, tokens, out_parts, attention_shift, midnorm_gain, midnorm_shift, expand_parts, expand_shift,
    reduce_parts, reduce_shift,
):
    width = tokens.shape[1]
    mixed = dot_wide(split(attended[...]), out_parts[:, : 2 * width]) + row_of(attention_shift)
    middle = tokens[...] + mixed
    unit, inverse = norm_parts(middle)
    normed = unit * row_of(midnorm_gain) + row_of(midnorm_shift)
    pre_act = dot_deep(split(normed), expand_parts[...]) + row_of(expand_shift)
    hidden, slope = gelu_parts(pre_act)
    hidden = split(hidden)
    branch = dot_wide(hidden, reduce_parts[:, : 2 * width]) + row_of(reduce_shift)
    return mixed, middle, (unit, inverse, normed), hidden, slope, branch


def fold_lanes(lanes):
    return sum(lanes[:, place : place + 128] for place in range(0, lanes.shape[1], 128))


def lanes_to_rows(lanes):
    return jnp.broadcast_to(lanes, (8, lanes.shape[1])).T[:, :1]


def add_squares(stats, live, stream, mixed, branch):
    for row, values in enumerate((stream, mixed, branch)):
        stats[row : row + 1, :] += column_sum(jnp.where(live, values * values, 0.0))


def block_kernel(
    devices, used_ref, attended, tokens, owners, targets, attention_out,
    attention_shift, midnorm_gain, midnorm_shift, expand_weight, expand_shift, reduce_weight,
    reduce_shift, lastnorm_gain, lastnorm_shift, head_turned, head_shift,
    predicted, grad_middle, grad_attended, stats, keep_out, send_out,
    sum_reduce, sum_expand, sum_out, sum_head, small, pack,
    out_stage, expand_stage, reduce_stage, out_parts, expand_parts, reduce_parts,
    head_high, head_low, turned_high, turned_low, target_parts, pred_rows, true_rows, distance, second,
    col_low, col_sum, shift_column, pack_sem, weight_sems,
):
    index = pl.program_id(0)
    used = used_ref[1]
    slot_count, width_out = targets.shape
    points = width_out // 3
    width = tokens.shape[1]
    pack_copies = [
        pltpu.make_async_copy(pack.at[0], keep_out, pack_sem.at[0]),
        pltpu.make_async_copy(pack.at[1], send_out, pack_sem.at[1]),
    ]

    @pl.when(index == 0)
    def _():
        staged = [
            (attention_out, out_stage, out_parts, 1),
            (expand_weight, expand_stage, expand_parts, 0),
            (reduce_weight, reduce_stage, reduce_parts, 1),
        ]
        copies = stage_weights(staged, weight_sems)
        shift_column[...] = lanes_to_rows(row_of(head_shift))
        turned_high[...], turned_low[...] = split(head_turned[...])
        head_high[...], head_low[...] = split(head_turned[...].T)
        high, low = split(targets[...].T)
        target_parts[:width_out, :] = high
        target_parts[width_out:, :] = low
        for total in (small, stats, sum_reduce, sum_head, sum_expand, sum_out):
            total[...] = jnp.zeros_like(total)
        split_staged(copies, staged)

    def chamfer_half(half):
        xs = [pred_rows[half, pl.ds(c, points, stride=3), :] for c in range(3)]

        def first(j, row_low):
            gap = [xs[c] - true_rows[half, pl.ds(3 * j + c, 1), :] for c in range(3)]
            apart = gap[0] * gap[0] + gap[1] * gap[1] + gap[2] * gap[2]
            distance[j] = apart
            lowest = jnp.min(apart, axis=0, keepdims=True)
            weight = jnp.exp(lowest - apart)
            inside = column_sum(weight)
            col_low[pl.ds(j, 1), :] = lowest
            col_sum[pl.ds(j, 1), :] = inside
            second[j] = weight * (1.0 / (points * inside))
            return jnp.minimum(row_low, apart)

        row_low = lax.fori_loop(
            0, points, first, jnp.full((points, 128), jnp.inf, F32), unroll=8
        )

        def middle_pass(j, row_sum):
            weight = jnp.exp(row_low - distance[j])
            distance[j] = weight
            return row_sum + weight

        row_sum = lax.fori_loop(0, points, middle_pass, jnp.zeros((points, 128), F32), unroll=8)
        row_scale = 1.0 / (points * row_sum)

        def last(j, carry):
            weight = second[j] + distance[j] * row_scale
            return (carry[0] + weight,) + tuple(
                carry[1 + c] + weight * true_rows[half, pl.ds(3 * j + c, 1), :] for c in range(3)
            )

        zero = jnp.zeros((points, 128), F32)
        sums = lax.fori_loop(0, points, last, (zero,) * 4, unroll=8)
        terms = column_sum(row_low - jnp.log(row_sum * (1.0 / points))) + column_sum(
            col_low[...] - jnp.log(col_sum[...] * (1.0 / points))
        )
        grads = [2.0 * (sums[0] * xs[c] - sums[1 + c]) for c in range(3)]
        return terms * (1.0 / points), grads

    @pl.when(index < used)
    def _():
        mixed, middle, (unit_mid, inverse_mid, normed_mid), hidden, slope, branch = block_rows(
            attended, tokens, out_parts, attention_shift, midnorm_gain, midnorm_shift, expand_parts, expand_shift,
            reduce_parts, reduce_shift,
        )
        stream = middle + branch
        unit, inverse = norm_parts(stream)
        normed = split(unit * row_of(lastnorm_gain) + row_of(lastnorm_shift))
        pred = dot3((turned_high[...], turned_low[...]), normed, 1, 1) + shift_column[...]
        predicted[...] = pred.T
        slots = lax.broadcasted_iota(jnp.int32, (slot_count, MASKED_TILE), 0)
        slot_row = owners[...]
        masked = slot_row >= 0
        add_squares(stats, lanes_to_rows(masked.astype(F32)) > 0.5, stream, mixed, branch)
        stats[3:4, :128] += fold_lanes(masked.astype(F32))
        for half in range(MASKED_TILE // 128):
            pred_rows[half] = pred[:, half * 128 : half * 128 + 128]
        chosen = (slots == slot_row).astype(F32).astype(BF16)
        true_points = dot(target_parts[...], chosen)
        true_points = true_points[:width_out] + true_points[width_out:]
        for half in range(MASKED_TILE // 128):
            true_rows[half] = true_points[:, half * 128 : half * 128 + 128]
        losses = []
        for half in range(MASKED_TILE // 128):
            terms, grads = chamfer_half(half)
            losses.append(terms)
            for c in range(3):
                pred_rows[half, pl.ds(c, points, stride=3), :] = grads[c]
        grad_turned = jnp.concatenate([pred_rows[half] for half in range(MASKED_TILE // 128)], axis=1)
        grad_turned = jnp.where(masked, grad_turned, 0.0)
        loss = jnp.where(masked, jnp.concatenate(losses, axis=1), 0.0)
        grad_pred = grad_turned.T
        sum_head[...] += dot3(split(grad_turned), normed)
        grad_last = dot3(split(grad_pred), (head_high[...], head_low[...]), 1, 1)
        grad_str = norm_back(grad_last, unit, inverse, row_of(lastnorm_gain))
        sum_reduce[...] += dot3(split(grad_str.T), hidden)
        small[0:1, :128] += fold_lanes(loss)
        small[1:2, :128] += fold_lanes(masked.astype(F32))
        small[5:6, :] += column_sum(grad_last * unit)
        small[6:7, :] += column_sum(grad_last)
        small[7:8, :] += column_sum(grad_str)
        small[8:9, :width_out] += column_sum(grad_pred)
        grad_pre = dot_deep(split(grad_str), reduce_parts[...], 1) * slope
        parts = split(grad_pre)
        sum_expand[...] += dot3(split(normed_mid.T), parts)
        grad_normed = dot_wide(parts, expand_parts[: 2 * width, :], 1)
        grad_mid = grad_str + norm_back(grad_normed, unit_mid, inverse_mid, row_of(midnorm_gain))
        grad_middle[...] = grad_mid
        shift_sum = column_sum(grad_pre)
        for part in range(shift_sum.shape[1] // width):
            small[16 + part : 17 + part, :] += shift_sum[:, part * width : part * width + width]
        small[20:21, :] += column_sum(grad_normed * unit_mid)
        small[21:22, :] += column_sum(grad_normed)
        small[22:23, :] += column_sum(grad_mid)
        parts = split(grad_mid)
        sum_out[...] += dot3(split(attended[...].T), parts)
        grad_attended[...] = dot_deep(parts, out_parts[...], 1)

    @pl.when(index >= used)
    def _():
        grad_attended[...] = jnp.zeros_like(grad_attended)

    @pl.when(index == used - 1)
    def _():
        pack_tiles([sum_reduce, sum_expand, sum_out, sum_head, small], pack, devices)
        for copy in pack_copies:
            copy.start()

    @pl.when(index == pl.num_programs(0) - 1)
    def _():
        for copy in pack_copies:
            copy.wait()


def row_map(index, used):
    return (jnp.minimum(index, used[0] - 1), 0)


def rows_spec(columns):
    return pl.BlockSpec((TILE, columns), row_map)


def whole_spec(array):
    return pl.BlockSpec(array.shape, lambda index, used: (0,) * len(array.shape))


def tile_spec(columns, number, extra=0, tile=TILE):
    def place(index, used):
        return (jnp.minimum(index, used[number] - 1 + extra), 0)

    return pl.BlockSpec((tile, columns), place)


def masked_spec(columns, extra=0):
    return tile_spec(columns, 1, extra, MASKED_TILE)


def lane_spec(number, tile=TILE):
    return pl.BlockSpec((1, tile), lambda index, used: (0, jnp.minimum(index, used[number] - 1)))


def staged_specs(weights, names):
    staged = ("attention_out", "expand_weight", "reduce_weight")
    return [any_spec() if name in staged else whole_spec(weights[name]) for name in names]


def parts_shapes(width, hidden_width):
    return [
        pltpu.VMEM((width, width), F32),
        pltpu.VMEM((width, hidden_width), F32),
        pltpu.VMEM((hidden_width, width), F32),
        pltpu.VMEM((width, 3 * width), BF16),
        pltpu.VMEM((3 * width, hidden_width), BF16),
        pltpu.VMEM((hidden_width, 3 * width), BF16),
    ]


def run_block(used, attended, tokens, owners, targets, weights, devices):
    masked_count, width = tokens.shape
    hidden_width = weights["expand_weight"].shape[1]
    slot_count, width_out = targets.shape
    points = width_out // 3
    names = (
        "attention_out", "attention_shift",
        "midnorm_gain", "midnorm_shift", "expand_weight", "expand_shift", "reduce_weight",
        "reduce_shift", "lastnorm_gain", "lastnorm_shift", "head_turned", "head_shift",
    )
    chunk = block_chunk(width, hidden_width, width_out)
    slots = slots_shape(chunk, devices)
    stats = shape(8, width)
    return pl.pallas_call(
        lambda *refs: block_kernel(devices, *refs),
        out_shape=(
            shape(masked_count, width_out),
            shape(masked_count, width),
            shape(masked_count + MASKED_TILE, width),
            stats,
            shape(*slots),
            shape(*slots),
        ),
        grid_spec=pltpu.PrefetchScalarGridSpec(
            num_scalar_prefetch=1,
            grid=(masked_count // MASKED_TILE + 1,),
            in_specs=[masked_spec(width), masked_spec(width), lane_spec(1, MASKED_TILE), whole_spec(targets)]
            + staged_specs(weights, names),
            out_specs=[
                masked_spec(width_out), masked_spec(width), masked_spec(width, 1), whole_spec(stats),
                any_spec(), any_spec(),
            ],
            scratch_shapes=[pltpu.VMEM(dims, F32) for dims in chunk]
            + [pltpu.VMEM((2,) + slots, F32)]
            + parts_shapes(width, hidden_width)
            + [pltpu.VMEM((width, width_out), BF16)] * 2
            + [pltpu.VMEM((width_out, width), BF16)] * 2
            + [
                pltpu.VMEM((2 * width_out, slot_count), BF16),
                pltpu.VMEM((MASKED_TILE // 128, width_out, 128), F32),
                pltpu.VMEM((MASKED_TILE // 128, width_out, 128), F32),
                pltpu.VMEM((points, points, 128), F32),
                pltpu.VMEM((points, points, 128), F32),
                pltpu.VMEM((points, 128), F32),
                pltpu.VMEM((points, 128), F32),
                pltpu.VMEM((width_out, 1), F32),
                pltpu.SemaphoreType.DMA((2,)),
                pltpu.SemaphoreType.DMA((3,)),
            ],
        ),
        compiler_params=pltpu.CompilerParams(vmem_limit_bytes=48 * 2**20),
        cost_estimate=cost(55),
        name="block",
    )(used, attended, tokens, owners, targets, *[weights[name] for name in names])


def visible_kernel(
    used_ref, attended, tokens, valid, stats_before, attention_out,
    attention_shift, midnorm_gain, midnorm_shift, expand_weight, expand_shift, reduce_weight,
    reduce_shift, lastnorm_gain, lastnorm_shift, head_turned, head_shift,
    predicted, stats,
    out_stage, expand_stage, reduce_stage, out_parts, expand_parts, reduce_parts, head_high, head_low, weight_sems,
):
    index = pl.program_id(0)

    @pl.when(index == 0)
    def _():
        staged = [
            (attention_out, out_stage, out_parts, 1),
            (expand_weight, expand_stage, expand_parts, 0),
            (reduce_weight, reduce_stage, reduce_parts, 1),
        ]
        copies = stage_weights(staged, weight_sems)
        head_high[...], head_low[...] = split(head_turned[...].T)
        stats[...] = stats_before[...]
        split_staged(copies, staged)

    @pl.when(index < used_ref[2])
    def _():
        mixed, middle, _, _, _, branch = block_rows(
            attended, tokens, out_parts, attention_shift, midnorm_gain, midnorm_shift, expand_parts, expand_shift,
            reduce_parts, reduce_shift,
        )
        stream = middle + branch
        unit, _ = norm_parts(stream)
        normed = split(unit * row_of(lastnorm_gain) + row_of(lastnorm_shift))
        predicted[...] = dot3(normed, (head_high[...], head_low[...])) + row_of(head_shift)
        add_squares(stats, lanes_to_rows(valid[...]) > 0.5, stream, mixed, branch)
        stats[3:4, :TILE] += valid[...]


def run_visible(used, attended, tokens, valid, stats, weights):
    visible_count, width = tokens.shape
    hidden_width = weights["expand_weight"].shape[1]
    width_out = weights["head_turned"].shape[0]
    names = (
        "attention_out", "attention_shift",
        "midnorm_gain", "midnorm_shift", "expand_weight", "expand_shift", "reduce_weight",
        "reduce_shift", "lastnorm_gain", "lastnorm_shift", "head_turned", "head_shift",
    )
    return pl.pallas_call(
        visible_kernel,
        out_shape=(shape(visible_count, width_out), shape(8, width)),
        grid_spec=pltpu.PrefetchScalarGridSpec(
            num_scalar_prefetch=1,
            grid=(visible_count // TILE,),
            in_specs=[tile_spec(width, 2), tile_spec(width, 2), lane_spec(2), whole_spec(stats)]
            + staged_specs(weights, names),
            out_specs=[tile_spec(width_out, 2), whole_spec(stats)],
            scratch_shapes=parts_shapes(width, hidden_width)
            + [pltpu.VMEM((width, width_out), BF16)] * 2
            + [pltpu.SemaphoreType.DMA((3,))],
        ),
        compiler_params=pltpu.CompilerParams(vmem_limit_bytes=36 * 2**20),
        cost_estimate=cost(16),
        name="visible",
    )(used, attended, tokens, valid, stats, *[weights[name] for name in names])


def block_chunk(width, hidden_width, width_out):
    return [(width, hidden_width), (width, hidden_width), (width, width), (width_out, width), (24, width)]


def in_chunk(width):
    return [(width, 3 * width), (16, width)]


def attention_back_kernel(
    lens, joint_hbm, grad_hbm, joint_grad_out, joint, grad_rows, joint_grad, in_sems, out_sem,
):
    width = grad_rows.shape[2]
    lane = lax.broadcasted_iota(jnp.int32, (CLOUD_MAX, 128), 1)
    first_head = lane < 64
    key_place = lax.broadcasted_iota(jnp.int32, (CLOUD_MAX, 2 * CLOUD_MAX), 0)
    query_place = lax.broadcasted_iota(jnp.int32, (CLOUD_MAX, 2 * CLOUD_MAX), 1) % CLOUD_MAX
    empty = jnp.zeros((CLOUD_MAX, 128), BF16)

    def both_heads(values):
        return jnp.concatenate(
            [jnp.where(first_head, values, 0.0), jnp.where(first_head, 0.0, values)], axis=0
        )

    def fetch(starts, half):
        copies = []
        for number, (start, masked_start) in enumerate(starts):
            rows = pl.ds(start_of(start), CLOUD_MAX)
            masked_rows = pl.ds(start_of(masked_start), CLOUD_MAX)
            slot = half * BACK_GROUP + number
            copies += [
                pltpu.make_async_copy(joint_hbm.at[rows], joint.at[slot], in_sems.at[0, slot]),
                pltpu.make_async_copy(grad_hbm.at[masked_rows], grad_rows.at[slot], in_sems.at[1, slot]),
            ]
        return copies

    def store(start, slot):
        rows = pl.ds(start_of(start), CLOUD_MAX)
        return pltpu.make_async_copy(joint_grad.at[slot], joint_grad_out.at[rows], out_sem)

    def starts_of(index, start, masked_start):
        starts = []
        for number in range(BACK_GROUP):
            starts.append((start, masked_start))
            length = lens[jnp.minimum(index * BACK_GROUP + number, lens.shape[0] - 1)]
            start = start + spaced(length)
            masked_start = masked_start + spaced(masked_of(length))
        return starts, start, masked_start

    groups = lens.shape[0] // BACK_GROUP
    starts, _, _ = starts_of(0, jnp.int32(0), jnp.int32(0))
    for copy in fetch(starts, 0):
        copy.start()
    work = [(number, pair) for number in range(BACK_GROUP) for pair in range(HEADS // 2)]

    def clouds(index, carry):
        before, start, masked_start = carry
        half = lax.rem(index, 2)
        starts, following, masked_following = starts_of(index, start, masked_start)

        @pl.when(index + 1 < groups)
        def _():
            after, _, _ = starts_of(index + 1, following, masked_following)
            for copy in fetch(after, 1 - half):
                copy.start()

        @pl.when(index > 0)
        def _():
            for number in range(1, BACK_GROUP):
                store(before[number - 1], (1 - half) * BACK_GROUP + number - 1).wait()
                store(before[number], (1 - half) * BACK_GROUP + number).start()

        for copy in fetch(starts, half):
            copy.wait()
        lengths = [lens[index * BACK_GROUP + number] for number in range(BACK_GROUP)]
        insides = [key_place < length for length in lengths]
        lives = [
            jnp.logical_and(inside, query_place < masked_of(length)) for inside, length in zip(insides, lengths)
        ]
        slots = [half * BACK_GROUP + number for number, _ in work]
        at = [
            [slice(part * width + pair * 128, part * width + pair * 128 + 128) for part in range(3)]
            for _, pair in work
        ]
        each = range(len(work))
        query = [split(both_heads(joint[slots[one], :, at[one][0]] * 0.125)) for one in each]
        key = [split(joint[slots[one], :, at[one][1]]) for one in each]
        value = [split(joint[slots[one], :, at[one][2]]) for one in each]
        grad = [split(both_heads(grad_rows[slots[one], :, at[one][0]])) for one in each]
        scores = [dot_pair(key[one], query[one]) for one in each]
        grad_probs = [dot_pair(value[one], grad[one]) for one in each]
        grad_wide = [jnp.concatenate(parts, axis=1) for parts in grad]
        query_wide = [jnp.concatenate(parts, axis=1) for parts in query]
        scores = [jnp.where(insides[number], score, -1e30) for (number, _), score in zip(work, scores)]
        peaks = [jnp.max(score, axis=0, keepdims=True) for score in scores]
        weights = [jnp.exp(score - peak) for score, peak in zip(scores, peaks)]
        scales = [1.0 / column_sum(weight) for weight in weights]
        probs = [
            jnp.where(lives[number], weight * scale, 0.0)
            for (number, _), weight, scale in zip(work, weights, scales)
        ]
        shared = [column_sum(prob * grad_prob) for prob, grad_prob in zip(probs, grad_probs)]
        grad_scores = [probs[one] * (grad_probs[one] - shared[one]) for one in each]
        turned = [grad_score.T for grad_score in grad_scores]
        for one in each:
            joint_grad[slots[one], :, at[one][2]] = dot_wide(split(probs[one]), grad_wide[one])
        for one in each:
            joint_grad[slots[one], :, at[one][1]] = dot_wide(split(grad_scores[one]), query_wide[one])
        for one in each:
            left = jnp.concatenate(split(turned[one]), axis=1)
            right = jnp.concatenate(
                [
                    jnp.concatenate([key[one][0], key[one][1]], axis=1),
                    jnp.concatenate([key[one][0], empty], axis=1),
                ],
                axis=0,
            )
            grad_query = dot(left, right)
            grad_query = (grad_query[:, :128] + grad_query[:, 128:]) * 0.125
            joint_grad[slots[one], :, at[one][0]] = jnp.where(
                first_head, grad_query[:CLOUD_MAX], grad_query[CLOUD_MAX:]
            )

        @pl.when(index > 0)
        def _():
            store(before[BACK_GROUP - 1], (1 - half) * BACK_GROUP + BACK_GROUP - 1).wait()

        store(starts[0][0], half * BACK_GROUP).start()
        return tuple(start for start, _ in starts), following, masked_following

    zero = jnp.int32(0)
    before, _, _ = lax.fori_loop(0, groups, clouds, ((zero,) * BACK_GROUP, zero, zero))
    half = (groups - 1) % 2
    for number in range(BACK_GROUP):
        store(before[number], half * BACK_GROUP + number).wait()
        if number + 1 < BACK_GROUP:
            store(before[number + 1], half * BACK_GROUP + number + 1).start()


def run_attention_back(lens, joint, grad_attended):
    width = grad_attended.shape[1]
    joint_width = joint.shape[1]
    return pl.pallas_call(
        attention_back_kernel,
        out_shape=shape(*joint.shape),
        in_specs=[smem_spec()] + [any_spec()] * 2,
        out_specs=any_spec(),
        scratch_shapes=[
            pltpu.VMEM((2 * BACK_GROUP, CLOUD_MAX, joint_width), F32),
            pltpu.VMEM((2 * BACK_GROUP, CLOUD_MAX, width), F32),
            pltpu.VMEM((2 * BACK_GROUP, CLOUD_MAX, joint_width), F32),
            pltpu.SemaphoreType.DMA((2, 2 * BACK_GROUP)),
            pltpu.SemaphoreType.DMA,
        ],
        compiler_params=pltpu.CompilerParams(vmem_limit_bytes=40 * 2**20),
        cost_estimate=cost(18),
        name="attention_back",
    )(lens, joint, grad_attended)


def in_back_kernel(
    devices, used_ref, lens, grad_joint, tokens, prenorm_gain, prenorm_shift, attention_in, stats,
    keep_out, send_out,
    sum_in, small, joint_sum, pack, pack_sem,
):
    index = pl.program_id(0)
    used = used_ref[0]
    width = tokens.shape[1]
    copies = [
        pltpu.make_async_copy(pack.at[0], keep_out, pack_sem.at[0]),
        pltpu.make_async_copy(pack.at[1], send_out, pack_sem.at[1]),
    ]

    @pl.when(index == 0)
    def _():
        sum_in[...] = jnp.zeros_like(sum_in)
        joint_sum[...] = jnp.zeros_like(joint_sum)

    @pl.when(index < used)
    def _():
        spread, _, _ = cloud_totals(lens)
        live = lax.broadcasted_iota(jnp.int32, (TILE, 1), 0) + index * TILE < spread
        unit, _ = norm_parts(tokens[...])
        grads = jnp.where(live, grad_joint[...], 0.0)
        joint_sum[...] += column_sum(grads)
        sum_in[...] += dot3(split(unit.T), split(grads))

    @pl.when(index == used - 1)
    def _():
        weighted = split(sum_in[...] * attention_in[...])
        ones = jnp.ones((8, joint_sum.shape[1]), BF16)
        small[...] = jnp.zeros_like(small)
        small[8:16, :] = stats[...]
        small[0:1, :] = (dot(ones, weighted[0], 1, 1) + dot(ones, weighted[1], 1, 1))[:1]
        columns = split(jnp.broadcast_to(joint_sum[...], (8, joint_sum.shape[1])))
        small[1:2, :] = dot3(columns, split(attention_in[...]), 1, 1)[:1]
        gains = jnp.broadcast_to(row_of(prenorm_gain), (8, width)).T[:, :1]
        shifts = jnp.broadcast_to(row_of(prenorm_shift), (8, width)).T[:, :1]
        sum_in[...] = sum_in[...] * gains + shifts * joint_sum[...]
        pack_tiles([sum_in, small], pack, devices)
        for copy in copies:
            copy.start()

    @pl.when(index == pl.num_programs(0) - 1)
    def _():
        for copy in copies:
            copy.wait()


def run_in_back(used, lens, grad_joint, tokens, weights, stats, devices):
    spaced_count, width = tokens.shape
    joint_width = grad_joint.shape[1]
    extra = [weights[name] for name in ("prenorm_gain", "prenorm_shift", "attention_in")]
    extra.append(stats)
    chunk = in_chunk(width)
    slots = slots_shape(chunk, devices)
    return pl.pallas_call(
        lambda used, lens, *refs: in_back_kernel(devices, used, lens, *refs),
        out_shape=(shape(*slots), shape(*slots)),
        grid_spec=pltpu.PrefetchScalarGridSpec(
            num_scalar_prefetch=1,
            grid=(spaced_count // TILE,),
            in_specs=[smem_spec(), rows_spec(joint_width), rows_spec(width)]
            + [whole_spec(array) for array in extra],
            out_specs=[any_spec()] * 2,
            scratch_shapes=[pltpu.VMEM(dims, F32) for dims in chunk]
            + [
                pltpu.VMEM((1, joint_width), F32),
                pltpu.VMEM((2,) + slots, F32),
                pltpu.SemaphoreType.DMA((2,)),
            ],
        ),
        compiler_params=pltpu.CompilerParams(vmem_limit_bytes=28 * 2**20),
        cost_estimate=cost(14),
        name="in_back",
    )(used, lens, grad_joint, tokens, *extra)


def input_kernel(
    used_ref, groups, grad_joint, tokens, grad_middle, prenorm_gain, attention_in, spaced_grad, in_parts,
):
    index = pl.program_id(0)

    @pl.when(index == 0)
    def _():
        split_weight(attention_in, in_parts, 0)

    @pl.when(index < used_ref[0])
    def _():
        unit, inverse = norm_parts(tokens[...])
        grad_normed = dot_wide(split(grad_joint[...]), in_parts[: 2 * tokens.shape[1], :], 1)
        spaced_grad[...] = norm_back(grad_normed, unit, inverse, row_of(prenorm_gain))

        def add_group(group, carry):
            source = groups[index * (TILE // 8) + group]
            rows = pl.ds(start_of(group * 8), 8)
            added = grad_middle[pl.ds(start_of(jnp.maximum(source, 0) * 8), 8), :]
            spaced_grad[rows, :] += jnp.where(source >= 0, added, 0.0)
            return carry

        lax.fori_loop(0, TILE // 8, add_group, 0, unroll=8)


def run_input(used, groups, grad_joint, tokens, grad_middle, weights):
    spaced_count, width = tokens.shape
    extra = [weights["prenorm_gain"], weights["attention_in"]]
    return pl.pallas_call(
        input_kernel,
        out_shape=shape(spaced_count, width),
        grid_spec=pltpu.PrefetchScalarGridSpec(
            num_scalar_prefetch=1,
            grid=(spaced_count // TILE,),
            in_specs=[smem_spec(), rows_spec(grad_joint.shape[1]), rows_spec(width), whole_spec(grad_middle)]
            + [whole_spec(array) for array in extra],
            out_specs=rows_spec(width),
            scratch_shapes=[pltpu.VMEM((3 * width, grad_joint.shape[1]), BF16)],
        ),
        compiler_params=pltpu.CompilerParams(vmem_limit_bytes=28 * 2**20),
        cost_estimate=cost(14),
        name="input_grad",
    )(used, groups, grad_joint, tokens, grad_middle, *extra)


def restore_kernel(
    lens, owner, spaced_grad, masked_pred, visible_pred, input_grad, predicted_turned, pred_rows
):
    token_count, width = input_grad.shape
    input_grad[...] = jnp.zeros_like(input_grad)
    pred_rows[...] = jnp.zeros_like(pred_rows)
    windows = cloud_windows(lens, token_count)
    earlier = earlier_table()
    order = lax.broadcasted_iota(jnp.int32, (2 * CLOUD_MAX, CLOUD_MAX), 1)
    places_down = lax.broadcasted_iota(jnp.int32, (CLOUD_MAX, 1), 0)
    for first in range(0, lens.shape[0], 4):
        clouds = range(first, min(first + 4, lens.shape[0]))
        places = [
            cloud_places(
                owner[:, pl.ds(windows[cloud][1], 2 * CLOUD_MAX)],
                windows[cloud][0] - windows[cloud][1], lens[cloud], earlier,
            )
            for cloud in clouds
        ]
        columns = [lanes_to_rows(place.astype(F32)).astype(jnp.int32) for place in places]
        picks = [(order == column).astype(F32).astype(BF16) for column in columns]
        for pick, cloud in zip(picks, clouds):
            _, base, spaced_start, masked_start, visible_start = windows[cloud]
            rows = pl.ds(base, 2 * CLOUD_MAX)
            length, masked = lens[cloud], masked_of(lens[cloud])
            source = spaced_grad[pl.ds(spaced_start, CLOUD_MAX), :]
            high, low = split(jnp.where(places_down < length, source, 0.0))
            input_grad[rows, :] += dot(pick, high) + dot(pick, low)
            source = masked_pred[pl.ds(masked_start, CLOUD_MAX), :]
            shifted = pltpu.roll(
                jnp.concatenate(
                    [visible_pred[pl.ds(visible_start, VISIBLE_MAX), :], jnp.zeros_like(source[VISIBLE_MAX:])], axis=0
                ),
                masked, 0,
            )
            source = jnp.where(places_down < masked, source, shifted)
            high, low = split(jnp.where(places_down < length, source, 0.0))
            pred_rows[rows, :] += dot(pick, high) + dot(pick, low)
    for place in range(0, token_count, 128):
        predicted_turned[:, place : place + 128] = pred_rows[place : place + 128, :].T


def run_restore(lens, owner, spaced_grad, masked_pred, visible_pred):
    token_count = owner.shape[1]
    width, width_out = spaced_grad.shape[1], masked_pred.shape[1]
    return pl.pallas_call(
        restore_kernel,
        out_shape=(shape(token_count, width), shape(width_out, token_count)),
        in_specs=[smem_spec()] + [vmem_spec()] * 4,
        out_specs=[vmem_spec()] * 2,
        scratch_shapes=[pltpu.VMEM((token_count, width_out), F32)],
        compiler_params=pltpu.CompilerParams(vmem_limit_bytes=24 * 2**20),
        cost_estimate=cost(8),
        name="restore",
    )(lens, owner, spaced_grad, masked_pred, visible_pred)


def gather_pack(mine, theirs, pack, sems):
    copies = [
        pltpu.make_async_copy(mine, pack.at[0], sems.at[0]),
        pltpu.make_async_copy(theirs, pack.at[1], sems.at[1]),
    ]
    for copy in copies:
        copy.start()
    for copy in copies:
        copy.wait()


def block_sums_kernel(
    devices, mine, theirs,
    reduce_out, expand_out, attention_out, head_out, lastnorm_gain, lastnorm_shift, reduce_shift, head_shift,
    expand_shift, midnorm_gain, midnorm_shift, attention_shift, loss_out, scale_out,
    sum_reduce, small, pack, sems,
):
    gather_pack(mine, theirs, pack, sems)
    unpack_tiles(pack, [sum_reduce, expand_out, attention_out, head_out, small], devices, None)
    width = small.shape[1]
    scale = 1.0 / jnp.sum(small[1:2, :], axis=1, keepdims=True)
    scale_out[...] = jnp.broadcast_to(scale, scale_out.shape)
    for target in (expand_out, attention_out, head_out):
        target[...] = target[...] * scale
    for row, target in (
        (5, lastnorm_gain), (6, lastnorm_shift), (7, reduce_shift),
        (20, midnorm_gain), (21, midnorm_shift), (22, attention_shift),
    ):
        target[...] = (small[row : row + 1, :] * scale)[0]
    for part in range(expand_shift.shape[0] // width):
        expand_shift[part * width : part * width + width] = (small[16 + part : 17 + part, :] * scale)[0]
    head_shift[...] = (small[8:9, :] * scale)[0, : head_shift.shape[0]]
    loss_out[...] = jnp.broadcast_to(jnp.sum(small[0:1, :], axis=1, keepdims=True) * scale, loss_out.shape)
    for place in range(0, reduce_out.shape[0], 128):
        reduce_out[place : place + 128, :] = sum_reduce[:, place : place + 128].T * scale


def in_sums_kernel(devices, scale, mine, theirs, in_out, prenorm_gain, prenorm_shift, rms_out, small, pack, sems):
    gather_pack(mine, theirs, pack, sems)
    unpack_tiles(pack, [in_out, small], devices, scale[...])
    prenorm_gain[...] = small[0, :]
    prenorm_shift[...] = small[1, :]
    totals = jnp.sum(small[8:16, :], axis=1, keepdims=True)
    rms_out[...] = jnp.broadcast_to(jnp.sqrt(totals / (totals[3:4] * small.shape[1])), rms_out.shape)


def run_sums(kernel, scale, mine, theirs, chunk, outs, keep, devices, name):
    scales = [] if scale is None else [scale]
    return pl.pallas_call(
        lambda *refs: kernel(devices, *refs),
        out_shape=tuple(shape(*dims) for dims in outs),
        in_specs=[vmem_spec()] * len(scales) + [any_spec()] * 2,
        out_specs=[vmem_spec()] * len(outs),
        scratch_shapes=[pltpu.VMEM(dims, F32) for dims in keep]
        + [
            pltpu.VMEM((2,) + slots_shape(chunk, devices), F32),
            pltpu.SemaphoreType.DMA((2,)),
        ],
        compiler_params=pltpu.CompilerParams(vmem_limit_bytes=24 * 2**20),
        cost_estimate=cost(4),
        name=name,
    )(*scales, mine, theirs)


def shards(
    tokens, cloud_lengths, owner_slot, targets, prenorm_gain, prenorm_shift, attention_in,
    attention_out, attention_shift, midnorm_gain, midnorm_shift, expand_weight, expand_shift,
    reduce_weight, reduce_shift, lastnorm_gain, lastnorm_shift, head_weight, head_shift,
):
    token_count, width = tokens.shape
    hidden_width = expand_weight.shape[1]
    devices = lax.axis_size("dp")
    slot_count, width_out = targets.shape
    capacity = slot_count // devices
    arrived = lax.all_to_all(
        targets.reshape(devices, capacity, width_out), "dp", split_axis=0, concat_axis=0, tiled=True
    ).reshape(slot_count, width_out)
    weights = dict(
        prenorm_gain=prenorm_gain, prenorm_shift=prenorm_shift, attention_in=attention_in,
        attention_out=attention_out, attention_shift=attention_shift,
        midnorm_gain=midnorm_gain, midnorm_shift=midnorm_shift,
        expand_weight=expand_weight, expand_shift=expand_shift, reduce_weight=reduce_weight,
        reduce_shift=reduce_shift, lastnorm_gain=lastnorm_gain,
        lastnorm_shift=lastnorm_shift, head_turned=head_weight.T,
        head_shift=head_shift,
    )
    owner = owner_slot[None]
    (
        spaced_tokens, joint, masked_tokens, masked_attended, visible_tokens, visible_attended,
        owners, valid, used, groups,
    ) = run_attend(
        tokens, cloud_lengths, owner, weights["prenorm_gain"], weights["prenorm_shift"], attention_in
    )
    masked_pred, grad_middle, grad_attended, stats, block_keep, block_send = run_block(
        used, masked_attended, masked_tokens, owners, arrived, weights, devices
    )
    block_sum = DeviceSum(block_keep, block_send, devices)
    grad_attended, stats = beside([block_sum], (grad_attended, stats))
    visible_pred, stats = beside(
        [block_sum], run_visible(used, visible_attended, visible_tokens, valid, stats, weights)
    )
    grad_attended, _ = lax.optimization_barrier((grad_attended, stats))
    grad_joint = beside([block_sum], run_attention_back(cloud_lengths, joint, grad_attended))
    in_keep, in_send = beside(
        [block_sum], run_in_back(used, cloud_lengths, grad_joint, spaced_tokens, weights, stats, devices)
    )
    in_sum = DeviceSum(in_keep, in_send, devices)
    sums = [in_sum, block_sum]
    grad_joint = beside([in_sum], grad_joint)
    spaced_grad = beside(sums, run_input(used, groups, grad_joint, spaced_tokens, grad_middle, weights))
    input_grad, predicted_turned = beside(
        sums, run_restore(cloud_lengths, owner, spaced_grad, masked_pred, visible_pred)
    )
    if not block_sum.done():
        block_sum.start()
        beside([in_sum], ())
        in_sum.start()
        moving = lax.optimization_barrier([one.moving for one in sums])
        for one, moved in zip(sums, moving):
            one.moving = moved
            one.finish()
    while not block_sum.done():
        beside(sums, ())
    chunk = block_chunk(width, hidden_width, width_out)
    vector = (width,)
    (
        grad_reduce, grad_expand, grad_out, grad_head_turned, grad_last_gain, grad_last_shift, grad_reduce_shift,
        grad_head_shift, grad_expand_shift, grad_mid_gain, grad_mid_shift, grad_out_shift, loss, scale,
    ) = beside(
        [in_sum],
        run_sums(
            block_sums_kernel, None, block_sum.total, block_sum.theirs, chunk,
            [
                (hidden_width, width), chunk[1], chunk[2], chunk[3], vector, vector, vector,
                (width_out,), (hidden_width,), vector, vector, vector, (8, 128), (8, 128),
            ],
            [chunk[0], chunk[4]], devices, "block_sums",
        ),
    )
    run_out([in_sum])
    chunk = in_chunk(width)
    grad_in, grad_pre_gain, grad_pre_shift, rms = run_sums(
        in_sums_kernel, scale, in_sum.total, in_sum.theirs, chunk,
        [chunk[0], (width,), (width,), (8, 128)], [chunk[1]], devices, "in_sums",
    )
    return (
        loss[0, 0],
        predicted_turned.T,
        input_grad,
        grad_pre_gain,
        grad_pre_shift,
        grad_in,
        grad_out,
        grad_out_shift,
        grad_mid_gain,
        grad_mid_shift,
        grad_expand,
        grad_expand_shift,
        grad_reduce,
        grad_reduce_shift,
        grad_last_gain,
        grad_last_shift,
        grad_head_turned.T,
        grad_head_shift,
        rms[:3, 0],
    )


def solution(mesh):
    row = P("dp", None)
    return jax.shard_map(
        shards,
        mesh=mesh,
        in_specs=(row, P("dp"), P("dp"), row) + (P(),) * 15,
        out_specs=(P(), row, row) + (P(),) * 16,
        check_vma=False,
    )
```

```python
import math

import jax
import jax.numpy as jnp
from jax import lax
from jax.experimental import pallas as pl
from jax.experimental.pallas import tpu as pltpu
from jax.sharding import PartitionSpec as P

HEADS = 6
CLOUD_MAX = 128
TILE = 256
GROUP = 2
BACK_GROUP = 1
JOINT_SLOTS = 3
JOINT_PIECES = 4
MASKED_TILE = 512
VISIBLE_MAX = 64
EPSILON = 1e-05
F32 = jnp.float32
BF16 = jnp.bfloat16
VMEM_BYTES = 60 * 1024 * 1024


def split(values):
    high = values.astype(BF16)
    low = (values - high.astype(F32)).astype(BF16)
    return high, low


def dot(left, right, left_dim=1, right_dim=0):
    return lax.dot_general(
        left, right, (((left_dim,), (right_dim,)), ((), ())), preferred_element_type=F32
    )


def dot3(left, right, left_dim=1, right_dim=0):
    left_high, left_low = left
    right_high, right_low = right
    return dot(left_high, right_high, left_dim, right_dim) + (
        dot(left_high, right_low, left_dim, right_dim)
        + dot(left_low, right_high, left_dim, right_dim)
    )


def dot_deep(left, triple, right_dim=0):
    left_high, left_low = left
    return dot(jnp.concatenate([left_high, left_high, left_low], axis=1), triple, 1, right_dim)


def dot_wide(left, pair, right_dim=0):
    left_high, left_low = left
    columns = pair.shape[1 - right_dim] // 2
    both = dot(left_high, pair, 1, right_dim)
    high = pair[:columns, :] if right_dim else pair[:, :columns]
    return both[:, :columns] + (both[:, columns:] + dot(left_low, high, 1, right_dim))


def dot_pair(left, right):
    right_high, right_low = right
    return dot(jnp.concatenate(left, axis=1), jnp.concatenate([right_high, right_high], axis=1), 1, 1) + dot(
        left[0], right_low, 1, 1
    )


def norm_parts(values):
    average = jnp.mean(values, axis=-1, keepdims=True)
    centred = values - average
    spread = jnp.mean(centred * centred, axis=-1, keepdims=True)
    inverse = lax.rsqrt(spread + EPSILON)
    return centred * inverse, inverse


def norm_back(grad_out, unit_rows, inverse, scale_gain):
    scaled = grad_out * scale_gain
    average_grad = jnp.mean(scaled, axis=-1, keepdims=True)
    project_grad = jnp.mean(scaled * unit_rows, axis=-1, keepdims=True)
    return inverse * (scaled - average_grad - unit_rows * project_grad)


def any_spec():
    return pl.BlockSpec(memory_space=pltpu.HBM)


def vmem_spec():
    return pl.BlockSpec(memory_space=pltpu.VMEM)


def smem_spec():
    return pl.BlockSpec(memory_space=pltpu.SMEM)


def cost(microseconds):
    return pl.CostEstimate(flops=microseconds * 10**9, bytes_accessed=microseconds * 10**6, transcendentals=0)


def shape(*dims):
    return jax.ShapeDtypeStruct(dims, F32)


def row_of(vector):
    return vector[...][None, :]


def column_sum(values):
    return jnp.sum(values, axis=0, keepdims=True)


def split_weight(source, target, axis, step=128):
    rows, columns = source.shape

    def body(index, carry):
        start = pl.multiple_of(index * step, step)
        for part, values in enumerate(split_three(source[pl.ds(start, step), :])):
            if axis == 0:
                target[pl.ds(start + part * rows, step), :] = values
            else:
                target[pl.ds(start, step), part * columns : part * columns + columns] = values
        return carry

    lax.fori_loop(0, rows // step, body, 0)


def split_three(values):
    high, low = split(values)
    return high, low, high


def spaced(length):
    return (length + 7) // 8 * 8


def aligned_rows(token_count, cloud_count):
    return (token_count + 8 * cloud_count + TILE - 1) // TILE * TILE


def masked_of(length):
    return 3 * length // 5


def tiles_of(rows, tile=TILE):
    return (rows + tile - 1) // tile


def compact_rows(token_count, cloud_count):
    return tiles_of(masked_of(token_count) + 8 * cloud_count, MASKED_TILE) * MASKED_TILE


def visible_rows(token_count, cloud_count):
    return tiles_of(token_count - masked_of(token_count) + 9 * cloud_count) * TILE


def cloud_totals(lens):
    spread, masked, visible = jnp.int32(0), jnp.int32(0), jnp.int32(0)
    for cloud in range(lens.shape[0]):
        length = lens[cloud]
        spread = spread + spaced(length)
        masked = masked + spaced(masked_of(length))
        visible = visible + spaced(length - masked_of(length))
    return spread, masked, visible


def cloud_windows(lens, token_count):
    start, spaced_start, masked_start, visible_start = (jnp.int32(0),) * 4
    windows = []
    for cloud in range(lens.shape[0]):
        length = lens[cloud]
        base = jnp.minimum(start // 128, token_count // 128 - 2) * 128
        windows.append(
            (start, pl.multiple_of(base, 128), start_of(spaced_start), start_of(masked_start), start_of(visible_start))
        )
        start = start + length
        spaced_start = spaced_start + spaced(length)
        masked_start = masked_start + spaced(masked_of(length))
        visible_start = visible_start + spaced(length - masked_of(length))
    return windows


def earlier_table():
    rows = lax.broadcasted_iota(jnp.int32, (2 * CLOUD_MAX, 2 * CLOUD_MAX), 0)
    columns = lax.broadcasted_iota(jnp.int32, (2 * CLOUD_MAX, 2 * CLOUD_MAX), 1)
    return (rows < columns).astype(F32).astype(BF16)


def cloud_places(slots, offset, length, earlier):
    lanes = lax.broadcasted_iota(jnp.int32, (1, 2 * CLOUD_MAX), 1)
    inside = jnp.logical_and(lanes >= offset, lanes < offset + length)
    masked = jnp.logical_and(inside, slots >= 0)
    flags = jnp.broadcast_to(masked.astype(F32), (8, 2 * CLOUD_MAX)).astype(BF16)
    rank = dot(flags, earlier)[:1].astype(jnp.int32)
    visible = masked_of(length) + lanes - offset - rank
    return jnp.where(masked, rank, jnp.where(inside, visible, -1))


def start_of(place):
    return pl.multiple_of(place, 8)


def gelu_parts(pre_act):
    cumulative = 0.5 * (1.0 + lax.erf(pre_act * (1.0 / math.sqrt(2.0))))
    density = jnp.exp(-0.5 * pre_act * pre_act) * (1.0 / math.sqrt(2.0 * math.pi))
    return pre_act * cumulative, cumulative + pre_act * density


def slot_place(relative, part, devices):
    x, y, rest = (relative >> 1) & 1, (relative >> 2) & 1, relative >> 3
    major, minor = (x, y) if part == 0 else (y, x)
    return relative & 1, major * (devices // 4) + minor * (devices // 8) + rest


def tile_list(shapes):
    return [
        (which, row, column)
        for which, (rows, columns) in enumerate(shapes)
        for row in range(0, rows, 8)
        for column in range(0, columns, 128)
    ]


def atom_tiles(shapes, devices):
    return -(-len(tile_list(shapes)) // (2 * devices))


def slots_shape(shapes, devices):
    return (2, devices // 2, atom_tiles(shapes, devices) * 8, 128)


def pack_tiles(sources, keep, send, devices):
    me = lax.axis_index("dp")
    tiles = tile_list([source.shape for source in sources])
    each = atom_tiles([source.shape for source in sources], devices)
    for atom in range(-(-len(tiles) // each)):
        part, owner = atom // devices, atom % devices
        bit, place = slot_place(me ^ owner, part, devices)

        def copy(target, atom=atom, part=part, place=place):
            for number, (which, row, column) in enumerate(tiles[atom * each : atom * each + each]):
                target[part, place, number * 8 : number * 8 + 8, :] = sources[which][
                    row : row + 8, column : column + 128
                ]

        pl.when(bit == 0)(lambda copy=copy: copy(keep))
        pl.when(bit == 1)(lambda copy=copy: copy(send))


def unpack_tiles(pack, targets, devices, scale):
    me = lax.axis_index("dp")
    tiles = tile_list([target.shape for target in targets])
    each = atom_tiles([target.shape for target in targets], devices)
    for atom in range(-(-len(tiles) // each)):
        part, owner = atom // devices, atom % devices
        bit, place = slot_place(me ^ owner, part, devices)
        for number, (which, row, column) in enumerate(tiles[atom * each : atom * each + each]):
            piece = pack[bit, part, place, number * 8 : number * 8 + 8, :]
            targets[which][row : row + 8, column : column + 128] = (
                piece if scale is None else piece * scale
            )


def swap(values, bits, devices):
    return lax.ppermute(values, "dp", [(device, device ^ bits) for device in range(devices)])


def rest_groups(devices):
    count = (devices // 8).bit_length() - 1
    groups = []
    while count:
        step = 2 if count >= 2 else 1
        count -= step
        groups.append((3 + count, 1 << step))
    return groups


class DeviceSum:
    def __init__(self, keep, send, devices):
        self.devices = devices
        self.groups = rest_groups(devices)
        self.keep, self.send = keep, send
        self.stage = 0
        self.last = 5 + 2 * len(self.groups)

    def start(self):
        devices, stage, count = self.devices, self.stage, len(self.groups)
        if stage == 0:
            self.moving = [swap(self.send, 1, devices)]
        elif stage <= 2:
            size = devices // (4, 8)[stage - 1]
            bits = ((2, 4), (4, 2))[stage - 1]
            self.moving = [swap(half[size:], bit, devices) for half, bit in zip(self.halves, bits)]
            self.halves = [half[:size] for half in self.halves]
        elif stage < 3 + count:
            shift, size = self.groups[stage - 3]
            total = self.total.reshape((size, -1) + self.total.shape[1:])
            self.moving = [swap(total[slot], slot << shift, devices) for slot in range(1, size)]
            self.total = total[0]
        elif stage < 3 + 2 * count:
            shift, size = self.groups[3 + 2 * count - 1 - stage]
            self.moving = [swap(self.total, slot << shift, devices) for slot in range(1, size)]
        elif stage < 5 + 2 * count:
            bits = ((4, 2), (2, 4))[stage - 3 - 2 * count]
            self.moving = [swap(half, bit, devices) for half, bit in zip(self.halves, bits)]
        else:
            self.moving = [swap(self.total, 1, devices)]

    def finish(self):
        stage, count = self.stage, len(self.groups)
        if stage == 0:
            total = self.keep + self.moving[0]
            self.halves = [total[0], total[1]]
        elif stage <= 2:
            self.halves = [half + moved for half, moved in zip(self.halves, self.moving)]
            if stage == 2:
                self.total = jnp.stack(self.halves, axis=1)
        elif stage < 3 + count:
            self.total = sum(self.moving, self.total)
        elif stage < 3 + 2 * count:
            self.total = jnp.concatenate([self.total] + self.moving, axis=0)
            if stage == 2 + 2 * count:
                self.halves = [self.total[:, 0], self.total[:, 1]]
        elif stage < 5 + 2 * count:
            self.halves = [jnp.concatenate([half, moved]) for half, moved in zip(self.halves, self.moving)]
            if stage == 4 + 2 * count:
                self.total = jnp.stack(self.halves)
        else:
            self.theirs = self.moving[0]
        self.stage += 1

    def done(self):
        return self.stage > self.last

    def state(self):
        if hasattr(self, "total") and (3 <= self.stage < 3 + 2 * len(self.groups) or self.stage >= self.last):
            return self.total
        return self.halves

    def set_state(self, state):
        if hasattr(self, "total") and (3 <= self.stage < 3 + 2 * len(self.groups) or self.stage >= self.last):
            self.total = state
        else:
            self.halves = state


def beside(sums, outs):
    sums = [one for one in sums if not one.done()]
    for one in sums:
        one.start()
    moving, outs = lax.optimization_barrier(([one.moving for one in sums], outs))
    for one, moved in zip(sums, moving):
        one.moving = moved
        one.finish()
    going = [one for one in sums if not one.done()]
    states, outs = lax.optimization_barrier(([one.state() for one in going], outs))
    for one, state in zip(going, states):
        one.set_state(state)
    return outs


def run_stage(one):
    one.start()
    one.finish()


def run_out(sums):
    while not all(one.done() for one in sums):
        for one in sums:
            if not one.done():
                run_stage(one)


def attend_kernel(
    lens, tokens_hbm, owner, prenorm_gain, prenorm_shift, attention_in,
    tokens_out, joint_out, masked_tokens_out, masked_attended_out, visible_tokens_out, visible_attended_out,
    owners, valid, used_out, groups_out,
    raw, tokens, joint, masked_tokens, masked_attended, visible_tokens, visible_attended, in_parts,
    token_sem, joint_sem, out_sems,
):
    token_count = owner.shape[1]
    tiles = tokens.shape[0] // TILE
    width = tokens.shape[1]
    spread, masked_total, visible_total = cloud_totals(lens)
    used, visible_used = tiles_of(spread), tiles_of(visible_total)
    masked_used = tiles_of(masked_total, MASKED_TILE)
    used_out[0] = used
    used_out[1] = masked_used
    used_out[2] = visible_used

    def tile_rows(index, tile=TILE):
        return pl.ds(pl.multiple_of(index * tile, tile), tile)

    token_copy = pltpu.make_async_copy(tokens_hbm, raw, token_sem)
    token_copy.start()
    split_weight(attention_in, in_parts, 0)
    owners[...] = jnp.full(owners.shape, -1, jnp.int32)
    valid[...] = jnp.zeros(valid.shape, F32)
    blank = jnp.zeros((TILE, width), F32)
    tokens[tile_rows(used - 1), :] = blank
    for kept in (masked_tokens, masked_attended):
        kept[tile_rows(masked_used - 1, MASKED_TILE), :] = jnp.zeros((MASKED_TILE, width), F32)
    for kept in (visible_tokens, visible_attended):
        kept[tile_rows(visible_used - 1), :] = blank

    def no_group(index, carry):
        groups_out[index] = -1
        return carry

    lax.fori_loop(0, groups_out.shape[0], no_group, 0, unroll=8)

    def cloud_groups(cloud, carry):
        spaced_group, masked_group = carry
        count = spaced(masked_of(lens[cloud])) // 8

        def group(index, carry):
            groups_out[spaced_group + index] = masked_group + index
            return carry

        lax.fori_loop(0, count, group, 0)
        return spaced_group + spaced(lens[cloud]) // 8, masked_group + count

    lax.fori_loop(0, lens.shape[0], cloud_groups, (jnp.int32(0), jnp.int32(0)))
    windows = cloud_windows(lens, token_count)
    earlier = earlier_table()
    wide = lax.broadcasted_iota(jnp.int32, (1, 2 * CLOUD_MAX), 1)
    order = lax.broadcasted_iota(jnp.int32, (CLOUD_MAX + VISIBLE_MAX, 2 * CLOUD_MAX), 0)
    token_copy.wait()
    for first in range(0, lens.shape[0], 4):
        clouds = range(first, min(first + 4, lens.shape[0]))
        slots = [owner[:, pl.ds(windows[cloud][1], 2 * CLOUD_MAX)] for cloud in clouds]
        places = [
            cloud_places(slot, windows[cloud][0] - windows[cloud][1], lens[cloud], earlier)
            for slot, cloud in zip(slots, clouds)
        ]
        rows_of = [
            jnp.where(order < CLOUD_MAX, order, order - CLOUD_MAX + masked_of(lens[cloud])) for cloud in clouds
        ]
        picks = [(row == place).astype(F32).astype(BF16) for row, place in zip(rows_of, places)]
        for pick, slot, cloud in zip(picks, slots, clouds):
            _, base, spaced_start, masked_start, visible_start = windows[cloud]
            rows = raw[pl.ds(base, 2 * CLOUD_MAX), :]
            high = rows.astype(BF16)
            rest = rows - high.astype(F32)
            mid, low = split(rest)
            moved = (dot(pick, high) + dot(pick, mid)) + dot(pick, low)
            tokens[pl.ds(spaced_start, CLOUD_MAX), :] = moved[:CLOUD_MAX]
            masked_tokens[pl.ds(masked_start, CLOUD_MAX), :] = moved[:CLOUD_MAX]
            visible_tokens[pl.ds(visible_start, VISIBLE_MAX), :] = moved[CLOUD_MAX:]
            parts = jnp.concatenate(
                [(slot >> 6).astype(F32), (slot & 63).astype(F32), jnp.zeros((6, 2 * CLOUD_MAX), F32)], axis=0
            )
            parts = dot(parts.astype(BF16), pick[:CLOUD_MAX], 1, 1)
            moved = (parts[0:1] * 64.0 + parts[1:2]).astype(jnp.int32)
            moved = jnp.concatenate([moved, jnp.zeros((1, CLOUD_MAX), jnp.int32)], axis=1)
            masked, visible = masked_of(lens[cloud]), lens[cloud] - masked_of(lens[cloud])
            offset = masked_start % 128
            lanes = pl.ds(pl.multiple_of(masked_start // 128 * 128, 128), 2 * CLOUD_MAX)
            inside = jnp.logical_and(wide >= offset, wide < offset + masked)
            owners[:, lanes] = jnp.where(inside, pltpu.roll(moved, offset, 1), owners[:, lanes])
            offset = visible_start % 128
            lanes = pl.ds(pl.multiple_of(visible_start // 128 * 128, 128), 2 * CLOUD_MAX)
            inside = jnp.logical_and(wide >= offset, wide < offset + visible)
            valid[:, lanes] = jnp.where(inside, 1.0, valid[:, lanes])

    def joint_copies(index):
        rows = tile_rows(index)
        return [
            pltpu.make_async_copy(joint.at[rows], joint_out.at[rows], joint_sem.at[index]),
            pltpu.make_async_copy(tokens.at[rows], tokens_out.at[rows], out_sems.at[0, index]),
        ]

    def joint_tile(index, carry):
        rows = tile_rows(index)
        unit, _ = norm_parts(tokens[rows, :])
        normed = split(unit * row_of(prenorm_gain) + row_of(prenorm_shift))
        joint[rows, :] = dot_deep(normed, in_parts[...])
        for copy in joint_copies(index):
            copy.start()
        return carry

    lax.fori_loop(0, used, joint_tile, 0)
    tail = pl.ds(pl.multiple_of(used * TILE, TILE), CLOUD_MAX)
    joint[tail, :] = jnp.zeros((CLOUD_MAX, joint.shape[1]), F32)
    tail_copy = pltpu.make_async_copy(joint.at[tail], joint_out.at[tail], joint_sem.at[tiles])
    tail_copy.start()

    lane = lax.broadcasted_iota(jnp.int32, (CLOUD_MAX, 128), 1)
    first_head = lane < 64
    wide_lane = lax.broadcasted_iota(jnp.int32, (CLOUD_MAX, CLOUD_MAX), 1)
    empty = jnp.zeros((CLOUD_MAX, 128), BF16)

    visible_order = lax.broadcasted_iota(jnp.int32, (VISIBLE_MAX, CLOUD_MAX), 0)
    visible_column = lax.broadcasted_iota(jnp.int32, (VISIBLE_MAX, CLOUD_MAX), 1)

    def clouds(index, carry):
        start, masked_start, visible_start = carry
        lengths = [lens[GROUP * index + number] for number in range(GROUP)]
        places, masked_places, visible_places = [], [], []
        for length in lengths:
            places.append(pl.ds(start_of(start), CLOUD_MAX))
            masked_places.append(pl.ds(start_of(masked_start), CLOUD_MAX))
            visible_places.append(pl.ds(start_of(visible_start), VISIBLE_MAX))
            start = start + spaced(length)
            masked_start = masked_start + spaced(masked_of(length))
            visible_start = visible_start + spaced(length - masked_of(length))
        picks = [
            jnp.logical_and(visible_column == visible_order + masked_of(length), visible_column < length)
            .astype(F32)
            .astype(BF16)
            for length in lengths
        ]
        insides = [wide_lane < length for length in lengths]
        work = [(number, pair) for number in range(GROUP) for pair in range(HEADS // 2)]
        lefts, rights = [], []
        for number, pair in work:
            rows = places[number]
            query = joint[rows, pair * 128 : pair * 128 + 128] * 0.125
            key_high, key_low = split(joint[rows, width + pair * 128 : width + pair * 128 + 128])
            both = jnp.concatenate(
                [jnp.where(first_head, query, 0.0), jnp.where(first_head, 0.0, query)], axis=0
            )
            lefts.append(jnp.concatenate(split(both), axis=1))
            rights.append(
                jnp.concatenate(
                    [
                        jnp.concatenate([key_high, key_high], axis=1),
                        jnp.concatenate([key_low, empty], axis=1),
                    ],
                    axis=0,
                )
            )
        scores = [dot(left, right, 1, 1) for left, right in zip(lefts, rights)]
        lefts = []
        for (number, _), score in zip(work, scores):
            parts = []
            for half in range(2):
                rows = slice(half * CLOUD_MAX, half * CLOUD_MAX + CLOUD_MAX)
                head = jnp.where(insides[number], score[rows, :128] + score[rows, 128:], -1e30)
                weight = jnp.exp(head - jnp.max(head, axis=-1, keepdims=True))
                prob = weight * (1.0 / jnp.sum(weight, axis=-1, keepdims=True))
                parts.append(jnp.concatenate(split(prob), axis=1))
            lefts.append(jnp.concatenate(parts, axis=0))
        rights = []
        for number, pair in work:
            value_high, value_low = split(
                joint[places[number], 2 * width + pair * 128 : 2 * width + pair * 128 + 128]
            )
            rights.append(
                jnp.concatenate(
                    [
                        jnp.concatenate([value_high, value_low], axis=1),
                        jnp.concatenate([value_high, empty], axis=1),
                    ],
                    axis=0,
                )
            )
        mixed = [dot(left, right) for left, right in zip(lefts, rights)]
        for (number, pair), both in zip(work, mixed):
            both = both[:, :128] + both[:, 128:]
            both = jnp.where(first_head, both[:CLOUD_MAX], both[CLOUD_MAX:])
            columns = slice(pair * 128, pair * 128 + 128)
            masked_attended[masked_places[number], columns] = both
            moved = dot(picks[number], jnp.concatenate(split(both), axis=1))
            visible_attended[visible_places[number], columns] = moved[:, :128] + moved[:, 128:]
        return start, masked_start, visible_start

    zero = jnp.int32(0)
    lax.fori_loop(0, lens.shape[0] // GROUP, clouds, (zero, zero, zero))

    def masked_copies(index):
        rows = tile_rows(index, MASKED_TILE)
        return [
            pltpu.make_async_copy(masked_tokens.at[rows], masked_tokens_out.at[rows], out_sems.at[1, index]),
            pltpu.make_async_copy(masked_attended.at[rows], masked_attended_out.at[rows], out_sems.at[2, index]),
        ]

    def visible_copies(index):
        rows = tile_rows(index)
        return [
            pltpu.make_async_copy(visible_tokens.at[rows], visible_tokens_out.at[rows], out_sems.at[3, index]),
            pltpu.make_async_copy(visible_attended.at[rows], visible_attended_out.at[rows], out_sems.at[4, index]),
        ]

    def begin(copies_of):
        def body(index, carry):
            for copy in copies_of(index):
                copy.start()
            return carry

        return body

    def finish(copies_of):
        def body(index, carry):
            for copy in copies_of(index):
                copy.wait()
            return carry

        return body

    lax.fori_loop(0, masked_used, begin(masked_copies), 0)
    lax.fori_loop(0, visible_used, begin(visible_copies), 0)
    tail_copy.wait()
    lax.fori_loop(0, used, finish(joint_copies), 0)
    lax.fori_loop(0, masked_used, finish(masked_copies), 0)
    lax.fori_loop(0, visible_used, finish(visible_copies), 0)


def run_attend(tokens, lens, owner, prenorm_gain, prenorm_shift, attention_in):
    token_count, width = tokens.shape
    joint_width = attention_in.shape[1]
    spaced_count = aligned_rows(token_count, lens.shape[0])
    masked_count = compact_rows(token_count, lens.shape[0])
    visible_count = visible_rows(token_count, lens.shape[0])
    tiles = spaced_count // TILE
    return pl.pallas_call(
        attend_kernel,
        out_shape=(
            shape(spaced_count, width),
            shape(spaced_count + CLOUD_MAX, joint_width),
            shape(masked_count, width),
            shape(masked_count, width),
            shape(visible_count, width),
            shape(visible_count, width),
            jax.ShapeDtypeStruct((1, masked_count + 256), jnp.int32),
            shape(1, visible_count + 256),
            jax.ShapeDtypeStruct((3,), jnp.int32),
            jax.ShapeDtypeStruct((spaced_count // 8,), jnp.int32),
        ),
        in_specs=[smem_spec(), any_spec()] + [vmem_spec()] * 4,
        out_specs=[any_spec()] * 6 + [vmem_spec()] * 2 + [smem_spec()] * 2,
        scratch_shapes=[
            pltpu.VMEM((token_count, width), F32),
            pltpu.VMEM((spaced_count, width), F32),
            pltpu.VMEM((spaced_count + CLOUD_MAX, joint_width), F32),
            pltpu.VMEM((masked_count + CLOUD_MAX, width), F32),
            pltpu.VMEM((masked_count + CLOUD_MAX, width), F32),
            pltpu.VMEM((visible_count + VISIBLE_MAX, width), F32),
            pltpu.VMEM((visible_count + VISIBLE_MAX, width), F32),
            pltpu.VMEM((3 * width, joint_width), BF16),
            pltpu.SemaphoreType.DMA,
            pltpu.SemaphoreType.DMA((tiles + 1,)),
            pltpu.SemaphoreType.DMA((5, tiles)),
        ],
        compiler_params=pltpu.CompilerParams(vmem_limit_bytes=48 * 2**20),
        cost_estimate=cost(26),
        name="attend",
    )(lens, tokens, owner, prenorm_gain, prenorm_shift, attention_in)


def stage_weights(staged, sems):
    copies = [
        pltpu.make_async_copy(weight, place, sems.at[number])
        for number, (weight, place, _, _) in enumerate(staged)
    ]
    for copy in copies:
        copy.start()
    return copies


def split_staged(copies, staged):
    for copy, (_, place, parts, axis) in zip(copies, staged):
        copy.wait()
        split_weight(place, parts, axis)


def block_rows(
    attended, tokens, out_parts, attention_shift, midnorm_gain, midnorm_shift, expand_parts, expand_shift,
    reduce_parts, reduce_shift,
):
    width = tokens.shape[1]
    mixed = dot_wide(split(attended[...]), out_parts[:, : 2 * width]) + row_of(attention_shift)
    middle = tokens[...] + mixed
    unit, inverse = norm_parts(middle)
    normed = unit * row_of(midnorm_gain) + row_of(midnorm_shift)
    pre_act = dot_deep(split(normed), expand_parts[...]) + row_of(expand_shift)
    hidden, slope = gelu_parts(pre_act)
    hidden = split(hidden)
    branch = dot_wide(hidden, reduce_parts[:, : 2 * width]) + row_of(reduce_shift)
    return mixed, middle, (unit, inverse, normed), hidden, slope, branch


def fold_lanes(lanes):
    return sum(lanes[:, place : place + 128] for place in range(0, lanes.shape[1], 128))


def lanes_to_rows(lanes):
    return jnp.broadcast_to(lanes, (8, lanes.shape[1])).T[:, :1]


def add_squares(stats, live, stream, mixed, branch):
    for row, values in enumerate((stream, mixed, branch)):
        stats[row : row + 1, :] += column_sum(jnp.where(live, values * values, 0.0))


def block_kernel(
    devices, used_ref, attended, tokens, owners, targets, attention_out,
    attention_shift, midnorm_gain, midnorm_shift, expand_weight, expand_shift, reduce_weight,
    reduce_shift, lastnorm_gain, lastnorm_shift, head_turned, head_shift,
    predicted, grad_middle, grad_attended, stats, keep, send,
    sum_reduce, sum_expand, sum_out, sum_head, small,
    out_stage, expand_stage, reduce_stage, out_parts, expand_parts, reduce_parts,
    head_high, head_low, turned_high, turned_low, target_parts, pred_rows, true_rows, distance, second,
    col_low, col_sum, shift_column, weight_sems,
):
    index = pl.program_id(0)
    used = used_ref[1]
    slot_count, width_out = targets.shape
    points = width_out // 3
    width = tokens.shape[1]

    @pl.when(index == 0)
    def _():
        staged = [
            (attention_out, out_stage, out_parts, 1),
            (expand_weight, expand_stage, expand_parts, 0),
            (reduce_weight, reduce_stage, reduce_parts, 1),
        ]
        copies = stage_weights(staged, weight_sems)
        shift_column[...] = lanes_to_rows(row_of(head_shift))
        turned_high[...], turned_low[...] = split(head_turned[...])
        head_high[...], head_low[...] = split(head_turned[...].T)
        high, low = split(targets[...].T)
        target_parts[:width_out, :] = high
        target_parts[width_out:, :] = low
        for total in (small, stats, sum_reduce, sum_head, sum_expand, sum_out):
            total[...] = jnp.zeros_like(total)
        split_staged(copies, staged)

    def chamfer_half(half):
        xs = [pred_rows[half, pl.ds(c, points, stride=3), :] for c in range(3)]

        def first(j, row_low):
            gap = [xs[c] - true_rows[half, pl.ds(3 * j + c, 1), :] for c in range(3)]
            apart = gap[0] * gap[0] + gap[1] * gap[1] + gap[2] * gap[2]
            distance[j] = apart
            lowest = jnp.min(apart, axis=0, keepdims=True)
            weight = jnp.exp(lowest - apart)
            inside = column_sum(weight)
            col_low[pl.ds(j, 1), :] = lowest
            col_sum[pl.ds(j, 1), :] = inside
            second[j] = weight * (1.0 / (points * inside))
            return jnp.minimum(row_low, apart)

        row_low = lax.fori_loop(
            0, points, first, jnp.full((points, 128), jnp.inf, F32), unroll=8
        )

        def middle_pass(j, row_sum):
            weight = jnp.exp(row_low - distance[j])
            distance[j] = weight
            return row_sum + weight

        row_sum = lax.fori_loop(0, points, middle_pass, jnp.zeros((points, 128), F32), unroll=8)
        row_scale = 1.0 / (points * row_sum)

        def last(j, carry):
            weight = second[j] + distance[j] * row_scale
            return (carry[0] + weight,) + tuple(
                carry[1 + c] + weight * true_rows[half, pl.ds(3 * j + c, 1), :] for c in range(3)
            )

        zero = jnp.zeros((points, 128), F32)
        sums = lax.fori_loop(0, points, last, (zero,) * 4, unroll=8)
        terms = column_sum(row_low - jnp.log(row_sum * (1.0 / points))) + column_sum(
            col_low[...] - jnp.log(col_sum[...] * (1.0 / points))
        )
        grads = [2.0 * (sums[0] * xs[c] - sums[1 + c]) for c in range(3)]
        return terms * (1.0 / points), grads

    @pl.when(index < used)
    def _():
        mixed, middle, (unit_mid, inverse_mid, normed_mid), hidden, slope, branch = block_rows(
            attended, tokens, out_parts, attention_shift, midnorm_gain, midnorm_shift, expand_parts, expand_shift,
            reduce_parts, reduce_shift,
        )
        stream = middle + branch
        unit, inverse = norm_parts(stream)
        normed = split(unit * row_of(lastnorm_gain) + row_of(lastnorm_shift))
        pred = dot3((turned_high[...], turned_low[...]), normed, 1, 1) + shift_column[...]
        predicted[...] = pred.T
        slots = lax.broadcasted_iota(jnp.int32, (slot_count, MASKED_TILE), 0)
        slot_row = owners[...]
        masked = slot_row >= 0
        add_squares(stats, lanes_to_rows(masked.astype(F32)) > 0.5, stream, mixed, branch)
        stats[3:4, :128] += fold_lanes(masked.astype(F32))
        for half in range(MASKED_TILE // 128):
            pred_rows[half] = pred[:, half * 128 : half * 128 + 128]
        chosen = (slots == slot_row).astype(F32).astype(BF16)
        true_points = dot(target_parts[...], chosen)
        true_points = true_points[:width_out] + true_points[width_out:]
        for half in range(MASKED_TILE // 128):
            true_rows[half] = true_points[:, half * 128 : half * 128 + 128]
        losses = []
        for half in range(MASKED_TILE // 128):
            terms, grads = chamfer_half(half)
            losses.append(terms)
            for c in range(3):
                pred_rows[half, pl.ds(c, points, stride=3), :] = grads[c]
        grad_turned = jnp.concatenate([pred_rows[half] for half in range(MASKED_TILE // 128)], axis=1)
        grad_turned = jnp.where(masked, grad_turned, 0.0)
        loss = jnp.where(masked, jnp.concatenate(losses, axis=1), 0.0)
        grad_pred = grad_turned.T
        sum_head[...] += dot3(split(grad_turned), normed)
        grad_last = dot3(split(grad_pred), (head_high[...], head_low[...]), 1, 1)
        grad_str = norm_back(grad_last, unit, inverse, row_of(lastnorm_gain))
        sum_reduce[...] += dot3(split(grad_str.T), hidden)
        small[0:1, :128] += fold_lanes(loss)
        small[1:2, :128] += fold_lanes(masked.astype(F32))
        small[5:6, :] += column_sum(grad_last * unit)
        small[6:7, :] += column_sum(grad_last)
        small[7:8, :] += column_sum(grad_str)
        small[8:9, :width_out] += column_sum(grad_pred)
        grad_pre = dot_deep(split(grad_str), reduce_parts[...], 1) * slope
        parts = split(grad_pre)
        sum_expand[...] += dot3(split(normed_mid.T), parts)
        grad_normed = dot_wide(parts, expand_parts[: 2 * width, :], 1)
        grad_mid = grad_str + norm_back(grad_normed, unit_mid, inverse_mid, row_of(midnorm_gain))
        grad_middle[...] = grad_mid
        shift_sum = column_sum(grad_pre)
        for part in range(shift_sum.shape[1] // width):
            small[16 + part : 17 + part, :] += shift_sum[:, part * width : part * width + width]
        small[20:21, :] += column_sum(grad_normed * unit_mid)
        small[21:22, :] += column_sum(grad_normed)
        small[22:23, :] += column_sum(grad_mid)
        parts = split(grad_mid)
        sum_out[...] += dot3(split(attended[...].T), parts)
        grad_attended[...] = dot_deep(parts, out_parts[...], 1)

    @pl.when(index >= used)
    def _():
        grad_attended[...] = jnp.zeros_like(grad_attended)

    @pl.when(index == used - 1)
    def _():
        pack_tiles([sum_reduce, sum_expand, sum_out, sum_head, small], keep, send, devices)


def row_map(index, used):
    return (jnp.minimum(index, used[0] - 1), 0)


def rows_spec(columns):
    return pl.BlockSpec((TILE, columns), row_map)


def whole_spec(array):
    return pl.BlockSpec(array.shape, lambda index, used: (0,) * len(array.shape))


def tile_spec(columns, number, extra=0, tile=TILE):
    def place(index, used):
        return (jnp.minimum(index, used[number] - 1 + extra), 0)

    return pl.BlockSpec((tile, columns), place)


def masked_spec(columns, extra=0):
    return tile_spec(columns, 1, extra, MASKED_TILE)


def lane_spec(number, tile=TILE):
    return pl.BlockSpec((1, tile), lambda index, used: (0, jnp.minimum(index, used[number] - 1)))


def staged_specs(weights, names):
    staged = ("attention_out", "expand_weight", "reduce_weight")
    return [any_spec() if name in staged else whole_spec(weights[name]) for name in names]


def parts_shapes(width, hidden_width):
    return [
        pltpu.VMEM((width, width), F32),
        pltpu.VMEM((width, hidden_width), F32),
        pltpu.VMEM((hidden_width, width), F32),
        pltpu.VMEM((width, 3 * width), BF16),
        pltpu.VMEM((3 * width, hidden_width), BF16),
        pltpu.VMEM((hidden_width, 3 * width), BF16),
    ]


def run_block(used, attended, tokens, owners, targets, weights, devices):
    masked_count, width = tokens.shape
    hidden_width = weights["expand_weight"].shape[1]
    slot_count, width_out = targets.shape
    points = width_out // 3
    names = (
        "attention_out", "attention_shift",
        "midnorm_gain", "midnorm_shift", "expand_weight", "expand_shift", "reduce_weight",
        "reduce_shift", "lastnorm_gain", "lastnorm_shift", "head_turned", "head_shift",
    )
    chunk = block_chunk(width, hidden_width, width_out)
    slots = slots_shape(chunk, devices)
    stats = shape(8, width)
    return pl.pallas_call(
        lambda *refs: block_kernel(devices, *refs),
        out_shape=(
            shape(masked_count, width_out),
            shape(masked_count, width),
            shape(masked_count + MASKED_TILE, width),
            stats,
            shape(*slots),
            shape(*slots),
        ),
        grid_spec=pltpu.PrefetchScalarGridSpec(
            num_scalar_prefetch=1,
            grid=(masked_count // MASKED_TILE + 1,),
            in_specs=[masked_spec(width), masked_spec(width), lane_spec(1, MASKED_TILE), whole_spec(targets)]
            + staged_specs(weights, names),
            out_specs=[
                masked_spec(width_out), masked_spec(width), masked_spec(width, 1), whole_spec(stats),
                vmem_spec(), vmem_spec(),
            ],
            scratch_shapes=[pltpu.VMEM(dims, F32) for dims in chunk]
            + parts_shapes(width, hidden_width)
            + [pltpu.VMEM((width, width_out), BF16)] * 2
            + [pltpu.VMEM((width_out, width), BF16)] * 2
            + [
                pltpu.VMEM((2 * width_out, slot_count), BF16),
                pltpu.VMEM((MASKED_TILE // 128, width_out, 128), F32),
                pltpu.VMEM((MASKED_TILE // 128, width_out, 128), F32),
                pltpu.VMEM((points, points, 128), F32),
                pltpu.VMEM((points, points, 128), F32),
                pltpu.VMEM((points, 128), F32),
                pltpu.VMEM((points, 128), F32),
                pltpu.VMEM((width_out, 1), F32),
                pltpu.SemaphoreType.DMA((3,)),
            ],
        ),
        compiler_params=pltpu.CompilerParams(vmem_limit_bytes=48 * 2**20),
        cost_estimate=cost(55),
        name="block",
    )(used, attended, tokens, owners, targets, *[weights[name] for name in names])


def visible_kernel(
    used_ref, attended, tokens, valid, stats_before, attention_out,
    attention_shift, midnorm_gain, midnorm_shift, expand_weight, expand_shift, reduce_weight,
    reduce_shift, lastnorm_gain, lastnorm_shift, head_turned, head_shift,
    predicted, stats,
    out_stage, expand_stage, reduce_stage, out_parts, expand_parts, reduce_parts, head_high, head_low, weight_sems,
):
    index = pl.program_id(0)

    @pl.when(index == 0)
    def _():
        staged = [
            (attention_out, out_stage, out_parts, 1),
            (expand_weight, expand_stage, expand_parts, 0),
            (reduce_weight, reduce_stage, reduce_parts, 1),
        ]
        copies = stage_weights(staged, weight_sems)
        head_high[...], head_low[...] = split(head_turned[...].T)
        stats[...] = stats_before[...]
        split_staged(copies, staged)

    @pl.when(index < used_ref[2])
    def _():
        mixed, middle, _, _, _, branch = block_rows(
            attended, tokens, out_parts, attention_shift, midnorm_gain, midnorm_shift, expand_parts, expand_shift,
            reduce_parts, reduce_shift,
        )
        stream = middle + branch
        unit, _ = norm_parts(stream)
        normed = split(unit * row_of(lastnorm_gain) + row_of(lastnorm_shift))
        predicted[...] = dot3(normed, (head_high[...], head_low[...])) + row_of(head_shift)
        add_squares(stats, lanes_to_rows(valid[...]) > 0.5, stream, mixed, branch)
        stats[3:4, :TILE] += valid[...]


def run_visible(used, attended, tokens, valid, stats, weights):
    visible_count, width = tokens.shape
    hidden_width = weights["expand_weight"].shape[1]
    width_out = weights["head_turned"].shape[0]
    names = (
        "attention_out", "attention_shift",
        "midnorm_gain", "midnorm_shift", "expand_weight", "expand_shift", "reduce_weight",
        "reduce_shift", "lastnorm_gain", "lastnorm_shift", "head_turned", "head_shift",
    )
    return pl.pallas_call(
        visible_kernel,
        out_shape=(shape(visible_count, width_out), shape(8, width)),
        grid_spec=pltpu.PrefetchScalarGridSpec(
            num_scalar_prefetch=1,
            grid=(visible_count // TILE,),
            in_specs=[tile_spec(width, 2), tile_spec(width, 2), lane_spec(2), whole_spec(stats)]
            + staged_specs(weights, names),
            out_specs=[tile_spec(width_out, 2), whole_spec(stats)],
            scratch_shapes=parts_shapes(width, hidden_width)
            + [pltpu.VMEM((width, width_out), BF16)] * 2
            + [pltpu.SemaphoreType.DMA((3,))],
        ),
        compiler_params=pltpu.CompilerParams(vmem_limit_bytes=36 * 2**20),
        cost_estimate=cost(16),
        name="visible",
    )(used, attended, tokens, valid, stats, *[weights[name] for name in names])


def block_chunk(width, hidden_width, width_out):
    return [(width, hidden_width), (width, hidden_width), (width, width), (width_out, width), (24, width)]


def in_chunk(width):
    return [(width, 3 * width), (16, width)]


def attention_back_kernel(
    lens, joint_hbm, grad_rows, joint_grad, joint, joint_sems,
):
    width = grad_rows.shape[1]
    lane = lax.broadcasted_iota(jnp.int32, (CLOUD_MAX, 128), 1)
    first_head = lane < 64
    key_place = lax.broadcasted_iota(jnp.int32, (CLOUD_MAX, CLOUD_MAX), 0)
    query_place = lax.broadcasted_iota(jnp.int32, (CLOUD_MAX, CLOUD_MAX), 1)
    empty = jnp.zeros((CLOUD_MAX, 128), BF16)

    def both_heads(values):
        return jnp.concatenate(
            [jnp.where(first_head, values, 0.0), jnp.where(first_head, 0.0, values)], axis=0
        )

    def starts_of(index, start, masked_start):
        starts = []
        for number in range(BACK_GROUP):
            starts.append((start, masked_start))
            length = lens[jnp.minimum(index * BACK_GROUP + number, lens.shape[0] - 1)]
            start = start + spaced(length)
            masked_start = masked_start + spaced(masked_of(length))
        return starts, start, masked_start

    def fetch(starts, slot):
        step = CLOUD_MAX // JOINT_PIECES
        return [
            pltpu.make_async_copy(
                joint_hbm.at[pl.ds(start_of(start + piece * step), step)],
                joint.at[slot * BACK_GROUP + number, pl.ds(piece * step, step)],
                joint_sems.at[slot * BACK_GROUP + number, piece],
            )
            for number, (start, _) in enumerate(starts)
            for piece in range(JOINT_PIECES)
        ]

    groups = lens.shape[0] // BACK_GROUP
    start, masked_start = jnp.int32(0), jnp.int32(0)
    for index in range(JOINT_SLOTS - 1):
        starts, start, masked_start = starts_of(index, start, masked_start)
        for copy in fetch(starts, index):
            copy.start()
    work = [(number, pair) for number in range(BACK_GROUP) for pair in range(HEADS // 2)]

    def clouds(index, carry):
        start, masked_start, ahead = carry
        starts, following, masked_following = starts_of(index, start, masked_start)
        ahead_starts, next_ahead, _ = starts_of(index + JOINT_SLOTS - 1, ahead, jnp.int32(0))
        slot = lax.rem(index, JOINT_SLOTS)

        @pl.when(index + JOINT_SLOTS - 1 < groups)
        def _():
            for copy in fetch(ahead_starts, lax.rem(index + JOINT_SLOTS - 1, JOINT_SLOTS)):
                copy.start()

        for copy in fetch(starts, slot):
            copy.wait()
        lengths = [lens[index * BACK_GROUP + number] for number in range(BACK_GROUP)]
        insides = [key_place < length for length in lengths]
        lives = [
            jnp.logical_and(inside, query_place < masked_of(length)) for inside, length in zip(insides, lengths)
        ]
        rows = [pl.ds(start_of(starts[number][0]), CLOUD_MAX) for number, _ in work]
        slots = [slot * BACK_GROUP + number for number, _ in work]
        masked_rows = [pl.ds(start_of(starts[number][1]), CLOUD_MAX) for number, _ in work]
        at = [
            [slice(part * width + pair * 128, part * width + pair * 128 + 128) for part in range(3)]
            for _, pair in work
        ]
        each = range(len(work))
        query = [split(both_heads(joint[slots[one], :, at[one][0]] * 0.125)) for one in each]
        key = [split(joint[slots[one], :, at[one][1]]) for one in each]
        value = [split(joint[slots[one], :, at[one][2]]) for one in each]
        grad = [split(both_heads(grad_rows[masked_rows[one], at[one][0]])) for one in each]
        scores = [dot_pair(key[one], query[one]) for one in each]
        grad_probs = [dot_pair(value[one], grad[one]) for one in each]
        grad_wide = [jnp.concatenate(parts, axis=1) for parts in grad]
        query_wide = [jnp.concatenate(parts, axis=1) for parts in query]
        prob_parts, grad_parts, turned_parts = [], [], []
        for one in each:
            inside, live = insides[work[one][0]], lives[work[one][0]]
            probs, grads, turned = [], [], []
            for half in range(2):
                lanes = slice(half * CLOUD_MAX, half * CLOUD_MAX + CLOUD_MAX)
                score = jnp.where(inside, scores[one][:, lanes], -1e30)
                weight = jnp.exp(score - jnp.max(score, axis=0, keepdims=True))
                prob = jnp.where(live, weight * (1.0 / column_sum(weight)), 0.0)
                grad_prob = grad_probs[one][:, lanes]
                grad_score = prob * (grad_prob - column_sum(prob * grad_prob))
                probs.append(split(prob))
                grads.append(split(grad_score))
                turned.append(split(grad_score.T))
            for parts, found, axis in ((prob_parts, probs, 1), (grad_parts, grads, 1), (turned_parts, turned, 0)):
                parts.append(
                    tuple(jnp.concatenate([found[0][part], found[1][part]], axis=axis) for part in range(2))
                )
        for one in each:
            joint_grad[rows[one], at[one][2]] = dot_wide(prob_parts[one], grad_wide[one])
        for one in each:
            joint_grad[rows[one], at[one][1]] = dot_wide(grad_parts[one], query_wide[one])
        for one in each:
            left = jnp.concatenate(turned_parts[one], axis=1)
            right = jnp.concatenate(
                [
                    jnp.concatenate([key[one][0], key[one][1]], axis=1),
                    jnp.concatenate([key[one][0], empty], axis=1),
                ],
                axis=0,
            )
            grad_query = dot(left, right)
            grad_query = (grad_query[:, :128] + grad_query[:, 128:]) * 0.125
            joint_grad[rows[one], at[one][0]] = jnp.where(
                first_head, grad_query[:CLOUD_MAX], grad_query[CLOUD_MAX:]
            )

        return following, masked_following, next_ahead

    lax.fori_loop(0, groups, clouds, (jnp.int32(0), jnp.int32(0), start))


def run_attention_back(lens, joint, grad_attended):
    return pl.pallas_call(
        attention_back_kernel,
        out_shape=shape(*joint.shape),
        in_specs=[smem_spec(), any_spec(), vmem_spec()],
        out_specs=vmem_spec(),
        scratch_shapes=[
            pltpu.VMEM((JOINT_SLOTS * BACK_GROUP, CLOUD_MAX, joint.shape[1]), F32),
            pltpu.SemaphoreType.DMA((JOINT_SLOTS * BACK_GROUP, JOINT_PIECES)),
        ],
        compiler_params=pltpu.CompilerParams(vmem_limit_bytes=36 * 2**20),
        cost_estimate=cost(18),
        name="attention_back",
    )(lens, joint, grad_attended)


def in_back_kernel(
    devices, used_ref, lens, grad_joint, tokens, prenorm_gain, prenorm_shift, attention_in, stats,
    keep, send, sum_in, small, joint_sum,
):
    width = tokens.shape[1]
    spread, _, _ = cloud_totals(lens)
    sum_in[...] = jnp.zeros_like(sum_in)
    joint_sum[...] = jnp.zeros_like(joint_sum)

    def tile(index, carry):
        rows = pl.ds(pl.multiple_of(index * TILE, TILE), TILE)
        live = lax.broadcasted_iota(jnp.int32, (TILE, 1), 0) + index * TILE < spread
        unit, _ = norm_parts(tokens[rows, :])
        grads = jnp.where(live, grad_joint[rows, :], 0.0)
        joint_sum[...] += column_sum(grads)
        sum_in[...] += dot3(split(unit.T), split(grads))
        return carry

    lax.fori_loop(0, used_ref[0], tile, 0)
    small[...] = jnp.zeros_like(small)
    small[8:16, :] = stats[...]
    for row, factor in ((0, sum_in[...]), (1, joint_sum[...])):
        column = jnp.sum(attention_in[...] * factor, axis=1, keepdims=True)
        small[row : row + 1, :] = jnp.broadcast_to(column, (width, 128)).T[:1, :]
    gains = lanes_to_rows(row_of(prenorm_gain))
    shifts = lanes_to_rows(row_of(prenorm_shift))
    sum_in[...] = sum_in[...] * gains + shifts * joint_sum[...]
    pack_tiles([sum_in, small], keep, send, devices)


def run_in_back(used, lens, grad_joint, tokens, weights, stats, devices):
    width = tokens.shape[1]
    joint_width = grad_joint.shape[1]
    extra = [weights[name] for name in ("prenorm_gain", "prenorm_shift", "attention_in")]
    chunk = in_chunk(width)
    slots = slots_shape(chunk, devices)
    return pl.pallas_call(
        lambda *refs: in_back_kernel(devices, *refs),
        out_shape=(shape(*slots), shape(*slots)),
        in_specs=[smem_spec()] * 2 + [vmem_spec()] * 6,
        out_specs=[vmem_spec()] * 2,
        scratch_shapes=[pltpu.VMEM(dims, F32) for dims in chunk] + [pltpu.VMEM((1, joint_width), F32)],
        compiler_params=pltpu.CompilerParams(vmem_limit_bytes=20 * 2**20),
        cost_estimate=cost(11),
        name="in_back",
    )(used, lens, grad_joint, tokens, *extra, stats)


def input_kernel(
    used_ref, groups, grad_joint, tokens, grad_middle, prenorm_gain, attention_in, spaced_grad, in_parts,
):
    split_weight(attention_in, in_parts, 0)

    def tile(index, carry):
        rows = pl.ds(pl.multiple_of(index * TILE, TILE), TILE)
        unit, inverse = norm_parts(tokens[rows, :])
        grad_normed = dot_wide(split(grad_joint[rows, :]), in_parts[: 2 * tokens.shape[1], :], 1)
        spaced_grad[rows, :] = norm_back(grad_normed, unit, inverse, row_of(prenorm_gain))
        return carry

    lax.fori_loop(0, used_ref[0], tile, 0)

    def add_group(group, carry):
        source = groups[group]
        rows = pl.ds(start_of(group * 8), 8)
        added = grad_middle[pl.ds(start_of(jnp.maximum(source, 0) * 8), 8), :]
        spaced_grad[rows, :] += jnp.where(source >= 0, added, 0.0)
        return carry

    lax.fori_loop(0, groups.shape[0], add_group, 0, unroll=8)


def run_input(used, groups, grad_joint, tokens, grad_middle, weights):
    spaced_count, width = tokens.shape
    return pl.pallas_call(
        input_kernel,
        out_shape=shape(spaced_count, width),
        in_specs=[smem_spec()] * 2 + [vmem_spec()] * 5,
        out_specs=vmem_spec(),
        scratch_shapes=[pltpu.VMEM((3 * width, grad_joint.shape[1]), BF16)],
        compiler_params=pltpu.CompilerParams(vmem_limit_bytes=20 * 2**20),
        cost_estimate=cost(10),
        name="input_grad",
    )(used, groups, grad_joint, tokens, grad_middle, weights["prenorm_gain"], weights["attention_in"])


def restore_kernel(
    lens, owner, spaced_grad, masked_pred, visible_pred, input_grad, predicted_turned, pred_rows
):
    token_count, width = input_grad.shape
    input_grad[...] = jnp.zeros_like(input_grad)
    pred_rows[...] = jnp.zeros_like(pred_rows)
    windows = cloud_windows(lens, token_count)
    earlier = earlier_table()
    order = lax.broadcasted_iota(jnp.int32, (2 * CLOUD_MAX, CLOUD_MAX), 1)
    places_down = lax.broadcasted_iota(jnp.int32, (CLOUD_MAX, 1), 0)
    for first in range(0, lens.shape[0], 4):
        clouds = range(first, min(first + 4, lens.shape[0]))
        places = [
            cloud_places(
                owner[:, pl.ds(windows[cloud][1], 2 * CLOUD_MAX)],
                windows[cloud][0] - windows[cloud][1], lens[cloud], earlier,
            )
            for cloud in clouds
        ]
        columns = [lanes_to_rows(place.astype(F32)).astype(jnp.int32) for place in places]
        picks = [(order == column).astype(F32).astype(BF16) for column in columns]
        for pick, cloud in zip(picks, clouds):
            _, base, spaced_start, masked_start, visible_start = windows[cloud]
            rows = pl.ds(base, 2 * CLOUD_MAX)
            length, masked = lens[cloud], masked_of(lens[cloud])
            source = spaced_grad[pl.ds(spaced_start, CLOUD_MAX), :]
            high, low = split(jnp.where(places_down < length, source, 0.0))
            input_grad[rows, :] += dot(pick, high) + dot(pick, low)
            source = masked_pred[pl.ds(masked_start, CLOUD_MAX), :]
            shifted = pltpu.roll(
                jnp.concatenate(
                    [visible_pred[pl.ds(visible_start, VISIBLE_MAX), :], jnp.zeros_like(source[VISIBLE_MAX:])], axis=0
                ),
                masked, 0,
            )
            source = jnp.where(places_down < masked, source, shifted)
            high, low = split(jnp.where(places_down < length, source, 0.0))
            pred_rows[rows, :] += dot(pick, high) + dot(pick, low)
    for place in range(0, token_count, 128):
        predicted_turned[:, place : place + 128] = pred_rows[place : place + 128, :].T


def run_restore(lens, owner, spaced_grad, masked_pred, visible_pred):
    token_count = owner.shape[1]
    width, width_out = spaced_grad.shape[1], masked_pred.shape[1]
    return pl.pallas_call(
        restore_kernel,
        out_shape=(shape(token_count, width), shape(width_out, token_count)),
        in_specs=[smem_spec()] + [vmem_spec()] * 4,
        out_specs=[vmem_spec()] * 2,
        scratch_shapes=[pltpu.VMEM((token_count, width_out), F32)],
        compiler_params=pltpu.CompilerParams(vmem_limit_bytes=24 * 2**20),
        cost_estimate=cost(8),
        name="restore",
    )(lens, owner, spaced_grad, masked_pred, visible_pred)


def gather_pack(mine, theirs, pack, sems):
    copies = [
        pltpu.make_async_copy(mine, pack.at[0], sems.at[0]),
        pltpu.make_async_copy(theirs, pack.at[1], sems.at[1]),
    ]
    for copy in copies:
        copy.start()
    for copy in copies:
        copy.wait()


def block_sums_kernel(
    devices, mine, theirs,
    reduce_out, expand_out, attention_out, head_out, lastnorm_gain, lastnorm_shift, reduce_shift, head_shift,
    expand_shift, midnorm_gain, midnorm_shift, attention_shift, loss_out, scale_out,
    sum_reduce, small, pack, sems,
):
    gather_pack(mine, theirs, pack, sems)
    unpack_tiles(pack, [sum_reduce, expand_out, attention_out, head_out, small], devices, None)
    width = small.shape[1]
    scale = 1.0 / jnp.sum(small[1:2, :], axis=1, keepdims=True)
    scale_out[...] = jnp.broadcast_to(scale, scale_out.shape)
    for target in (expand_out, attention_out, head_out):
        target[...] = target[...] * scale
    for row, target in (
        (5, lastnorm_gain), (6, lastnorm_shift), (7, reduce_shift),
        (20, midnorm_gain), (21, midnorm_shift), (22, attention_shift),
    ):
        target[...] = (small[row : row + 1, :] * scale)[0]
    for part in range(expand_shift.shape[0] // width):
        expand_shift[part * width : part * width + width] = (small[16 + part : 17 + part, :] * scale)[0]
    head_shift[...] = (small[8:9, :] * scale)[0, : head_shift.shape[0]]
    loss_out[0] = jnp.sum(small[0:1, :]) / jnp.sum(small[1:2, :])
    for place in range(0, reduce_out.shape[0], 128):
        reduce_out[place : place + 128, :] = sum_reduce[:, place : place + 128].T * scale


def in_sums_kernel(devices, scale, mine, theirs, in_out, prenorm_gain, prenorm_shift, rms_out, small, pack, sems):
    gather_pack(mine, theirs, pack, sems)
    unpack_tiles(pack, [in_out, small], devices, scale[...])
    prenorm_gain[...] = small[0, :]
    prenorm_shift[...] = small[1, :]
    totals = jnp.sum(small[8:16, :], axis=1, keepdims=True)
    rms_out[...] = jnp.broadcast_to(jnp.sqrt(totals / (totals[3:4] * small.shape[1])), rms_out.shape)


def run_sums(kernel, scale, mine, theirs, chunk, outs, keep, devices, name):
    scales = [] if scale is None else [scale]
    return pl.pallas_call(
        lambda *refs: kernel(devices, *refs),
        out_shape=tuple(shape(*dims) for dims in outs),
        in_specs=[vmem_spec()] * len(scales) + [any_spec()] * 2,
        out_specs=[smem_spec() if dims == (1,) else vmem_spec() for dims in outs],
        scratch_shapes=[pltpu.VMEM(dims, F32) for dims in keep]
        + [
            pltpu.VMEM((2,) + slots_shape(chunk, devices), F32),
            pltpu.SemaphoreType.DMA((2,)),
        ],
        compiler_params=pltpu.CompilerParams(vmem_limit_bytes=24 * 2**20),
        cost_estimate=cost(4),
        name=name,
    )(*scales, mine, theirs)


def shards(
    tokens, cloud_lengths, owner_slot, targets, prenorm_gain, prenorm_shift, attention_in,
    attention_out, attention_shift, midnorm_gain, midnorm_shift, expand_weight, expand_shift,
    reduce_weight, reduce_shift, lastnorm_gain, lastnorm_shift, head_weight, head_shift,
):
    token_count, width = tokens.shape
    hidden_width = expand_weight.shape[1]
    devices = lax.axis_size("dp")
    slot_count, width_out = targets.shape
    capacity = slot_count // devices
    arrived = lax.all_to_all(
        targets.reshape(devices, capacity, width_out), "dp", split_axis=0, concat_axis=0, tiled=True
    ).reshape(slot_count, width_out)
    weights = dict(
        prenorm_gain=prenorm_gain, prenorm_shift=prenorm_shift, attention_in=attention_in,
        attention_out=attention_out, attention_shift=attention_shift,
        midnorm_gain=midnorm_gain, midnorm_shift=midnorm_shift,
        expand_weight=expand_weight, expand_shift=expand_shift, reduce_weight=reduce_weight,
        reduce_shift=reduce_shift, lastnorm_gain=lastnorm_gain,
        lastnorm_shift=lastnorm_shift, head_turned=head_weight.T,
        head_shift=head_shift,
    )
    owner = owner_slot[None]
    (
        spaced_tokens, joint, masked_tokens, masked_attended, visible_tokens, visible_attended,
        owners, valid, used, groups,
    ) = run_attend(
        tokens, cloud_lengths, owner, weights["prenorm_gain"], weights["prenorm_shift"], attention_in
    )
    masked_pred, grad_middle, grad_attended, stats, block_keep, block_send = run_block(
        used, masked_attended, masked_tokens, owners, arrived, weights, devices
    )
    block_sum = DeviceSum(block_keep, block_send, devices)
    grad_attended, stats = beside([block_sum], (grad_attended, stats))
    visible_pred, stats = beside(
        [block_sum], run_visible(used, visible_attended, visible_tokens, valid, stats, weights)
    )
    grad_attended, _ = lax.optimization_barrier((grad_attended, stats))
    grad_joint = beside([block_sum], run_attention_back(cloud_lengths, joint, grad_attended))
    in_keep, in_send = beside(
        [block_sum], run_in_back(used, cloud_lengths, grad_joint, spaced_tokens, weights, stats, devices)
    )
    in_sum = DeviceSum(in_keep, in_send, devices)
    sums = [in_sum, block_sum]
    grad_joint = beside([in_sum], grad_joint)
    spaced_grad = beside(sums, run_input(used, groups, grad_joint, spaced_tokens, grad_middle, weights))
    input_grad, predicted_turned = beside(
        sums, run_restore(cloud_lengths, owner, spaced_grad, masked_pred, visible_pred)
    )
    if not block_sum.done():
        block_sum.start()
        beside([in_sum], ())
        in_sum.start()
        moving = lax.optimization_barrier([one.moving for one in sums])
        for one, moved in zip(sums, moving):
            one.moving = moved
            one.finish()
    while not block_sum.done():
        beside(sums, ())
    chunk = block_chunk(width, hidden_width, width_out)
    vector = (width,)
    (
        grad_reduce, grad_expand, grad_out, grad_head_turned, grad_last_gain, grad_last_shift, grad_reduce_shift,
        grad_head_shift, grad_expand_shift, grad_mid_gain, grad_mid_shift, grad_out_shift, loss, scale,
    ) = beside(
        [in_sum],
        run_sums(
            block_sums_kernel, None, block_sum.total, block_sum.theirs, chunk,
            [
                (hidden_width, width), chunk[1], chunk[2], chunk[3], vector, vector, vector,
                (width_out,), (hidden_width,), vector, vector, vector, (1,), (8, 128),
            ],
            [chunk[0], chunk[4]], devices, "block_sums",
        ),
    )
    run_out([in_sum])
    chunk = in_chunk(width)
    grad_in, grad_pre_gain, grad_pre_shift, rms = run_sums(
        in_sums_kernel, scale, in_sum.total, in_sum.theirs, chunk,
        [chunk[0], (width,), (width,), (8, 128)], [chunk[1]], devices, "in_sums",
    )
    return (
        loss.reshape(()),
        predicted_turned.T,
        input_grad,
        grad_pre_gain,
        grad_pre_shift,
        grad_in,
        grad_out,
        grad_out_shift,
        grad_mid_gain,
        grad_mid_shift,
        grad_expand,
        grad_expand_shift,
        grad_reduce,
        grad_reduce_shift,
        grad_last_gain,
        grad_last_shift,
        grad_head_turned.T,
        grad_head_shift,
        rms[:3, 0],
    )


def solution(mesh):
    row = P("dp", None)
    return jax.shard_map(
        shards,
        mesh=mesh,
        in_specs=(row, P("dp"), P("dp"), row) + (P(),) * 15,
        out_specs=(P(), row, row) + (P(),) * 16,
        check_vma=False,
    )
```

```python
import math

import jax
import jax.numpy as jnp
from jax import lax
from jax.experimental import pallas as pl
from jax.experimental.pallas import tpu as pltpu
from jax.sharding import PartitionSpec as P

HEADS = 6
CLOUD_MAX = 128
TILE = 256
GROUP = 4
BACK_GROUP = 1
JOINT_SLOTS = 3
JOINT_PIECES = 4
MASKED_TILE = 512
VISIBLE_MAX = 64
EPSILON = 1e-05
F32 = jnp.float32
BF16 = jnp.bfloat16
VMEM_BYTES = 60 * 1024 * 1024


def split(values):
    high = values.astype(BF16)
    low = (values - high.astype(F32)).astype(BF16)
    return high, low


def dot(left, right, left_dim=1, right_dim=0):
    return lax.dot_general(
        left, right, (((left_dim,), (right_dim,)), ((), ())), preferred_element_type=F32
    )


def dot3(left, right, left_dim=1, right_dim=0):
    left_high, left_low = left
    right_high, right_low = right
    return dot(left_high, right_high, left_dim, right_dim) + (
        dot(left_high, right_low, left_dim, right_dim)
        + dot(left_low, right_high, left_dim, right_dim)
    )


def dot_deep(left, triple, right_dim=0):
    left_high, left_low = left
    return dot(jnp.concatenate([left_high, left_high, left_low], axis=1), triple, 1, right_dim)


def dot_wide(left, pair, right_dim=0):
    left_high, left_low = left
    columns = pair.shape[1 - right_dim] // 2
    both = dot(left_high, pair, 1, right_dim)
    high = pair[:columns, :] if right_dim else pair[:, :columns]
    return both[:, :columns] + (both[:, columns:] + dot(left_low, high, 1, right_dim))


def dot_pair(left, right):
    right_high, right_low = right
    return dot(jnp.concatenate(left, axis=1), jnp.concatenate([right_high, right_high], axis=1), 1, 1) + dot(
        left[0], right_low, 1, 1
    )


def norm_parts(values):
    average = jnp.mean(values, axis=-1, keepdims=True)
    centred = values - average
    spread = jnp.mean(centred * centred, axis=-1, keepdims=True)
    inverse = lax.rsqrt(spread + EPSILON)
    return centred * inverse, inverse


def norm_back(grad_out, unit_rows, inverse, scale_gain):
    scaled = grad_out * scale_gain
    average_grad = jnp.mean(scaled, axis=-1, keepdims=True)
    project_grad = jnp.mean(scaled * unit_rows, axis=-1, keepdims=True)
    return inverse * (scaled - average_grad - unit_rows * project_grad)


def any_spec():
    return pl.BlockSpec(memory_space=pltpu.HBM)


def vmem_spec():
    return pl.BlockSpec(memory_space=pltpu.VMEM)


def smem_spec():
    return pl.BlockSpec(memory_space=pltpu.SMEM)


def cost(microseconds):
    return pl.CostEstimate(flops=microseconds * 10**9, bytes_accessed=microseconds * 10**6, transcendentals=0)


def shape(*dims):
    return jax.ShapeDtypeStruct(dims, F32)


def row_of(vector):
    return vector[...][None, :]


def column_sum(values):
    return jnp.sum(values, axis=0, keepdims=True)


def split_weight(source, target, axis, step=128):
    rows, columns = source.shape

    def body(index, carry):
        start = pl.multiple_of(index * step, step)
        for part, values in enumerate(split_three(source[pl.ds(start, step), :])):
            if axis == 0:
                target[pl.ds(start + part * rows, step), :] = values
            else:
                target[pl.ds(start, step), part * columns : part * columns + columns] = values
        return carry

    lax.fori_loop(0, rows // step, body, 0)


def split_three(values):
    high, low = split(values)
    return high, low, high


def spaced(length):
    return (length + 7) // 8 * 8


def aligned_rows(token_count, cloud_count):
    return (token_count + 8 * cloud_count + TILE - 1) // TILE * TILE


def masked_of(length):
    return 3 * length // 5


def tiles_of(rows, tile=TILE):
    return (rows + tile - 1) // tile


def compact_rows(token_count, cloud_count):
    return tiles_of(masked_of(token_count) + 8 * cloud_count, MASKED_TILE) * MASKED_TILE


def visible_rows(token_count, cloud_count):
    return tiles_of(token_count - masked_of(token_count) + 9 * cloud_count) * TILE


def cloud_totals(lens):
    spread, masked, visible = jnp.int32(0), jnp.int32(0), jnp.int32(0)
    for cloud in range(lens.shape[0]):
        length = lens[cloud]
        spread = spread + spaced(length)
        masked = masked + spaced(masked_of(length))
        visible = visible + spaced(length - masked_of(length))
    return spread, masked, visible


def cloud_windows(lens, token_count):
    start, spaced_start, masked_start, visible_start = (jnp.int32(0),) * 4
    windows = []
    for cloud in range(lens.shape[0]):
        length = lens[cloud]
        base = jnp.minimum(start // 128, token_count // 128 - 2) * 128
        windows.append(
            (start, pl.multiple_of(base, 128), start_of(spaced_start), start_of(masked_start), start_of(visible_start))
        )
        start = start + length
        spaced_start = spaced_start + spaced(length)
        masked_start = masked_start + spaced(masked_of(length))
        visible_start = visible_start + spaced(length - masked_of(length))
    return windows


def earlier_table():
    rows = lax.broadcasted_iota(jnp.int32, (2 * CLOUD_MAX, 2 * CLOUD_MAX), 0)
    columns = lax.broadcasted_iota(jnp.int32, (2 * CLOUD_MAX, 2 * CLOUD_MAX), 1)
    return (rows < columns).astype(F32).astype(BF16)


def cloud_places(slots, offset, length, earlier):
    lanes = lax.broadcasted_iota(jnp.int32, (1, 2 * CLOUD_MAX), 1)
    inside = jnp.logical_and(lanes >= offset, lanes < offset + length)
    masked = jnp.logical_and(inside, slots >= 0)
    flags = jnp.broadcast_to(masked.astype(F32), (8, 2 * CLOUD_MAX)).astype(BF16)
    rank = dot(flags, earlier)[:1].astype(jnp.int32)
    visible = masked_of(length) + lanes - offset - rank
    return jnp.where(masked, rank, jnp.where(inside, visible, -1))


def start_of(place):
    return pl.multiple_of(place, 8)


def gelu_parts(pre_act):
    cumulative = 0.5 * (1.0 + lax.erf(pre_act * (1.0 / math.sqrt(2.0))))
    density = jnp.exp(-0.5 * pre_act * pre_act) * (1.0 / math.sqrt(2.0 * math.pi))
    return pre_act * cumulative, cumulative + pre_act * density


def slot_place(relative, part, devices):
    x, y, rest = (relative >> 1) & 1, (relative >> 2) & 1, relative >> 3
    major, minor = (x, y) if part == 0 else (y, x)
    return relative & 1, major * (devices // 4) + minor * (devices // 8) + rest


def tile_list(shapes):
    return [
        (which, row, column)
        for which, (rows, columns) in enumerate(shapes)
        for row in range(0, rows, 8)
        for column in range(0, columns, 128)
    ]


def atom_tiles(shapes, devices):
    return -(-len(tile_list(shapes)) // (2 * devices))


def slots_shape(shapes, devices):
    return (2, devices // 2, atom_tiles(shapes, devices) * 8, 128)


def pack_tiles(sources, keep, send, devices):
    me = lax.axis_index("dp")
    tiles = tile_list([source.shape for source in sources])
    each = atom_tiles([source.shape for source in sources], devices)
    for atom in range(-(-len(tiles) // each)):
        part, owner = atom // devices, atom % devices
        bit, place = slot_place(me ^ owner, part, devices)

        def copy(target, atom=atom, part=part, place=place):
            for number, (which, row, column) in enumerate(tiles[atom * each : atom * each + each]):
                target[part, place, number * 8 : number * 8 + 8, :] = sources[which][
                    row : row + 8, column : column + 128
                ]

        pl.when(bit == 0)(lambda copy=copy: copy(keep))
        pl.when(bit == 1)(lambda copy=copy: copy(send))


def unpack_tiles(pack, targets, devices, scale):
    me = lax.axis_index("dp")
    tiles = tile_list([target.shape for target in targets])
    each = atom_tiles([target.shape for target in targets], devices)
    for atom in range(-(-len(tiles) // each)):
        part, owner = atom // devices, atom % devices
        bit, place = slot_place(me ^ owner, part, devices)
        for number, (which, row, column) in enumerate(tiles[atom * each : atom * each + each]):
            piece = pack[bit, part, place, number * 8 : number * 8 + 8, :]
            targets[which][row : row + 8, column : column + 128] = (
                piece if scale is None else piece * scale
            )


def swap(values, bits, devices):
    return lax.ppermute(values, "dp", [(device, device ^ bits) for device in range(devices)])


def rest_groups(devices):
    count = (devices // 8).bit_length() - 1
    groups = []
    while count:
        step = 2 if count >= 2 else 1
        count -= step
        groups.append((3 + count, 1 << step))
    return groups


class DeviceSum:
    def __init__(self, keep, send, devices):
        self.devices = devices
        self.groups = rest_groups(devices)
        self.keep, self.send = keep, send
        self.stage = 0
        self.last = 5 + 2 * len(self.groups)

    def start(self):
        devices, stage, count = self.devices, self.stage, len(self.groups)
        if stage == 0:
            self.moving = [swap(self.send, 1, devices)]
        elif stage <= 2:
            size = devices // (4, 8)[stage - 1]
            bits = ((2, 4), (4, 2))[stage - 1]
            self.moving = [swap(half[size:], bit, devices) for half, bit in zip(self.halves, bits)]
            self.halves = [half[:size] for half in self.halves]
        elif stage < 3 + count:
            shift, size = self.groups[stage - 3]
            total = self.total.reshape((size, -1) + self.total.shape[1:])
            self.moving = [swap(total[slot], slot << shift, devices) for slot in range(1, size)]
            self.total = total[0]
        elif stage < 3 + 2 * count:
            shift, size = self.groups[3 + 2 * count - 1 - stage]
            self.moving = [swap(self.total, slot << shift, devices) for slot in range(1, size)]
        elif stage < 5 + 2 * count:
            bits = ((4, 2), (2, 4))[stage - 3 - 2 * count]
            self.moving = [swap(half, bit, devices) for half, bit in zip(self.halves, bits)]
        else:
            self.moving = [swap(self.total, 1, devices)]

    def finish(self):
        stage, count = self.stage, len(self.groups)
        if stage == 0:
            total = self.keep + self.moving[0]
            self.halves = [total[0], total[1]]
        elif stage <= 2:
            self.halves = [half + moved for half, moved in zip(self.halves, self.moving)]
            if stage == 2:
                self.total = jnp.stack(self.halves, axis=1)
        elif stage < 3 + count:
            self.total = sum(self.moving, self.total)
        elif stage < 3 + 2 * count:
            self.total = jnp.concatenate([self.total] + self.moving, axis=0)
            if stage == 2 + 2 * count:
                self.halves = [self.total[:, 0], self.total[:, 1]]
        elif stage < 5 + 2 * count:
            self.halves = [jnp.concatenate([half, moved]) for half, moved in zip(self.halves, self.moving)]
            if stage == 4 + 2 * count:
                self.total = jnp.stack(self.halves)
        else:
            self.theirs = self.moving[0]
        self.stage += 1

    def done(self):
        return self.stage > self.last

    def state(self):
        if hasattr(self, "total") and (3 <= self.stage < 3 + 2 * len(self.groups) or self.stage >= self.last):
            return self.total
        return self.halves

    def set_state(self, state):
        if hasattr(self, "total") and (3 <= self.stage < 3 + 2 * len(self.groups) or self.stage >= self.last):
            self.total = state
        else:
            self.halves = state


def beside(sums, outs):
    sums = [one for one in sums if not one.done()]
    for one in sums:
        one.start()
    moving, outs = lax.optimization_barrier(([one.moving for one in sums], outs))
    for one, moved in zip(sums, moving):
        one.moving = moved
        one.finish()
    going = [one for one in sums if not one.done()]
    states, outs = lax.optimization_barrier(([one.state() for one in going], outs))
    for one, state in zip(going, states):
        one.set_state(state)
    return outs


def run_stage(one):
    one.start()
    one.finish()


def run_out(sums):
    while not all(one.done() for one in sums):
        for one in sums:
            if not one.done():
                run_stage(one)


def attend_kernel(
    lens, tokens_hbm, owner, prenorm_gain, prenorm_shift, attention_in,
    tokens_out, joint_out, masked_tokens_out, masked_attended_out, visible_tokens_out, visible_attended_out,
    owners, valid, used_out, groups_out,
    raw, tokens, joint, masked_tokens, masked_attended, visible_tokens, visible_attended, in_parts,
    token_sem, joint_sem, out_sems,
):
    token_count = owner.shape[1]
    tiles = tokens.shape[0] // TILE
    width = tokens.shape[1]
    spread, masked_total, visible_total = cloud_totals(lens)
    used, visible_used = tiles_of(spread), tiles_of(visible_total)
    masked_used = tiles_of(masked_total, MASKED_TILE)
    used_out[0] = used
    used_out[1] = masked_used
    used_out[2] = visible_used

    def tile_rows(index, tile=TILE):
        return pl.ds(pl.multiple_of(index * tile, tile), tile)

    token_copy = pltpu.make_async_copy(tokens_hbm, raw, token_sem)
    token_copy.start()
    split_weight(attention_in, in_parts, 0)
    owners[...] = jnp.full(owners.shape, -1, jnp.int32)
    valid[...] = jnp.zeros(valid.shape, F32)
    blank = jnp.zeros((TILE, width), F32)
    tokens[tile_rows(used - 1), :] = blank
    for kept in (masked_tokens, masked_attended):
        kept[tile_rows(masked_used - 1, MASKED_TILE), :] = jnp.zeros((MASKED_TILE, width), F32)
    for kept in (visible_tokens, visible_attended):
        kept[tile_rows(visible_used - 1), :] = blank

    def no_group(index, carry):
        groups_out[index] = -1
        return carry

    lax.fori_loop(0, groups_out.shape[0], no_group, 0, unroll=8)

    def cloud_groups(cloud, carry):
        spaced_group, masked_group = carry
        count = spaced(masked_of(lens[cloud])) // 8

        def group(index, carry):
            groups_out[spaced_group + index] = masked_group + index
            return carry

        lax.fori_loop(0, count, group, 0)
        return spaced_group + spaced(lens[cloud]) // 8, masked_group + count

    lax.fori_loop(0, lens.shape[0], cloud_groups, (jnp.int32(0), jnp.int32(0)))
    windows = cloud_windows(lens, token_count)
    earlier = earlier_table()
    wide = lax.broadcasted_iota(jnp.int32, (1, 2 * CLOUD_MAX), 1)
    order = lax.broadcasted_iota(jnp.int32, (CLOUD_MAX + VISIBLE_MAX, 2 * CLOUD_MAX), 0)
    token_copy.wait()
    for first in range(0, lens.shape[0], 4):
        clouds = range(first, min(first + 4, lens.shape[0]))
        slots = [owner[:, pl.ds(windows[cloud][1], 2 * CLOUD_MAX)] for cloud in clouds]
        places = [
            cloud_places(slot, windows[cloud][0] - windows[cloud][1], lens[cloud], earlier)
            for slot, cloud in zip(slots, clouds)
        ]
        rows_of = [
            jnp.where(order < CLOUD_MAX, order, order - CLOUD_MAX + masked_of(lens[cloud])) for cloud in clouds
        ]
        picks = [(row == place).astype(F32).astype(BF16) for row, place in zip(rows_of, places)]
        for pick, slot, cloud in zip(picks, slots, clouds):
            _, base, spaced_start, masked_start, visible_start = windows[cloud]
            rows = raw[pl.ds(base, 2 * CLOUD_MAX), :]
            high = rows.astype(BF16)
            rest = rows - high.astype(F32)
            mid, low = split(rest)
            moved = dot(pick, jnp.concatenate([high, mid, low], axis=1))
            moved = (moved[:, :width] + moved[:, width : 2 * width]) + moved[:, 2 * width :]
            tokens[pl.ds(spaced_start, CLOUD_MAX), :] = moved[:CLOUD_MAX]
            masked_tokens[pl.ds(masked_start, CLOUD_MAX), :] = moved[:CLOUD_MAX]
            visible_tokens[pl.ds(visible_start, VISIBLE_MAX), :] = moved[CLOUD_MAX:]
            parts = jnp.concatenate(
                [(slot >> 6).astype(F32), (slot & 63).astype(F32), jnp.zeros((6, 2 * CLOUD_MAX), F32)], axis=0
            )
            parts = dot(parts.astype(BF16), pick[:CLOUD_MAX], 1, 1)
            moved = (parts[0:1] * 64.0 + parts[1:2]).astype(jnp.int32)
            moved = jnp.concatenate([moved, jnp.zeros((1, CLOUD_MAX), jnp.int32)], axis=1)
            masked, visible = masked_of(lens[cloud]), lens[cloud] - masked_of(lens[cloud])
            offset = masked_start % 128
            lanes = pl.ds(pl.multiple_of(masked_start // 128 * 128, 128), 2 * CLOUD_MAX)
            inside = jnp.logical_and(wide >= offset, wide < offset + masked)
            owners[:, lanes] = jnp.where(inside, pltpu.roll(moved, offset, 1), owners[:, lanes])
            offset = visible_start % 128
            lanes = pl.ds(pl.multiple_of(visible_start // 128 * 128, 128), 2 * CLOUD_MAX)
            inside = jnp.logical_and(wide >= offset, wide < offset + visible)
            valid[:, lanes] = jnp.where(inside, 1.0, valid[:, lanes])

    def joint_copies(index):
        rows = tile_rows(index)
        return [
            pltpu.make_async_copy(joint.at[rows], joint_out.at[rows], joint_sem.at[index]),
            pltpu.make_async_copy(tokens.at[rows], tokens_out.at[rows], out_sems.at[0, index]),
        ]

    def joint_tile(index, carry):
        rows = tile_rows(index)
        unit, _ = norm_parts(tokens[rows, :])
        normed = split(unit * row_of(prenorm_gain) + row_of(prenorm_shift))
        joint[rows, :] = dot_deep(normed, in_parts[...])
        for copy in joint_copies(index):
            copy.start()
        return carry

    lax.fori_loop(0, used, joint_tile, 0)
    tail = pl.ds(pl.multiple_of(used * TILE, TILE), CLOUD_MAX)
    joint[tail, :] = jnp.zeros((CLOUD_MAX, joint.shape[1]), F32)
    tail_copy = pltpu.make_async_copy(joint.at[tail], joint_out.at[tail], joint_sem.at[tiles])
    tail_copy.start()

    lane = lax.broadcasted_iota(jnp.int32, (CLOUD_MAX, 128), 1)
    first_head = lane < 64
    wide_lane = lax.broadcasted_iota(jnp.int32, (CLOUD_MAX, CLOUD_MAX), 1)
    empty = jnp.zeros((CLOUD_MAX, 128), BF16)

    visible_order = lax.broadcasted_iota(jnp.int32, (VISIBLE_MAX, CLOUD_MAX), 0)
    visible_column = lax.broadcasted_iota(jnp.int32, (VISIBLE_MAX, CLOUD_MAX), 1)

    def clouds(index, carry):
        start, masked_start, visible_start = carry
        lengths = [lens[GROUP * index + number] for number in range(GROUP)]
        places, masked_places, visible_places = [], [], []
        for length in lengths:
            places.append(pl.ds(start_of(start), CLOUD_MAX))
            masked_places.append(pl.ds(start_of(masked_start), CLOUD_MAX))
            visible_places.append(pl.ds(start_of(visible_start), VISIBLE_MAX))
            start = start + spaced(length)
            masked_start = masked_start + spaced(masked_of(length))
            visible_start = visible_start + spaced(length - masked_of(length))
        picks = [
            jnp.logical_and(visible_column == visible_order + masked_of(length), visible_column < length)
            .astype(F32)
            .astype(BF16)
            for length in lengths
        ]
        insides = [wide_lane < length for length in lengths]
        work = [(number, pair) for number in range(GROUP) for pair in range(HEADS // 2)]
        lefts, rights = [], []
        for number, pair in work:
            rows = places[number]
            query = joint[rows, pair * 128 : pair * 128 + 128] * 0.125
            key_high, key_low = split(joint[rows, width + pair * 128 : width + pair * 128 + 128])
            both = jnp.concatenate(
                [jnp.where(first_head, query, 0.0), jnp.where(first_head, 0.0, query)], axis=0
            )
            lefts.append(jnp.concatenate(split(both), axis=1))
            rights.append(
                jnp.concatenate(
                    [
                        jnp.concatenate([key_high, key_high], axis=1),
                        jnp.concatenate([key_low, empty], axis=1),
                    ],
                    axis=0,
                )
            )
        scores = [dot(left, right, 1, 1) for left, right in zip(lefts, rights)]
        lefts = []
        for (number, _), score in zip(work, scores):
            parts = []
            for half in range(2):
                rows = slice(half * CLOUD_MAX, half * CLOUD_MAX + CLOUD_MAX)
                head = jnp.where(insides[number], score[rows, :128] + score[rows, 128:], -1e30)
                weight = jnp.exp(head - jnp.max(head, axis=-1, keepdims=True))
                prob = weight * (1.0 / jnp.sum(weight, axis=-1, keepdims=True))
                parts.append(jnp.concatenate(split(prob), axis=1))
            lefts.append(jnp.concatenate(parts, axis=0))
        rights = []
        for number, pair in work:
            value_high, value_low = split(
                joint[places[number], 2 * width + pair * 128 : 2 * width + pair * 128 + 128]
            )
            rights.append(
                jnp.concatenate(
                    [
                        jnp.concatenate([value_high, value_low], axis=1),
                        jnp.concatenate([value_high, empty], axis=1),
                    ],
                    axis=0,
                )
            )
        mixed = [dot(left, right) for left, right in zip(lefts, rights)]
        for (number, pair), both in zip(work, mixed):
            both = both[:, :128] + both[:, 128:]
            both = jnp.where(first_head, both[:CLOUD_MAX], both[CLOUD_MAX:])
            columns = slice(pair * 128, pair * 128 + 128)
            masked_attended[masked_places[number], columns] = both
            moved = dot(picks[number], jnp.concatenate(split(both), axis=1))
            visible_attended[visible_places[number], columns] = moved[:, :128] + moved[:, 128:]
        return start, masked_start, visible_start

    zero = jnp.int32(0)
    lax.fori_loop(0, lens.shape[0] // GROUP, clouds, (zero, zero, zero))

    def masked_copies(index):
        rows = tile_rows(index, MASKED_TILE)
        return [
            pltpu.make_async_copy(masked_tokens.at[rows], masked_tokens_out.at[rows], out_sems.at[1, index]),
            pltpu.make_async_copy(masked_attended.at[rows], masked_attended_out.at[rows], out_sems.at[2, index]),
        ]

    def visible_copies(index):
        rows = tile_rows(index)
        return [
            pltpu.make_async_copy(visible_tokens.at[rows], visible_tokens_out.at[rows], out_sems.at[3, index]),
            pltpu.make_async_copy(visible_attended.at[rows], visible_attended_out.at[rows], out_sems.at[4, index]),
        ]

    def begin(copies_of):
        def body(index, carry):
            for copy in copies_of(index):
                copy.start()
            return carry

        return body

    def finish(copies_of):
        def body(index, carry):
            for copy in copies_of(index):
                copy.wait()
            return carry

        return body

    lax.fori_loop(0, masked_used, begin(masked_copies), 0)
    lax.fori_loop(0, visible_used, begin(visible_copies), 0)
    tail_copy.wait()
    lax.fori_loop(0, used, finish(joint_copies), 0)
    lax.fori_loop(0, masked_used, finish(masked_copies), 0)
    lax.fori_loop(0, visible_used, finish(visible_copies), 0)


def run_attend(tokens, lens, owner, prenorm_gain, prenorm_shift, attention_in):
    token_count, width = tokens.shape
    joint_width = attention_in.shape[1]
    spaced_count = aligned_rows(token_count, lens.shape[0])
    masked_count = compact_rows(token_count, lens.shape[0])
    visible_count = visible_rows(token_count, lens.shape[0])
    tiles = spaced_count // TILE
    return pl.pallas_call(
        attend_kernel,
        out_shape=(
            shape(spaced_count, width),
            shape(spaced_count + CLOUD_MAX, joint_width),
            shape(masked_count, width),
            shape(masked_count, width),
            shape(visible_count, width),
            shape(visible_count, width),
            jax.ShapeDtypeStruct((1, masked_count + 256), jnp.int32),
            shape(1, visible_count + 256),
            jax.ShapeDtypeStruct((3,), jnp.int32),
            jax.ShapeDtypeStruct((spaced_count // 8,), jnp.int32),
        ),
        in_specs=[smem_spec(), any_spec()] + [vmem_spec()] * 4,
        out_specs=[any_spec()] * 6 + [vmem_spec()] * 2 + [smem_spec()] * 2,
        scratch_shapes=[
            pltpu.VMEM((token_count, width), F32),
            pltpu.VMEM((spaced_count, width), F32),
            pltpu.VMEM((spaced_count + CLOUD_MAX, joint_width), F32),
            pltpu.VMEM((masked_count + CLOUD_MAX, width), F32),
            pltpu.VMEM((masked_count + CLOUD_MAX, width), F32),
            pltpu.VMEM((visible_count + VISIBLE_MAX, width), F32),
            pltpu.VMEM((visible_count + VISIBLE_MAX, width), F32),
            pltpu.VMEM((3 * width, joint_width), BF16),
            pltpu.SemaphoreType.DMA,
            pltpu.SemaphoreType.DMA((tiles + 1,)),
            pltpu.SemaphoreType.DMA((5, tiles)),
        ],
        compiler_params=pltpu.CompilerParams(vmem_limit_bytes=48 * 2**20),
        cost_estimate=cost(26),
        name="attend",
    )(lens, tokens, owner, prenorm_gain, prenorm_shift, attention_in)


def stage_weights(staged, sems):
    copies = [
        pltpu.make_async_copy(weight, place, sems.at[number])
        for number, (weight, place, _, _) in enumerate(staged)
    ]
    for copy in copies:
        copy.start()
    return copies


def split_staged(copies, staged):
    for copy, (_, place, parts, axis) in zip(copies, staged):
        copy.wait()
        split_weight(place, parts, axis)


def block_rows(
    attended, tokens, out_parts, attention_shift, midnorm_gain, midnorm_shift, expand_parts, expand_shift,
    reduce_parts, reduce_shift,
):
    width = tokens.shape[1]
    mixed = dot_wide(split(attended[...]), out_parts[:, : 2 * width]) + row_of(attention_shift)
    middle = tokens[...] + mixed
    unit, inverse = norm_parts(middle)
    normed = unit * row_of(midnorm_gain) + row_of(midnorm_shift)
    pre_act = dot_deep(split(normed), expand_parts[...]) + row_of(expand_shift)
    hidden, slope = gelu_parts(pre_act)
    hidden = split(hidden)
    branch = dot_wide(hidden, reduce_parts[:, : 2 * width]) + row_of(reduce_shift)
    return mixed, middle, (unit, inverse, normed), hidden, slope, branch


def fold_lanes(lanes):
    return sum(lanes[:, place : place + 128] for place in range(0, lanes.shape[1], 128))


def lanes_to_rows(lanes):
    return jnp.broadcast_to(lanes, (8, lanes.shape[1])).T[:, :1]


def add_squares(stats, live, stream, mixed, branch):
    for row, values in enumerate((stream, mixed, branch)):
        stats[row : row + 1, :] += column_sum(jnp.where(live, values * values, 0.0))


def block_kernel(
    devices, used_ref, attended, tokens, owners, targets, attention_out,
    attention_shift, midnorm_gain, midnorm_shift, expand_weight, expand_shift, reduce_weight,
    reduce_shift, lastnorm_gain, lastnorm_shift, head_turned, head_shift,
    predicted, grad_middle, grad_attended, stats, keep, send,
    sum_reduce, sum_expand, sum_out, sum_head, small,
    out_stage, expand_stage, reduce_stage, out_parts, expand_parts, reduce_parts,
    head_high, head_low, turned_high, turned_low, target_parts, pred_rows, true_rows, distance, second,
    col_low, col_sum, shift_column, weight_sems,
):
    index = pl.program_id(0)
    used = used_ref[1]
    slot_count, width_out = targets.shape
    points = width_out // 3
    width = tokens.shape[1]

    @pl.when(index == 0)
    def _():
        staged = [
            (attention_out, out_stage, out_parts, 1),
            (expand_weight, expand_stage, expand_parts, 0),
            (reduce_weight, reduce_stage, reduce_parts, 1),
        ]
        copies = stage_weights(staged, weight_sems)
        shift_column[...] = lanes_to_rows(row_of(head_shift))
        turned_high[...], turned_low[...] = split(head_turned[...])
        head_high[...], head_low[...] = split(head_turned[...].T)
        high, low = split(targets[...].T)
        target_parts[:width_out, :] = high
        target_parts[width_out:, :] = low
        for total in (small, stats, sum_reduce, sum_head, sum_expand, sum_out):
            total[...] = jnp.zeros_like(total)
        split_staged(copies, staged)

    def chamfer_half(half):
        xs = [pred_rows[half, pl.ds(c, points, stride=3), :] for c in range(3)]

        def first(j, row_low):
            gap = [xs[c] - true_rows[half, pl.ds(3 * j + c, 1), :] for c in range(3)]
            apart = gap[0] * gap[0] + gap[1] * gap[1] + gap[2] * gap[2]
            distance[j] = apart
            lowest = jnp.min(apart, axis=0, keepdims=True)
            weight = jnp.exp(lowest - apart)
            inside = column_sum(weight)
            col_low[pl.ds(j, 1), :] = lowest
            col_sum[pl.ds(j, 1), :] = inside
            second[j] = weight * (1.0 / (points * inside))
            return jnp.minimum(row_low, apart)

        row_low = lax.fori_loop(
            0, points, first, jnp.full((points, 128), jnp.inf, F32), unroll=8
        )

        def middle_pass(j, row_sum):
            weight = jnp.exp(row_low - distance[j])
            distance[j] = weight
            return row_sum + weight

        row_sum = lax.fori_loop(0, points, middle_pass, jnp.zeros((points, 128), F32), unroll=8)
        row_scale = 1.0 / (points * row_sum)

        def last(j, carry):
            weight = second[j] + distance[j] * row_scale
            return (carry[0] + weight,) + tuple(
                carry[1 + c] + weight * true_rows[half, pl.ds(3 * j + c, 1), :] for c in range(3)
            )

        zero = jnp.zeros((points, 128), F32)
        sums = lax.fori_loop(0, points, last, (zero,) * 4, unroll=8)
        terms = column_sum(row_low - jnp.log(row_sum * (1.0 / points))) + column_sum(
            col_low[...] - jnp.log(col_sum[...] * (1.0 / points))
        )
        grads = [2.0 * (sums[0] * xs[c] - sums[1 + c]) for c in range(3)]
        return terms * (1.0 / points), grads

    @pl.when(index < used)
    def _():
        mixed, middle, (unit_mid, inverse_mid, normed_mid), hidden, slope, branch = block_rows(
            attended, tokens, out_parts, attention_shift, midnorm_gain, midnorm_shift, expand_parts, expand_shift,
            reduce_parts, reduce_shift,
        )
        stream = middle + branch
        unit, inverse = norm_parts(stream)
        normed = split(unit * row_of(lastnorm_gain) + row_of(lastnorm_shift))
        pred = dot3((turned_high[...], turned_low[...]), normed, 1, 1) + shift_column[...]
        predicted[...] = pred.T
        slots = lax.broadcasted_iota(jnp.int32, (slot_count, MASKED_TILE), 0)
        slot_row = owners[...]
        masked = slot_row >= 0
        add_squares(stats, lanes_to_rows(masked.astype(F32)) > 0.5, stream, mixed, branch)
        stats[3:4, :128] += fold_lanes(masked.astype(F32))
        for half in range(MASKED_TILE // 128):
            pred_rows[half] = pred[:, half * 128 : half * 128 + 128]
        chosen = (slots == slot_row).astype(F32).astype(BF16)
        true_points = dot(target_parts[...], chosen)
        true_points = true_points[:width_out] + true_points[width_out:]
        for half in range(MASKED_TILE // 128):
            true_rows[half] = true_points[:, half * 128 : half * 128 + 128]
        losses = []
        for half in range(MASKED_TILE // 128):
            terms, grads = chamfer_half(half)
            losses.append(terms)
            for c in range(3):
                pred_rows[half, pl.ds(c, points, stride=3), :] = grads[c]
        grad_turned = jnp.concatenate([pred_rows[half] for half in range(MASKED_TILE // 128)], axis=1)
        grad_turned = jnp.where(masked, grad_turned, 0.0)
        loss = jnp.where(masked, jnp.concatenate(losses, axis=1), 0.0)
        grad_pred = grad_turned.T
        sum_head[...] += dot3(split(grad_turned), normed)
        grad_last = dot3(split(grad_pred), (head_high[...], head_low[...]), 1, 1)
        grad_str = norm_back(grad_last, unit, inverse, row_of(lastnorm_gain))
        sum_reduce[...] += dot3(split(grad_str.T), hidden)
        small[0:1, :128] += fold_lanes(loss)
        small[1:2, :128] += fold_lanes(masked.astype(F32))
        small[5:6, :] += column_sum(grad_last * unit)
        small[6:7, :] += column_sum(grad_last)
        small[7:8, :] += column_sum(grad_str)
        small[8:9, :width_out] += column_sum(grad_pred)
        grad_pre = dot_deep(split(grad_str), reduce_parts[...], 1) * slope
        parts = split(grad_pre)
        sum_expand[...] += dot3(split(normed_mid.T), parts)
        grad_normed = dot_wide(parts, expand_parts[: 2 * width, :], 1)
        grad_mid = grad_str + norm_back(grad_normed, unit_mid, inverse_mid, row_of(midnorm_gain))
        grad_middle[...] = grad_mid
        shift_sum = column_sum(grad_pre)
        for part in range(shift_sum.shape[1] // width):
            small[16 + part : 17 + part, :] += shift_sum[:, part * width : part * width + width]
        small[20:21, :] += column_sum(grad_normed * unit_mid)
        small[21:22, :] += column_sum(grad_normed)
        small[22:23, :] += column_sum(grad_mid)
        parts = split(grad_mid)
        sum_out[...] += dot3(split(attended[...].T), parts)
        grad_attended[...] = dot_deep(parts, out_parts[...], 1)

    @pl.when(index >= used)
    def _():
        grad_attended[...] = jnp.zeros_like(grad_attended)

    @pl.when(index == used - 1)
    def _():
        pack_tiles([sum_reduce, sum_expand, sum_out, sum_head, small], keep, send, devices)


def row_map(index, used):
    return (jnp.minimum(index, used[0] - 1), 0)


def rows_spec(columns):
    return pl.BlockSpec((TILE, columns), row_map)


def whole_spec(array):
    return pl.BlockSpec(array.shape, lambda index, used: (0,) * len(array.shape))


def tile_spec(columns, number, extra=0, tile=TILE):
    def place(index, used):
        return (jnp.minimum(index, used[number] - 1 + extra), 0)

    return pl.BlockSpec((tile, columns), place)


def masked_spec(columns, extra=0):
    return tile_spec(columns, 1, extra, MASKED_TILE)


def lane_spec(number, tile=TILE):
    return pl.BlockSpec((1, tile), lambda index, used: (0, jnp.minimum(index, used[number] - 1)))


def staged_specs(weights, names):
    staged = ("attention_out", "expand_weight", "reduce_weight")
    return [any_spec() if name in staged else whole_spec(weights[name]) for name in names]


def parts_shapes(width, hidden_width):
    return [
        pltpu.VMEM((width, width), F32),
        pltpu.VMEM((width, hidden_width), F32),
        pltpu.VMEM((hidden_width, width), F32),
        pltpu.VMEM((width, 3 * width), BF16),
        pltpu.VMEM((3 * width, hidden_width), BF16),
        pltpu.VMEM((hidden_width, 3 * width), BF16),
    ]


def run_block(used, attended, tokens, owners, targets, weights, devices):
    masked_count, width = tokens.shape
    hidden_width = weights["expand_weight"].shape[1]
    slot_count, width_out = targets.shape
    points = width_out // 3
    names = (
        "attention_out", "attention_shift",
        "midnorm_gain", "midnorm_shift", "expand_weight", "expand_shift", "reduce_weight",
        "reduce_shift", "lastnorm_gain", "lastnorm_shift", "head_turned", "head_shift",
    )
    chunk = block_chunk(width, hidden_width, width_out)
    slots = slots_shape(chunk, devices)
    stats = shape(8, width)
    return pl.pallas_call(
        lambda *refs: block_kernel(devices, *refs),
        out_shape=(
            shape(masked_count, width_out),
            shape(masked_count, width),
            shape(masked_count + MASKED_TILE, width),
            stats,
            shape(*slots),
            shape(*slots),
        ),
        grid_spec=pltpu.PrefetchScalarGridSpec(
            num_scalar_prefetch=1,
            grid=(masked_count // MASKED_TILE + 1,),
            in_specs=[masked_spec(width), masked_spec(width), lane_spec(1, MASKED_TILE), whole_spec(targets)]
            + staged_specs(weights, names),
            out_specs=[
                masked_spec(width_out), masked_spec(width), masked_spec(width, 1), whole_spec(stats),
                vmem_spec(), vmem_spec(),
            ],
            scratch_shapes=[pltpu.VMEM(dims, F32) for dims in chunk]
            + parts_shapes(width, hidden_width)
            + [pltpu.VMEM((width, width_out), BF16)] * 2
            + [pltpu.VMEM((width_out, width), BF16)] * 2
            + [
                pltpu.VMEM((2 * width_out, slot_count), BF16),
                pltpu.VMEM((MASKED_TILE // 128, width_out, 128), F32),
                pltpu.VMEM((MASKED_TILE // 128, width_out, 128), F32),
                pltpu.VMEM((points, points, 128), F32),
                pltpu.VMEM((points, points, 128), F32),
                pltpu.VMEM((points, 128), F32),
                pltpu.VMEM((points, 128), F32),
                pltpu.VMEM((width_out, 1), F32),
                pltpu.SemaphoreType.DMA((3,)),
            ],
        ),
        compiler_params=pltpu.CompilerParams(vmem_limit_bytes=48 * 2**20),
        cost_estimate=cost(55),
        name="block",
    )(used, attended, tokens, owners, targets, *[weights[name] for name in names])


def visible_kernel(
    used_ref, attended, tokens, valid, stats_before, attention_out,
    attention_shift, midnorm_gain, midnorm_shift, expand_weight, expand_shift, reduce_weight,
    reduce_shift, lastnorm_gain, lastnorm_shift, head_turned, head_shift,
    predicted, stats,
    out_stage, expand_stage, reduce_stage, out_parts, expand_parts, reduce_parts, head_high, head_low, weight_sems,
):
    index = pl.program_id(0)

    @pl.when(index == 0)
    def _():
        staged = [
            (attention_out, out_stage, out_parts, 1),
            (expand_weight, expand_stage, expand_parts, 0),
            (reduce_weight, reduce_stage, reduce_parts, 1),
        ]
        copies = stage_weights(staged, weight_sems)
        head_high[...], head_low[...] = split(head_turned[...].T)
        stats[...] = stats_before[...]
        split_staged(copies, staged)

    @pl.when(index < used_ref[2])
    def _():
        mixed, middle, _, _, _, branch = block_rows(
            attended, tokens, out_parts, attention_shift, midnorm_gain, midnorm_shift, expand_parts, expand_shift,
            reduce_parts, reduce_shift,
        )
        stream = middle + branch
        unit, _ = norm_parts(stream)
        normed = split(unit * row_of(lastnorm_gain) + row_of(lastnorm_shift))
        predicted[...] = dot3(normed, (head_high[...], head_low[...])) + row_of(head_shift)
        add_squares(stats, lanes_to_rows(valid[...]) > 0.5, stream, mixed, branch)
        stats[3:4, :TILE] += valid[...]


def run_visible(used, attended, tokens, valid, stats, weights):
    visible_count, width = tokens.shape
    hidden_width = weights["expand_weight"].shape[1]
    width_out = weights["head_turned"].shape[0]
    names = (
        "attention_out", "attention_shift",
        "midnorm_gain", "midnorm_shift", "expand_weight", "expand_shift", "reduce_weight",
        "reduce_shift", "lastnorm_gain", "lastnorm_shift", "head_turned", "head_shift",
    )
    return pl.pallas_call(
        visible_kernel,
        out_shape=(shape(visible_count, width_out), shape(8, width)),
        grid_spec=pltpu.PrefetchScalarGridSpec(
            num_scalar_prefetch=1,
            grid=(visible_count // TILE,),
            in_specs=[tile_spec(width, 2), tile_spec(width, 2), lane_spec(2), whole_spec(stats)]
            + staged_specs(weights, names),
            out_specs=[tile_spec(width_out, 2), whole_spec(stats)],
            scratch_shapes=parts_shapes(width, hidden_width)
            + [pltpu.VMEM((width, width_out), BF16)] * 2
            + [pltpu.SemaphoreType.DMA((3,))],
        ),
        compiler_params=pltpu.CompilerParams(vmem_limit_bytes=36 * 2**20),
        cost_estimate=cost(16),
        name="visible",
    )(used, attended, tokens, valid, stats, *[weights[name] for name in names])


def block_chunk(width, hidden_width, width_out):
    return [(width, hidden_width), (width, hidden_width), (width, width), (width_out, width), (24, width)]


def in_chunk(width):
    return [(width, 3 * width), (16, width)]


def attention_back_kernel(
    lens, joint_hbm, grad_rows, joint_grad, joint, joint_sems,
):
    width = grad_rows.shape[1]
    lane = lax.broadcasted_iota(jnp.int32, (CLOUD_MAX, 128), 1)
    first_head = lane < 64
    key_place = lax.broadcasted_iota(jnp.int32, (CLOUD_MAX, CLOUD_MAX), 0)
    query_place = lax.broadcasted_iota(jnp.int32, (CLOUD_MAX, CLOUD_MAX), 1)
    empty = jnp.zeros((CLOUD_MAX, 128), BF16)

    def both_heads(values):
        return jnp.concatenate(
            [jnp.where(first_head, values, 0.0), jnp.where(first_head, 0.0, values)], axis=0
        )

    def starts_of(index, start, masked_start):
        starts = []
        for number in range(BACK_GROUP):
            starts.append((start, masked_start))
            length = lens[jnp.minimum(index * BACK_GROUP + number, lens.shape[0] - 1)]
            start = start + spaced(length)
            masked_start = masked_start + spaced(masked_of(length))
        return starts, start, masked_start

    def fetch(starts, slot):
        step = CLOUD_MAX // JOINT_PIECES
        return [
            pltpu.make_async_copy(
                joint_hbm.at[pl.ds(start_of(start + piece * step), step)],
                joint.at[slot * BACK_GROUP + number, pl.ds(piece * step, step)],
                joint_sems.at[slot * BACK_GROUP + number, piece],
            )
            for number, (start, _) in enumerate(starts)
            for piece in range(JOINT_PIECES)
        ]

    groups = lens.shape[0] // BACK_GROUP
    start, masked_start = jnp.int32(0), jnp.int32(0)
    for index in range(JOINT_SLOTS - 1):
        starts, start, masked_start = starts_of(index, start, masked_start)
        for copy in fetch(starts, index):
            copy.start()
    work = [(number, pair) for number in range(BACK_GROUP) for pair in range(HEADS // 2)]

    def clouds(index, carry):
        start, masked_start, ahead = carry
        starts, following, masked_following = starts_of(index, start, masked_start)
        ahead_starts, next_ahead, _ = starts_of(index + JOINT_SLOTS - 1, ahead, jnp.int32(0))
        slot = lax.rem(index, JOINT_SLOTS)

        @pl.when(index + JOINT_SLOTS - 1 < groups)
        def _():
            for copy in fetch(ahead_starts, lax.rem(index + JOINT_SLOTS - 1, JOINT_SLOTS)):
                copy.start()

        for copy in fetch(starts, slot):
            copy.wait()
        lengths = [lens[index * BACK_GROUP + number] for number in range(BACK_GROUP)]
        insides = [key_place < length for length in lengths]
        lives = [
            jnp.logical_and(inside, query_place < masked_of(length)) for inside, length in zip(insides, lengths)
        ]
        rows = [pl.ds(start_of(starts[number][0]), CLOUD_MAX) for number, _ in work]
        slots = [slot * BACK_GROUP + number for number, _ in work]
        masked_rows = [pl.ds(start_of(starts[number][1]), CLOUD_MAX) for number, _ in work]
        at = [
            [slice(part * width + pair * 128, part * width + pair * 128 + 128) for part in range(3)]
            for _, pair in work
        ]
        each = range(len(work))
        query = [split(both_heads(joint[slots[one], :, at[one][0]] * 0.125)) for one in each]
        key = [split(joint[slots[one], :, at[one][1]]) for one in each]
        value = [split(joint[slots[one], :, at[one][2]]) for one in each]
        grad = [split(both_heads(grad_rows[masked_rows[one], at[one][0]])) for one in each]
        scores = [dot_pair(key[one], query[one]) for one in each]
        grad_probs = [dot_pair(value[one], grad[one]) for one in each]
        grad_wide = [jnp.concatenate(parts, axis=1) for parts in grad]
        query_wide = [jnp.concatenate(parts, axis=1) for parts in query]
        prob_parts, grad_parts, turned_parts = [], [], []
        for one in each:
            inside, live = insides[work[one][0]], lives[work[one][0]]
            probs, grads, turned = [], [], []
            for half in range(2):
                lanes = slice(half * CLOUD_MAX, half * CLOUD_MAX + CLOUD_MAX)
                score = jnp.where(inside, scores[one][:, lanes], -1e30)
                weight = jnp.exp(score - jnp.max(score, axis=0, keepdims=True))
                prob = jnp.where(live, weight * (1.0 / column_sum(weight)), 0.0)
                grad_prob = grad_probs[one][:, lanes]
                grad_score = prob * (grad_prob - column_sum(prob * grad_prob))
                probs.append(split(prob))
                grads.append(split(grad_score))
                turned.append(split(grad_score.T))
            for parts, found, axis in ((prob_parts, probs, 1), (grad_parts, grads, 1), (turned_parts, turned, 0)):
                parts.append(
                    tuple(jnp.concatenate([found[0][part], found[1][part]], axis=axis) for part in range(2))
                )
        for one in each:
            joint_grad[rows[one], at[one][2]] = dot_wide(prob_parts[one], grad_wide[one])
        for one in each:
            joint_grad[rows[one], at[one][1]] = dot_wide(grad_parts[one], query_wide[one])
        for one in each:
            left = jnp.concatenate(turned_parts[one], axis=1)
            right = jnp.concatenate(
                [
                    jnp.concatenate([key[one][0], key[one][1]], axis=1),
                    jnp.concatenate([key[one][0], empty], axis=1),
                ],
                axis=0,
            )
            grad_query = dot(left, right)
            grad_query = (grad_query[:, :128] + grad_query[:, 128:]) * 0.125
            joint_grad[rows[one], at[one][0]] = jnp.where(
                first_head, grad_query[:CLOUD_MAX], grad_query[CLOUD_MAX:]
            )

        return following, masked_following, next_ahead

    lax.fori_loop(0, groups, clouds, (jnp.int32(0), jnp.int32(0), start))


def run_attention_back(lens, joint, grad_attended):
    return pl.pallas_call(
        attention_back_kernel,
        out_shape=shape(*joint.shape),
        in_specs=[smem_spec(), any_spec(), vmem_spec()],
        out_specs=vmem_spec(),
        scratch_shapes=[
            pltpu.VMEM((JOINT_SLOTS * BACK_GROUP, CLOUD_MAX, joint.shape[1]), F32),
            pltpu.SemaphoreType.DMA((JOINT_SLOTS * BACK_GROUP, JOINT_PIECES)),
        ],
        compiler_params=pltpu.CompilerParams(vmem_limit_bytes=36 * 2**20),
        cost_estimate=cost(18),
        name="attention_back",
    )(lens, joint, grad_attended)


def in_back_kernel(
    devices, used_ref, lens, grad_joint, tokens, prenorm_gain, prenorm_shift, attention_in, stats,
    keep, send, sum_in, small, joint_sum,
):
    width = tokens.shape[1]
    spread, _, _ = cloud_totals(lens)
    sum_in[...] = jnp.zeros_like(sum_in)
    joint_sum[...] = jnp.zeros_like(joint_sum)

    def tile(index, carry):
        rows = pl.ds(pl.multiple_of(index * TILE, TILE), TILE)
        live = lax.broadcasted_iota(jnp.int32, (TILE, 1), 0) + index * TILE < spread
        unit, _ = norm_parts(tokens[rows, :])
        grads = jnp.where(live, grad_joint[rows, :], 0.0)
        joint_sum[...] += column_sum(grads)
        sum_in[...] += dot3(split(unit.T), split(grads))
        return carry

    lax.fori_loop(0, used_ref[0], tile, 0)
    small[...] = jnp.zeros_like(small)
    small[8:16, :] = stats[...]
    for row, factor in ((0, sum_in[...]), (1, joint_sum[...])):
        column = jnp.sum(attention_in[...] * factor, axis=1, keepdims=True)
        small[row : row + 1, :] = jnp.broadcast_to(column, (width, 128)).T[:1, :]
    gains = lanes_to_rows(row_of(prenorm_gain))
    shifts = lanes_to_rows(row_of(prenorm_shift))
    sum_in[...] = sum_in[...] * gains + shifts * joint_sum[...]
    pack_tiles([sum_in, small], keep, send, devices)


def run_in_back(used, lens, grad_joint, tokens, weights, stats, devices):
    width = tokens.shape[1]
    joint_width = grad_joint.shape[1]
    extra = [weights[name] for name in ("prenorm_gain", "prenorm_shift", "attention_in")]
    chunk = in_chunk(width)
    slots = slots_shape(chunk, devices)
    return pl.pallas_call(
        lambda *refs: in_back_kernel(devices, *refs),
        out_shape=(shape(*slots), shape(*slots)),
        in_specs=[smem_spec()] * 2 + [vmem_spec()] * 6,
        out_specs=[vmem_spec()] * 2,
        scratch_shapes=[pltpu.VMEM(dims, F32) for dims in chunk] + [pltpu.VMEM((1, joint_width), F32)],
        compiler_params=pltpu.CompilerParams(vmem_limit_bytes=20 * 2**20),
        cost_estimate=cost(11),
        name="in_back",
    )(used, lens, grad_joint, tokens, *extra, stats)


def input_kernel(
    used_ref, groups, grad_joint, tokens, grad_middle, prenorm_gain, attention_in, spaced_grad, in_parts,
):
    split_weight(attention_in, in_parts, 0)

    def tile(index, carry):
        rows = pl.ds(pl.multiple_of(index * TILE, TILE), TILE)
        unit, inverse = norm_parts(tokens[rows, :])
        grad_normed = dot_wide(split(grad_joint[rows, :]), in_parts[: 2 * tokens.shape[1], :], 1)
        spaced_grad[rows, :] = norm_back(grad_normed, unit, inverse, row_of(prenorm_gain))
        return carry

    lax.fori_loop(0, used_ref[0], tile, 0)

    def add_group(group, carry):
        source = groups[group]
        rows = pl.ds(start_of(group * 8), 8)
        added = grad_middle[pl.ds(start_of(jnp.maximum(source, 0) * 8), 8), :]
        spaced_grad[rows, :] += jnp.where(source >= 0, added, 0.0)
        return carry

    def add_groups(index, carry):
        for group in range(TILE // 8):
            add_group(index * (TILE // 8) + group, carry)
        return carry

    lax.fori_loop(0, used_ref[0], add_groups, 0)


def run_input(used, groups, grad_joint, tokens, grad_middle, weights):
    spaced_count, width = tokens.shape
    return pl.pallas_call(
        input_kernel,
        out_shape=shape(spaced_count, width),
        in_specs=[smem_spec()] * 2 + [vmem_spec()] * 5,
        out_specs=vmem_spec(),
        scratch_shapes=[pltpu.VMEM((3 * width, grad_joint.shape[1]), BF16)],
        compiler_params=pltpu.CompilerParams(vmem_limit_bytes=20 * 2**20),
        cost_estimate=cost(10),
        name="input_grad",
    )(used, groups, grad_joint, tokens, grad_middle, weights["prenorm_gain"], weights["attention_in"])


def restore_kernel(
    lens, owner, spaced_grad, masked_pred, visible_pred, input_grad, predicted_turned, pred_rows
):
    token_count, width = input_grad.shape
    input_grad[...] = jnp.zeros_like(input_grad)
    pred_rows[...] = jnp.zeros_like(pred_rows)
    windows = cloud_windows(lens, token_count)
    earlier = earlier_table()
    order = lax.broadcasted_iota(jnp.int32, (2 * CLOUD_MAX, CLOUD_MAX), 1)
    places_down = lax.broadcasted_iota(jnp.int32, (CLOUD_MAX, 1), 0)
    for first in range(0, lens.shape[0], 4):
        clouds = range(first, min(first + 4, lens.shape[0]))
        places = [
            cloud_places(
                owner[:, pl.ds(windows[cloud][1], 2 * CLOUD_MAX)],
                windows[cloud][0] - windows[cloud][1], lens[cloud], earlier,
            )
            for cloud in clouds
        ]
        columns = [lanes_to_rows(place.astype(F32)).astype(jnp.int32) for place in places]
        picks = [(order == column).astype(F32).astype(BF16) for column in columns]
        for pick, cloud in zip(picks, clouds):
            _, base, spaced_start, masked_start, visible_start = windows[cloud]
            rows = pl.ds(base, 2 * CLOUD_MAX)
            length, masked = lens[cloud], masked_of(lens[cloud])
            source = spaced_grad[pl.ds(spaced_start, CLOUD_MAX), :]
            high, low = split(jnp.where(places_down < length, source, 0.0))
            input_grad[rows, :] += dot(pick, high) + dot(pick, low)
            source = masked_pred[pl.ds(masked_start, CLOUD_MAX), :]
            shifted = pltpu.roll(
                jnp.concatenate(
                    [visible_pred[pl.ds(visible_start, VISIBLE_MAX), :], jnp.zeros_like(source[VISIBLE_MAX:])], axis=0
                ),
                masked, 0,
            )
            source = jnp.where(places_down < masked, source, shifted)
            high, low = split(jnp.where(places_down < length, source, 0.0))
            pred_rows[rows, :] += dot(pick, high) + dot(pick, low)
    for place in range(0, token_count, 128):
        predicted_turned[:, place : place + 128] = pred_rows[place : place + 128, :].T


def run_restore(lens, owner, spaced_grad, masked_pred, visible_pred):
    token_count = owner.shape[1]
    width, width_out = spaced_grad.shape[1], masked_pred.shape[1]
    return pl.pallas_call(
        restore_kernel,
        out_shape=(shape(token_count, width), shape(width_out, token_count)),
        in_specs=[smem_spec()] + [vmem_spec()] * 4,
        out_specs=[vmem_spec()] * 2,
        scratch_shapes=[pltpu.VMEM((token_count, width_out), F32)],
        compiler_params=pltpu.CompilerParams(vmem_limit_bytes=24 * 2**20),
        cost_estimate=cost(8),
        name="restore",
    )(lens, owner, spaced_grad, masked_pred, visible_pred)


def gather_pack(mine, theirs, pack, sems):
    copies = [
        pltpu.make_async_copy(mine, pack.at[0], sems.at[0]),
        pltpu.make_async_copy(theirs, pack.at[1], sems.at[1]),
    ]
    for copy in copies:
        copy.start()
    for copy in copies:
        copy.wait()


def block_sums_kernel(
    devices, mine, theirs,
    reduce_out, expand_out, attention_out, head_out, lastnorm_gain, lastnorm_shift, reduce_shift, head_shift,
    expand_shift, midnorm_gain, midnorm_shift, attention_shift, loss_out, scale_out,
    sum_reduce, small, pack, sems,
):
    gather_pack(mine, theirs, pack, sems)
    unpack_tiles(pack, [sum_reduce, expand_out, attention_out, head_out, small], devices, None)
    width = small.shape[1]
    scale = 1.0 / jnp.sum(small[1:2, :], axis=1, keepdims=True)
    scale_out[...] = jnp.broadcast_to(scale, scale_out.shape)
    for target in (expand_out, attention_out, head_out):
        target[...] = target[...] * scale
    for row, target in (
        (5, lastnorm_gain), (6, lastnorm_shift), (7, reduce_shift),
        (20, midnorm_gain), (21, midnorm_shift), (22, attention_shift),
    ):
        target[...] = (small[row : row + 1, :] * scale)[0]
    for part in range(expand_shift.shape[0] // width):
        expand_shift[part * width : part * width + width] = (small[16 + part : 17 + part, :] * scale)[0]
    head_shift[...] = (small[8:9, :] * scale)[0, : head_shift.shape[0]]
    loss_out[0] = jnp.sum(small[0:1, :]) / jnp.sum(small[1:2, :])
    for place in range(0, reduce_out.shape[0], 128):
        reduce_out[place : place + 128, :] = sum_reduce[:, place : place + 128].T * scale


def in_sums_kernel(devices, scale, mine, theirs, in_out, prenorm_gain, prenorm_shift, rms_out, small, pack, sems):
    gather_pack(mine, theirs, pack, sems)
    unpack_tiles(pack, [in_out, small], devices, scale[...])
    prenorm_gain[...] = small[0, :]
    prenorm_shift[...] = small[1, :]
    totals = jnp.sum(small[8:16, :], axis=1, keepdims=True)
    rms_out[...] = jnp.broadcast_to(jnp.sqrt(totals / (totals[3:4] * small.shape[1])), rms_out.shape)


def run_sums(kernel, scale, mine, theirs, chunk, outs, keep, devices, name):
    scales = [] if scale is None else [scale]
    return pl.pallas_call(
        lambda *refs: kernel(devices, *refs),
        out_shape=tuple(shape(*dims) for dims in outs),
        in_specs=[vmem_spec()] * len(scales) + [any_spec()] * 2,
        out_specs=[smem_spec() if dims == (1,) else vmem_spec() for dims in outs],
        scratch_shapes=[pltpu.VMEM(dims, F32) for dims in keep]
        + [
            pltpu.VMEM((2,) + slots_shape(chunk, devices), F32),
            pltpu.SemaphoreType.DMA((2,)),
        ],
        compiler_params=pltpu.CompilerParams(vmem_limit_bytes=24 * 2**20),
        cost_estimate=cost(4),
        name=name,
    )(*scales, mine, theirs)


def shards(
    tokens, cloud_lengths, owner_slot, targets, prenorm_gain, prenorm_shift, attention_in,
    attention_out, attention_shift, midnorm_gain, midnorm_shift, expand_weight, expand_shift,
    reduce_weight, reduce_shift, lastnorm_gain, lastnorm_shift, head_weight, head_shift,
):
    token_count, width = tokens.shape
    hidden_width = expand_weight.shape[1]
    devices = lax.axis_size("dp")
    slot_count, width_out = targets.shape
    capacity = slot_count // devices
    arrived = lax.all_to_all(
        targets.reshape(devices, capacity, width_out), "dp", split_axis=0, concat_axis=0, tiled=True
    ).reshape(slot_count, width_out)
    weights = dict(
        prenorm_gain=prenorm_gain, prenorm_shift=prenorm_shift, attention_in=attention_in,
        attention_out=attention_out, attention_shift=attention_shift,
        midnorm_gain=midnorm_gain, midnorm_shift=midnorm_shift,
        expand_weight=expand_weight, expand_shift=expand_shift, reduce_weight=reduce_weight,
        reduce_shift=reduce_shift, lastnorm_gain=lastnorm_gain,
        lastnorm_shift=lastnorm_shift, head_turned=head_weight.T,
        head_shift=head_shift,
    )
    owner = owner_slot[None]
    (
        spaced_tokens, joint, masked_tokens, masked_attended, visible_tokens, visible_attended,
        owners, valid, used, groups,
    ) = run_attend(
        tokens, cloud_lengths, owner, weights["prenorm_gain"], weights["prenorm_shift"], attention_in
    )
    masked_pred, grad_middle, grad_attended, stats, block_keep, block_send = run_block(
        used, masked_attended, masked_tokens, owners, arrived, weights, devices
    )
    block_sum = DeviceSum(block_keep, block_send, devices)
    grad_attended, stats = beside([block_sum], (grad_attended, stats))
    visible_pred, stats = beside(
        [block_sum], run_visible(used, visible_attended, visible_tokens, valid, stats, weights)
    )
    grad_attended, _ = lax.optimization_barrier((grad_attended, stats))
    grad_joint = beside([block_sum], run_attention_back(cloud_lengths, joint, grad_attended))
    in_keep, in_send = beside(
        [block_sum], run_in_back(used, cloud_lengths, grad_joint, spaced_tokens, weights, stats, devices)
    )
    in_sum = DeviceSum(in_keep, in_send, devices)
    sums = [in_sum, block_sum]
    grad_joint = beside([in_sum], grad_joint)
    spaced_grad = beside(sums, run_input(used, groups, grad_joint, spaced_tokens, grad_middle, weights))
    input_grad, predicted_turned = beside(
        sums, run_restore(cloud_lengths, owner, spaced_grad, masked_pred, visible_pred)
    )
    if not block_sum.done():
        block_sum.start()
        beside([in_sum], ())
        in_sum.start()
        moving = lax.optimization_barrier([one.moving for one in sums])
        for one, moved in zip(sums, moving):
            one.moving = moved
            one.finish()
    while not block_sum.done():
        beside(sums, ())
    chunk = block_chunk(width, hidden_width, width_out)
    vector = (width,)
    (
        grad_reduce, grad_expand, grad_out, grad_head_turned, grad_last_gain, grad_last_shift, grad_reduce_shift,
        grad_head_shift, grad_expand_shift, grad_mid_gain, grad_mid_shift, grad_out_shift, loss, scale,
    ) = beside(
        [in_sum],
        run_sums(
            block_sums_kernel, None, block_sum.total, block_sum.theirs, chunk,
            [
                (hidden_width, width), chunk[1], chunk[2], chunk[3], vector, vector, vector,
                (width_out,), (hidden_width,), vector, vector, vector, (1,), (8, 128),
            ],
            [chunk[0], chunk[4]], devices, "block_sums",
        ),
    )
    run_out([in_sum])
    chunk = in_chunk(width)
    grad_in, grad_pre_gain, grad_pre_shift, rms = run_sums(
        in_sums_kernel, scale, in_sum.total, in_sum.theirs, chunk,
        [chunk[0], (width,), (width,), (8, 128)], [chunk[1]], devices, "in_sums",
    )
    return (
        loss.reshape(()),
        predicted_turned.T,
        input_grad,
        grad_pre_gain,
        grad_pre_shift,
        grad_in,
        grad_out,
        grad_out_shift,
        grad_mid_gain,
        grad_mid_shift,
        grad_expand,
        grad_expand_shift,
        grad_reduce,
        grad_reduce_shift,
        grad_last_gain,
        grad_last_shift,
        grad_head_turned.T,
        grad_head_shift,
        rms[:3, 0],
    )


def solution(mesh):
    row = P("dp", None)
    return jax.shard_map(
        shards,
        mesh=mesh,
        in_specs=(row, P("dp"), P("dp"), row) + (P(),) * 15,
        out_specs=(P(), row, row) + (P(),) * 16,
        check_vma=False,
    )
```
